32 devices in a mesh: pipe: 4 (over y, x), dp: 8 (over z, core).
Axes of the slice: x: 2, y: 2, z: 4, core: 2. Of those that a mesh axis runs over, the one named last changes fastest.
Arguments:
- block_input: bfloat16 [4, 784, 2048], P(None, 'dp'), may hold values from -20 to 20
- proj_weight: bfloat16 [4, 2048, 512], P('pipe'), may hold values from -0.125 to 0.125
- spatial_weight: bfloat16 [4, 4608, 256], P('pipe'), may hold values from -0.09375 to 0.09375
- norm_gain: float32 [2, 3072], replicated, may hold values from 0.1 to 1.9
- norm_shift: float32 [2, 3072], replicated, may hold values from -1.5 to 1.5
- output_grad: bfloat16 [4, 784, 2048], P(None, 'dp'), may hold values from -6 to 6
- image_ids: int32 [4, 16], P(None, 'dp'), may hold values from 0 to 63
Outputs:
- block_output: bfloat16 [4, 784, 2048], P(None, 'dp', 'pipe')
- input_grad: bfloat16 [4, 784, 2048], P(None, 'dp', 'pipe')
- proj_grad: float32 [4, 2048, 512], P('pipe')
- spatial_grad: float32 [4, 4608, 256], P('pipe')
- gain_grad: float32 [2, 3072], P(None, 'pipe')
- shift_grad: float32 [2, 3072], P(None, 'pipe')
- memory_bank: float32 [64, 2048], P('dp', 'pipe')
The draws below stay inside these ranges and needn't reach their ends.
All inputs are finite; a program needn't handle non-finite values.
Results may differ from the reference program's by a relative error of at most 0.019.
Values may be sent and summed in bfloat16 or wider, within the bound.
A program may use at most 256 MiB of HBM per device.

```python
import jax
import jax.numpy as jnp
from jax import lax

CH = 2048
MID = 512
SIDE = 7
MICRO = 4
HALF = 256
IMGS = 16
ROWS = 784
NORMS = 3072
BANK = 64


def draw_block_input(key, part):
    key = jax.random.fold_in(key, 11)
    first_key, second_key = jax.random.split(key, 2)
    image_index = jnp.arange(ROWS) // (SIDE * SIDE)
    rising = jnp.exp(jnp.log(3.0) * image_index.astype(jnp.float32) / max(IMGS - 1, 1))
    column = jnp.exp(jax.random.uniform(second_key, (CH,), minval=-1.0, maxval=1.0))
    draws = jnp.clip(jax.random.normal(first_key, (MICRO, ROWS, CH)), -4.0, 4.0)
    return (draws * rising[None, :, None] * column[None, None, :] * 0.6).astype(jnp.bfloat16)


def with_ends(values, own_key, least, largest):
    dims = values.shape
    place = [jax.random.randint(jax.random.fold_in(own_key, axis), (), 0, dims[axis]) for axis in range(len(dims))]
    values = values.at[tuple(place)].set(least)
    longest = dims.index(max(dims))
    place[longest] = (place[longest] + 1) % dims[longest]
    return values.at[tuple(place)].set(largest)


def level_of(stream_key, shape, pieces, low, largest):
    def one(position, shards_of):
        steps = jax.random.uniform(jax.random.fold_in(jax.random.fold_in(stream_key, 6), position), (shards_of,), jnp.float32, low / len(pieces), largest / len(pieces))
        return jnp.repeat(jnp.exp(steps), shape[position] // shards_of).reshape((-1,) + (1,) * (len(shape) - position - 1))

    loudness = one(*pieces[0])
    for cut in pieces[1:]:
        loudness = loudness * one(*cut)
    return loudness


def gaussian(key, dims, scale, limit, cuts=(), held_as=jnp.bfloat16):
    level = level_of(key, dims, cuts, -0.22, 0.18) if cuts else 1.0
    result = jax.random.normal(key, dims, jnp.float32) * scale * level
    return jnp.minimum(jnp.maximum(result, -limit), limit).astype(held_as)


def setup_inputs(seed: int = 0) -> dict:
    arg_keys = jax.random.split(jax.random.key(seed), 8)
    return {
        "block_input": draw_block_input(jax.random.fold_in(arg_keys[7], 71), 0),
        "proj_weight": gaussian(arg_keys[1], (4, CH, MID), CH ** -0.5, 0.125, ((0, 4),)),
        "spatial_weight": gaussian(arg_keys[2], (4, 9 * MID, HALF), (9 * MID) ** -0.5, 0.09375, ((0, 4),)),
        "norm_gain": jnp.clip(1.0 + 0.18 * jax.random.normal(arg_keys[3], (2, NORMS), jnp.float32), 0.1, 1.9),
        "norm_shift": gaussian(arg_keys[4], (2, NORMS), 0.3, 1.5, (), jnp.float32),
        "output_grad": gaussian(arg_keys[5], (MICRO, ROWS, CH), 1.0, 6.0, ((1, 8),)),
        "image_ids": with_ends(jax.random.randint(arg_keys[6], (MICRO, IMGS), 0, BANK), jax.random.fold_in(arg_keys[6], 1), 0, BANK - 1).astype(jnp.int32),
    }


EPS = 1e-05

@jax.custom_vjp
def low(v):
    return lax.optimization_barrier(v.astype(jnp.bfloat16)).astype(jnp.float32)

@jax.custom_vjp
def low_back(v):
    return v

def low_keep(v):
    return (low(v), None)

def low_pass(kept, grad):
    return (grad,)

def back_keep(v):
    return (v, None)

def back_low(kept, grad):
    return (low(grad),)
low.defvjp(low_keep, low_pass)
low_back.defvjp(back_keep, back_low)

def smooth(values):
    return jax.nn.gelu(values, approximate=True)

def unfold_taps(hidden):
    row_count, channels = hidden.shape
    images = row_count // (SIDE * SIDE)
    image_grid = hidden.reshape(images, SIDE, SIDE, channels)
    padded = jnp.pad(image_grid, ((0, 0), (1, 1), (1, 1), (0, 0)))
    tap_list = [padded[:, row_off:row_off + SIDE, col_off:col_off + SIDE, :] for row_off in range(3) for col_off in range(3)]
    return jnp.stack(tap_list, axis=3).reshape(row_count, 9 * channels)

def batch_norm(values, scale_part, offset_part):
    average = lax.optimization_barrier(jnp.mean(values, axis=0))
    inverse = lax.rsqrt(lax.optimization_barrier(jnp.mean(values * values, axis=0)) - average * average + EPS)
    return (values - average) * inverse * scale_part + offset_part

def bottleneck(block_in, w_reduce, w_expand, w_spatial, scale_row, offset_row):
    middle = w_reduce.shape[1]
    pre_one = low_back(jnp.dot(block_in, w_reduce, precision=lax.Precision.HIGHEST))
    hidden_one = low(smooth(batch_norm(pre_one, scale_row[:middle], offset_row[:middle])))
    pre_two = low_back(jnp.dot(unfold_taps(hidden_one), w_spatial, precision=lax.Precision.HIGHEST))
    hidden_two = low(smooth(batch_norm(pre_two, scale_row[middle:2 * middle], offset_row[middle:2 * middle])))
    pre_three = low_back(jnp.dot(hidden_two, w_expand.T, precision=lax.Precision.HIGHEST))
    return smooth(batch_norm(pre_three, scale_row[2 * middle:], offset_row[2 * middle:]) + block_in)

def forward(block_input, proj_weight, spatial_weight, norm_gain, norm_shift):
    outputs = []
    for micro_index in range(MICRO):
        current = block_input[micro_index]
        for block_index in range(2):
            spatial_full = jnp.concatenate([spatial_weight[2 * block_index], spatial_weight[2 * block_index + 1]], axis=1)
            current = bottleneck(current, proj_weight[2 * block_index], proj_weight[2 * block_index + 1], spatial_full, norm_gain[block_index], norm_shift[block_index])
            if block_index == 0:
                current = low(current)
        outputs.append(current)
    return jnp.stack(outputs)

def reference(block_input, proj_weight, spatial_weight, norm_gain, norm_shift, output_grad, image_ids):
    inputs = (block_input.astype(jnp.float32), proj_weight.astype(jnp.float32), spatial_weight.astype(jnp.float32), norm_gain.astype(jnp.float32), norm_shift.astype(jnp.float32))
    output, pullback = jax.vjp(forward, *inputs)
    gradients = pullback(output_grad.astype(jnp.float32))
    rounded = output.astype(jnp.bfloat16)
    pooled = lax.optimization_barrier(jnp.mean(rounded.astype(jnp.float32).reshape(MICRO, IMGS, SIDE * SIDE, CH), axis=2))
    bank = jax.ops.segment_sum(pooled.reshape(MICRO * IMGS, CH), image_ids.reshape(MICRO * IMGS).astype(jnp.int32), num_segments=BANK)
    return (rounded, gradients[0].astype(jnp.bfloat16), gradients[1], gradients[2], gradients[3], gradients[4], bank)
```

```python
import functools
import math
import types

import jax
import jax.numpy as jnp
from jax import lax
from jax.experimental import pallas as pl
from jax.experimental.pallas import tpu as pltpu
from jax.sharding import PartitionSpec as P

SIDE = 7
TAPS = 9
EPS = 1e-05
LANES = 128
GROUPS = 2
MESH = pl.DeviceIdType.MESH
F32 = jnp.float32
BF16 = jnp.bfloat16


def gelu_pair(v):
    c0 = math.sqrt(2.0 / math.pi)
    c1 = 0.044715
    sq = v * v
    t = jnp.tanh(c0 * v * (1.0 + c1 * sq))
    half = 0.5 + 0.5 * t
    slope = half + (0.5 * c0) * v * (1.0 - t * t) * (1.0 + (3.0 * c1) * sq)
    return v * half, slope


def dot(a, b):
    return jnp.dot(a, b, preferred_element_type=F32)


def dot_nt(a, b):
    return lax.dot_general(a, b, (((1,), (1,)), ((), ())), preferred_element_type=F32)


def dot_tn(a, b):
    return lax.dot_general(a, b, (((0,), (0,)), ((), ())), preferred_element_type=F32)


class Sizes:
    def __init__(self, mesh, block_input, proj, spatial, bank_rows):
        self.pipes = mesh.shape["pipe"]
        self.dps = mesh.shape["dp"]
        self.micro = block_input.shape[0]
        self.rows = block_input.shape[1]
        self.pad = -(-self.rows // 16) * 16
        self.ch = block_input.shape[2]
        self.mid = proj.shape[2]
        self.images = self.rows // (SIDE * SIDE)
        self.cs = self.ch // self.pipes
        self.msd = self.mid // self.pipes
        self.groups = GROUPS
        self.gm = self.micro // self.groups
        self.zs = self.dps // 2
        self.total = self.rows * self.dps
        self.bank = bank_rows
        self.deep = (self.cs // 2) % (16 * self.zs) == 0 and (TAPS * self.mid // 2) % (16 * self.zs) == 0


def scratch_list(c):
    full = (c.micro, c.pad)
    seg = (c.pipes, c.micro, c.pad, LANES)
    items = [
        ("u_all", pltpu.VMEM(full + (c.ch,), BF16)),
        ("u_seg", pltpu.VMEM((2,) + full + (c.cs,), BF16)),
        ("g_seg", pltpu.VMEM(full + (c.cs,), BF16)),
        ("p_own", pltpu.VMEM((c.ch, c.mid), BF16)),
        ("pq", pltpu.VMEM((c.pipes, c.cs, c.mid), BF16)),
        ("wf", pltpu.VMEM((2, TAPS, c.mid, LANES), BF16)),
        ("wb", pltpu.VMEM((2, TAPS, LANES, c.mid), BF16)),
        ("mask", pltpu.VMEM((TAPS, c.pad, LANES), F32)),
        ("z1", pltpu.VMEM((2,) + full + (LANES,), F32)),
        ("d1", pltpu.VMEM((2,) + full + (LANES,), F32)),
        ("z2", pltpu.VMEM((2,) + full + (LANES,), F32)),
        ("d2", pltpu.VMEM((2,) + full + (LANES,), F32)),
        ("z3", pltpu.VMEM((2,) + full + (c.cs,), F32)),
        ("d3", pltpu.VMEM((2,) + full + (c.cs,), F32)),
        ("e3", pltpu.VMEM(full + (c.cs,), F32)),
        ("t1", pltpu.VMEM(full + (LANES,), F32)),
        ("gr1", pltpu.VMEM((2, c.micro, 1, LANES), F32)),
        ("gr2", pltpu.VMEM((2, c.micro, 1, LANES), F32)),
        ("gr3", pltpu.VMEM((2, c.micro, 1, c.cs), F32)),
        ("h1", pltpu.VMEM((2,) + seg, BF16)),
        ("h2", pltpu.VMEM((2,) + seg, BF16)),
        ("da3", pltpu.VMEM((2,) + full + (c.cs,), BF16)),
        ("da2", pltpu.VMEM((2,) + seg, BF16)),
        ("da1", pltpu.VMEM((2,) + seg, BF16)),
        ("first", pltpu.VMEM(full + (LANES,), BF16)),
        ("put", pltpu.VMEM((4,) + seg, BF16)),
        ("got", pltpu.VMEM((4,) + seg, BF16)),
        ("out_seg", pltpu.VMEM(full + (c.cs,), BF16)),
        ("in_seg", pltpu.VMEM(full + (c.cs,), BF16)),
        ("ar_small", pltpu.VMEM((8, c.dps, c.micro, 2, LANES), F32)),
        ("ar_wide", pltpu.VMEM((4, c.dps, c.micro, 2, c.cs), F32)),
        ("pool", pltpu.VMEM((c.micro * c.images, 1, c.cs), F32)),
        ("bank_put", pltpu.VMEM((c.dps, c.bank, c.cs), F32)),
        ("bank_got", pltpu.VMEM((c.dps, c.bank, c.cs), F32)),
        ("norm_sum", pltpu.VMEM((c.pipes, 6, 8, LANES), F32)),
        ("gp", pltpu.VMEM((c.pipes, c.cs, c.mid), BF16)),
        ("gw", pltpu.VMEM((2, TAPS * c.mid, LANES), BF16)),
        ("ar_s", pltpu.SemaphoreType.DMA((12, c.groups))),
        ("ar_r", pltpu.SemaphoreType.DMA((12, c.groups))),
        ("ag_s", pltpu.SemaphoreType.DMA((8, c.groups))),
        ("ag_r", pltpu.SemaphoreType.DMA((8, c.groups))),
        ("rs_s", pltpu.SemaphoreType.DMA((4, c.groups))),
        ("rs_r", pltpu.SemaphoreType.DMA((4, c.groups))),
        ("w_s", pltpu.SemaphoreType.DMA((3, c.pipes))),
        ("pq_r", pltpu.SemaphoreType.DMA((c.pipes,))),
        ("wf_r", pltpu.SemaphoreType.DMA((2,))),
        ("wb_r", pltpu.SemaphoreType.DMA((2, 2))),
        ("bank_s", pltpu.SemaphoreType.DMA((1,))),
        ("bank_r", pltpu.SemaphoreType.DMA((1,))),
        ("ns_s", pltpu.SemaphoreType.DMA((1,))),
        ("ns_r", pltpu.SemaphoreType.DMA((1,))),
        ("in_r", pltpu.SemaphoreType.DMA((4,))),
        ("out_r", pltpu.SemaphoreType.DMA((6,))),
    ]
    if c.deep:
        prow, wrow = c.cs // 2, TAPS * c.mid // 2
        items += [
            ("p_sib", pltpu.VMEM((c.pipes, prow, c.mid), BF16)),
            ("w_sib", pltpu.VMEM((2, wrow, LANES), BF16)),
            ("p_z", pltpu.VMEM((c.pipes, c.zs, prow // c.zs, c.mid), BF16)),
            ("w_z", pltpu.VMEM((2, c.zs, wrow // c.zs, LANES), BF16)),
            ("p_fin", pltpu.VMEM((c.pipes, prow, c.mid), BF16)),
            ("w_fin", pltpu.VMEM((2, wrow, LANES), BF16)),
            ("p_out", pltpu.VMEM((c.ch, c.mid), BF16)),
            ("w_out", pltpu.VMEM((TAPS * c.mid, 2 * LANES), BF16)),
            ("gs", pltpu.SemaphoreType.DMA((6, 5))),
            ("gr", pltpu.SemaphoreType.DMA((6, 5))),
            ("own_s", pltpu.SemaphoreType.DMA((6,))),
            ("fin_s", pltpu.SemaphoreType.DMA((6,))),
            ("fin_r", pltpu.SemaphoreType.DMA((6,))),
        ]
    return items


def body(c, names, *refs):
    (u_hbm, go_hbm, pw_hbm, sw_hbm, gain_ref, shift_ref, ids_ref) = refs[:7]
    (bo_out, ig_out, gp_out, gw_out, ns_out, mb_out) = refs[7:13]
    s = types.SimpleNamespace(**dict(zip(names, refs[13:])))
    me_p = lax.axis_index("pipe")
    me_d = lax.axis_index("dp")
    me_x = lax.rem(me_p, 2)
    me_y = lax.div(me_p, 2)
    NP, ND, M, GM, G, R = c.pipes, c.dps, c.micro, c.gm, c.groups, c.pad
    flat = GM * R
    count = float(c.total)

    def shard(k, p):
        half = lax.div(p, 2)
        return 2 * lax.rem(p, 2) + (half if k == 0 else 1 - half)

    def pipe_peer(i):
        return lax.rem(me_p + i, NP)

    def dp_peer(i):
        return lax.rem(me_d + i, ND)

    def remote(src, dst, ss, rs, p, d):
        return pltpu.make_async_remote_copy(
            src_ref=src, dst_ref=dst, send_sem=ss, recv_sem=rs, device_id=(p, d), device_id_type=MESH
        )

    def take_recv(view, ss, rs):
        remote(view, view, ss, rs, me_p, me_d).wait_recv()

    def take_send(view, ss, rs):
        remote(view, view, ss, rs, me_p, me_d).wait_send()

    def group(g):
        return pl.ds(g * GM, GM)

    lane0 = pl.multiple_of(me_p * c.cs, LANES)
    seg_cols = pl.ds(lane0, c.cs)
    load_u = pltpu.make_async_copy(u_hbm.at[:, :, seg_cols], s.u_seg.at[0], s.in_r.at[0])
    load_g = pltpu.make_async_copy(go_hbm.at[:, :, seg_cols], s.g_seg, s.in_r.at[1])
    load_all = pltpu.make_async_copy(u_hbm, s.u_all, s.in_r.at[2])
    load_p = pltpu.make_async_copy(pw_hbm, s.p_own, s.in_r.at[3])

    @pl.when(me_p == 0)
    def _():
        load_all.start()
        load_p.start()

    load_u.start()
    load_g.start()

    barrier = pltpu.get_barrier_semaphore()
    for i in range(1, NP):
        pl.semaphore_signal(barrier, inc=1, device_id=(pipe_peer(i), me_d), device_id_type=MESH)

    @pl.loop(1, ND)
    def _(i):
        pl.semaphore_signal(barrier, inc=1, device_id=(me_p, dp_peer(i)), device_id_type=MESH)

    row = lax.broadcasted_iota(jnp.int32, (R, LANES), 0)
    image = jnp.zeros_like(row)
    for n in range(1, c.images):
        image = image + (row >= n * SIDE * SIDE).astype(jnp.int32)
    pixel = row - image * (SIDE * SIDE)
    up = jnp.zeros_like(row)
    for n in range(1, SIDE):
        up = up + (pixel >= n * SIDE).astype(jnp.int32)
    across = pixel - up * SIDE
    for t in range(TAPS):
        i, j = t // 3 - 1, t % 3 - 1
        ok = (up + i >= 0) & (up + i < SIDE) & (across + j >= 0) & (across + j < SIDE) & (row < c.rows)
        s.mask[t] = ok.astype(F32)
    s.norm_sum[...] = jnp.zeros_like(s.norm_sum)

    pl.semaphore_wait(barrier, NP - 1 + ND - 1)

    def rows_of(p):
        return pl.ds(pl.multiple_of(p * c.cs, 16), c.cs)

    def proj_send(i):
        p = pipe_peer(i)
        return remote(pw_hbm.at[rows_of(p)], s.pq.at[me_p], s.w_s.at[0, i], s.pq_r.at[me_p], p, me_d)

    def front_send():
        return remote(
            sw_hbm.at[:, :, pl.ds(LANES, LANES)], s.wf.at[me_y], s.w_s.at[1, 0], s.wf_r.at[me_y], lax.rem(me_p + 2, NP), me_d
        )

    def back_rows(p):
        sh = 2 * lax.rem(p, 2) + lax.rem(lax.div(p, 2) + me_y, 2)
        return pl.ds(pl.multiple_of(sh * LANES, LANES), LANES)

    def back_cols():
        return pl.ds(pl.multiple_of(me_x * 2 * LANES, LANES), 2 * LANES)

    def back_send(i):
        p = pipe_peer(i)
        return remote(
            sw_hbm.at[:, back_rows(p), :], s.wb.at[me_y, :, :, back_cols()], s.w_s.at[2, i], s.wb_r.at[me_y, me_x], p, me_d
        )

    pltpu.make_async_copy(pw_hbm.at[rows_of(me_p)], s.pq.at[me_p], s.pq_r.at[me_p]).start()
    pltpu.make_async_copy(sw_hbm.at[:, :, pl.ds(0, LANES)], s.wf.at[me_y], s.wf_r.at[me_y]).start()
    pltpu.make_async_copy(
        sw_hbm.at[:, back_rows(me_p), :], s.wb.at[me_y, :, :, back_cols()], s.wb_r.at[me_y, me_x]
    ).start()
    front_send().start()

    def need_proj(i):
        pltpu.make_async_copy(s.pq.at[i], s.pq.at[i], s.pq_r.at[i]).wait()

    def need_front(k):
        pltpu.make_async_copy(s.wf.at[k], s.wf.at[k], s.wf_r.at[k]).wait()

    def need_back(k):
        for e in range(2):
            view = s.wb.at[k, :, :, pl.ds(e * 2 * LANES, 2 * LANES)]
            pltpu.make_async_copy(view, view, s.wb_r.at[k, e]).wait()

    def ar_ref(idx):
        return s.ar_small.at[idx] if idx < 8 else s.ar_wide.at[idx - 8]

    def ar_send(idx, g, first, second):
        buf = ar_ref(idx)
        buf[me_d, group(g), 0:1, :] = first
        buf[me_d, group(g), 1:2, :] = second

        @pl.loop(1, ND)
        def _(i):
            view = buf.at[me_d, group(g)]
            remote(view, view, s.ar_s.at[idx, g], s.ar_r.at[idx, g], me_p, dp_peer(i)).start()

    def ar_take(idx, g):
        buf = ar_ref(idx)
        take_recv(buf.at[pl.ds(0, ND - 1), group(g)], s.ar_s.at[idx, g], s.ar_r.at[idx, g])
        tot = buf[0, group(g)]
        for d in range(1, ND):
            tot = tot + buf[d, group(g)]
        return tot[:, 0:1, :], tot[:, 1:2, :]

    def ag_send(idx, g, buf, slot):
        view = buf.at[slot, group(g)]
        for i in range(1, NP):
            remote(view, view, s.ag_s.at[idx, g], s.ag_r.at[idx, g], pipe_peer(i), me_d).start()

    def ag_take(idx, g, buf):
        take_recv(buf.at[pl.ds(0, NP - 1), group(g)], s.ag_s.at[idx, g], s.ag_r.at[idx, g])
        return jnp.concatenate([buf[j, group(g)].reshape(flat, LANES) for j in range(NP)], axis=1)

    def rs_send(idx, g, k, partial):
        for j in range(NP):
            s.put[idx, j, group(g)] = partial[:, j * LANES : (j + 1) * LANES].reshape(GM, R, LANES).astype(BF16)
        for i in range(1, NP):
            p = pipe_peer(i)
            remote(
                s.put.at[idx, shard(k, p), group(g)],
                s.got.at[idx, me_p, group(g)],
                s.rs_s.at[idx, g],
                s.rs_r.at[idx, g],
                p,
                me_d,
            ).start()

    def rs_take(idx, g, k):
        take_recv(s.got.at[idx, pl.ds(0, NP - 1), group(g)], s.rs_s.at[idx, g], s.rs_r.at[idx, g])
        tot = s.put[idx, shard(k, me_p), group(g)].astype(F32)
        for i in range(1, NP):
            tot = tot + s.got[idx, pipe_peer(i), group(g)].astype(F32)
        return tot

    def shard_cols(base, k):
        return pl.ds(pl.multiple_of(base + shard(k, me_p) * LANES, LANES), LANES)

    def norm_cols(which, k):
        if which == 1:
            return shard_cols(0, k)
        if which == 2:
            return shard_cols(c.mid, k)
        return pl.ds(pl.multiple_of(2 * c.mid + me_p * c.cs, LANES), c.cs)

    def real_rows(width):
        return lax.broadcasted_iota(jnp.int32, (GM, R, width), 1) < c.rows

    ZD = {1: (s.z1, s.d1, s.gr1), 2: (s.z2, s.d2, s.gr2), 3: (s.z3, s.d3, s.gr3)}
    FWD = {(0, 1): 0, (0, 2): 1, (1, 1): 2, (1, 2): 3, (0, 3): 8, (1, 3): 9}
    BWD = {(1, 2): 4, (1, 1): 5, (0, 2): 6, (0, 1): 7, (1, 3): 10, (0, 3): 11}

    def stats_out(k, which, g, a):
        ZD[which][0][k, group(g)] = a
        ar_send(FWD[(k, which)], g, jnp.sum(a, axis=1, keepdims=True), jnp.sum(a * a, axis=1, keepdims=True))

    def normed(k, which, g):
        z_ref, _, gr_ref = ZD[which]
        one, two = ar_take(FWD[(k, which)], g)
        mean = one / count
        inv = lax.rsqrt(two / count - mean * mean + EPS)
        z = (z_ref[k, group(g)] - mean) * inv
        z_ref[k, group(g)] = z
        gain = gain_ref[k : k + 1, norm_cols(which, k)][None]
        gr_ref[k, group(g)] = gain * inv
        return z * gain + shift_ref[k : k + 1, norm_cols(which, k)][None]

    def hidden_out(k, which, g, idx, buf):
        act, slope = gelu_pair(normed(k, which, g))
        ZD[which][1][k, group(g)] = slope
        mine = shard(k, me_p)
        buf[k, mine, group(g)] = jnp.where(real_rows(LANES), act, 0.0).astype(BF16)
        ag_send(idx, g, buf.at[k], mine)

    def back_out(k, which, g, up):
        ar_send(
            BWD[(k, which)],
            g,
            jnp.sum(up, axis=1, keepdims=True),
            jnp.sum(up * ZD[which][0][k, group(g)], axis=1, keepdims=True),
        )

    def back_in(k, which, g, up):
        z_ref, _, gr_ref = ZD[which]
        one, two = ar_take(BWD[(k, which)], g)
        chunk0 = {1: 0, 2: 1, 3: 2}[which]
        for n in range(one.shape[-1] // LANES):
            lanes = slice(n * LANES, (n + 1) * LANES)
            s.norm_sum[me_p, chunk0 + n, 2 * k : 2 * k + 1, :] += jnp.sum(two[:, :, lanes], axis=0)
            s.norm_sum[me_p, chunk0 + n, 2 * k + 1 : 2 * k + 2, :] += jnp.sum(one[:, :, lanes], axis=0)
        grad = gr_ref[k, group(g)] * (up - one / count - z_ref[k, group(g)] * (two / count))
        return jnp.where(real_rows(grad.shape[-1]), grad, 0.0).astype(BF16)

    def shifted(v, by):
        by = by % flat
        return v if by == 0 else pltpu.roll(v, by, 0)

    def tap_shift(t):
        return SIDE * (t // 3 - 1) + (t % 3 - 1)

    def masked(v, t):
        return v.reshape(GM, R, LANES) * s.mask[t][None]

    def conv(k, h):
        acc = None
        for t0 in range(0, TAPS, 2):
            taps = [t for t in (t0, t0 + 1) if t < TAPS]
            w = s.wf[k, taps[0]] if len(taps) == 1 else jnp.concatenate([s.wf[k, t] for t in taps], axis=1)
            y = dot(h, w)
            for n, t in enumerate(taps):
                part = masked(shifted(y[:, n * LANES : (n + 1) * LANES], -tap_shift(t)), t)
                acc = part if acc is None else acc + part
        return acc

    def conv_back(k, d):
        acc = None
        for t0 in range(0, TAPS, 2):
            taps = [t for t in (t0, t0 + 1) if t < TAPS]
            w = s.wb[k, taps[0]] if len(taps) == 1 else jnp.concatenate([s.wb[k, t] for t in taps], axis=0)
            y = dot_nt(d, w)
            for n, t in enumerate(taps):
                part = masked(y[:, n * LANES : (n + 1) * LANES], t).reshape(flat, LANES)
                part = shifted(part, tap_shift(t))
                acc = part if acc is None else acc + part
        return acc.reshape(GM, R, LANES)

    @pl.when(me_p == 0)
    def _():
        load_all.wait()
        load_p.wait()

        @pl.loop(0, G)
        def _(g):
            a = dot(s.u_all[group(g)].reshape(flat, c.ch), s.p_own[...])
            for j in range(NP):
                s.put[0, j, group(g)] = a[:, j * LANES : (j + 1) * LANES].reshape(GM, R, LANES).astype(BF16)
            s.first[group(g)] = s.put[0, 0, group(g)]
            for p in range(1, NP):
                remote(
                    s.put.at[0, shard(0, jnp.int32(p)), group(g)], s.first.at[group(g)], s.rs_s.at[0, g], s.rs_r.at[0, g], p, me_d
                ).start()

    for i in range(1, NP):
        proj_send(i).start()

    for k in range(2):

        @pl.loop(0, G)
        def _(g):
            if k == 0:

                @pl.when(me_p != 0)
                def _():
                    take_recv(s.first.at[group(g)], s.rs_s.at[0, g], s.rs_r.at[0, g])

                a = s.first[group(g)].astype(F32)
            else:
                a = rs_take(1, g, 1)
            stats_out(k, 1, g, a)

        @pl.loop(0, G)
        def _(g):
            hidden_out(k, 1, g, 2 * k, s.h1)

        need_front(k)

        @pl.loop(0, G)
        def _(g):
            stats_out(k, 2, g, conv(k, ag_take(2 * k, g, s.h1.at[k])))

        @pl.loop(0, G)
        def _(g):
            hidden_out(k, 2, g, 2 * k + 1, s.h2)

        need_proj(2 * k + 1)
        if k == 0:
            load_u.wait()
            for i in range(1, NP):
                back_send(i).start()

        @pl.loop(0, G)
        def _(g):
            a = dot_nt(ag_take(2 * k + 1, g, s.h2.at[k]), s.pq[2 * k + 1])
            stats_out(k, 3, g, a.reshape(GM, R, c.cs))

        if k == 0:
            need_proj(2)

            @pl.loop(0, G)
            def _(g):
                v = normed(0, 3, g) + s.u_seg[0, group(g)].astype(F32)
                act, slope = gelu_pair(v)
                s.d3[0, group(g)] = slope
                o = jnp.where(real_rows(c.cs), act, 0.0).astype(BF16)
                s.u_seg[1, group(g)] = o
                rs_send(1, g, 1, dot(o.reshape(flat, c.cs), s.pq[2]))

    load_g.wait()

    @pl.loop(0, G)
    def _(g):
        v = normed(1, 3, g) + s.u_seg[1, group(g)].astype(F32)
        act, slope = gelu_pair(v)
        o = jnp.where(real_rows(c.cs), act, 0.0).astype(BF16)
        s.out_seg[group(g)] = o
        e = s.g_seg[group(g)].astype(F32) * slope
        s.e3[group(g)] = e
        back_out(1, 3, g, e)
        o32 = o.astype(F32)
        place = lax.broadcasted_iota(jnp.int32, (GM, R, c.cs), 1)
        for n in range(c.images):
            here = (place >= n * SIDE * SIDE) & (place < (n + 1) * SIDE * SIDE)
            mean = jnp.sum(jnp.where(here, o32, 0.0), axis=1, keepdims=True) / float(SIDE * SIDE)
            for m in range(GM):
                s.pool[(g * GM + m) * c.images + n] = mean[m]

    out_copy = pltpu.make_async_copy(s.out_seg, bo_out, s.out_r.at[0])
    out_copy.start()

    banks = ND * c.bank
    which = lax.broadcasted_iota(jnp.int32, (banks, c.cs), 0)
    term = jnp.zeros((banks, c.cs), F32)
    for n in range(M * c.images):
        ids = jnp.concatenate([ids_ref[n : n + 1, :]] * (c.cs // LANES), axis=1)
        term = term + jnp.where(which == ids, s.pool[n], 0.0)
    s.bank_put[...] = term.reshape(ND, c.bank, c.cs)

    @pl.loop(1, ND)
    def _(i):
        d = dp_peer(i)
        remote(s.bank_put.at[d], s.bank_got.at[me_d], s.bank_s.at[0], s.bank_r.at[0], me_p, d).start()

    s.bank_got[me_d] = s.bank_put[me_d]

    def all_rows(ref):
        return ref[...].reshape(M * R, ref.shape[-1])

    def all_seg(ref):
        return jnp.concatenate([ref[j].reshape(M * R, LANES) for j in range(NP)], axis=1)

    def grad_q(k):
        h = all_seg(s.h2.at[k])
        s.gp[2 * k + 1] = dot_tn(all_rows(s.da3.at[k]), h).astype(BF16)

    def grad_p(k):
        d = all_seg(s.da1.at[k])
        s.gp[2 * k] = dot_tn(all_rows(s.u_seg.at[k]), d).astype(BF16)

    def grad_w(k):
        h = all_seg(s.h1.at[k])
        d = s.da2[k, shard(k, me_p)].astype(F32)
        for t0 in range(0, TAPS, 2):
            taps = [t for t in (t0, t0 + 1) if t < TAPS]
            cols = []
            for t in taps:
                part = (d * s.mask[t][None]).reshape(M * R, LANES)
                by = tap_shift(t) % (M * R)
                cols.append((part if by == 0 else pltpu.roll(part, by, 0)).astype(BF16))
            v = dot_tn(h, cols[0] if len(cols) == 1 else jnp.concatenate(cols, axis=1))
            for n, t in enumerate(taps):
                s.gw[k, t * c.mid : (t + 1) * c.mid, :] = v[:, n * LANES : (n + 1) * LANES].astype(BF16)

    me_c = lax.rem(me_d, 2)
    me_z = lax.div(me_d, 2)
    sib = me_d + 1 - 2 * me_c

    def half_rows(n, which):
        return pl.ds(pl.multiple_of(which * n, 16), n)

    def job_refs(job):
        if job < NP:
            return s.gp.at[job], s.p_sib.at[job], s.p_z.at[job], s.p_fin.at[job], c.cs // 2
        k = job - NP
        return s.gw.at[k], s.w_sib.at[k], s.w_z.at[k], s.w_fin.at[k], TAPS * c.mid // 2

    def z_dev(z):
        return 2 * z + me_c

    def z_peer(i):
        return lax.rem(me_z + i, c.zs)

    def job_core(job):
        own, got, _, _, n = job_refs(job)
        remote(own.at[half_rows(n, 1 - me_c)], got, s.gs.at[job, 0], s.gr.at[job, 0], me_p, sib).start()

    def job_spread(job):
        own, got, zbuf, fin, n = job_refs(job)
        q = n // c.zs
        take_recv(got, s.gs.at[job, 0], s.gr.at[job, 0])
        got[...] = (got[...].astype(F32) + own[half_rows(n, me_c), :].astype(F32)).astype(BF16)
        for i in range(1, c.zs):
            z = z_peer(i)
            remote(got.at[half_rows(q, z)], zbuf.at[me_z], s.gs.at[job, 1], s.gr.at[job, 1], me_p, z_dev(z)).start()
        zbuf[me_z] = got[half_rows(q, me_z), :]

    def job_sum(job):
        _, got, zbuf, fin, n = job_refs(job)
        q = n // c.zs
        if c.zs > 1:
            take_recv(zbuf.at[pl.ds(0, c.zs - 1)], s.gs.at[job, 1], s.gr.at[job, 1])
        tot = zbuf[0].astype(F32)
        for z in range(1, c.zs):
            tot = tot + zbuf[z].astype(F32)
        fin[half_rows(q, me_z), :] = tot.astype(BF16)
        view = fin.at[half_rows(q, me_z)]
        for i in range(1, c.zs):
            remote(view, view, s.gs.at[job, 2], s.gr.at[job, 2], me_p, z_dev(z_peer(i))).start()

    def job_place(job, p, core):
        n = job_refs(job)[4]
        if job < NP:
            return s.p_out.at[pl.ds(pl.multiple_of(p * 2 * n + core * n, 16), n)]
        k = job - NP
        side = lax.div(p, 2) if k == 0 else 1 - lax.div(p, 2)
        return s.w_out.at[half_rows(n, core), pl.ds(pl.multiple_of(side * LANES, LANES), LANES)]

    def job_home(job, p):
        return job if job < NP else 2 * (job - NP) + lax.rem(p, 2)

    def job_holds(job):
        return me_p == job if job < NP else me_y == job - NP

    def job_plane(job):
        _, _, _, fin, n = job_refs(job)
        if c.zs > 1:
            take_recv(fin.at[pl.ds(0, n // c.zs * (c.zs - 1))], s.gs.at[job, 2], s.gr.at[job, 2])
        home = job_home(job, me_p)

        @pl.when(me_p != home)
        def _():
            remote(fin, job_place(job, me_p, me_c), s.gs.at[job, 3], s.gr.at[job, 3], home, me_d).start()

        @pl.when(me_p == home)
        def _():
            pltpu.make_async_copy(fin, job_place(job, me_p, me_c), s.own_s.at[job]).start()

    def job_sources(job):
        if job < NP:
            return [lax.rem(me_p + i, NP) for i in range(1, NP)]
        return [lax.rem(me_p + 2, NP)]

    def job_share(job):
        _, _, _, fin, n = job_refs(job)

        @pl.when(job_holds(job))
        def _():
            pltpu.make_async_copy(fin, job_place(job, me_p, me_c), s.own_s.at[job]).wait()
            src = job_sources(job)
            if job < NP:
                view = s.p_out.at[pl.ds(0, n * len(src))]
            else:
                view = fin
            take_recv(view, s.gs.at[job, 3], s.gr.at[job, 3])
            for p in [me_p] + src:
                view = job_place(job, p, me_c)
                remote(view, view, s.fin_s.at[job], s.fin_r.at[job], me_p, sib).start()

    def job_end(job):
        _, _, _, fin, n = job_refs(job)
        half, q = fin, n // c.zs
        take_send(half, s.gs.at[job, 0], s.gr.at[job, 0])
        if c.zs > 1:
            take_send(fin.at[pl.ds(0, q * (c.zs - 1))], s.gs.at[job, 1], s.gr.at[job, 1])
            take_send(fin.at[pl.ds(0, q * (c.zs - 1))], s.gs.at[job, 2], s.gr.at[job, 2])

        @pl.when(me_p != job_home(job, me_p))
        def _():
            take_send(half, s.gs.at[job, 3], s.gr.at[job, 3])

        @pl.when(job_holds(job))
        def _():
            parts = NP if job < NP else 2
            view = s.p_out.at[pl.ds(0, n * parts)] if job < NP else s.w_out.at[pl.ds(0, n)]
            take_recv(view, s.fin_s.at[job], s.fin_r.at[job])
            take_send(view, s.fin_s.at[job], s.fin_r.at[job])

    for k in (1, 0):
        side = 2 * (1 - k)

        @pl.loop(0, G)
        def _(g):
            grad = back_in(k, 3, g, s.e3[group(g)])
            s.da3[k, group(g)] = grad
            rs_send(2 + (1 - k), g, k, dot(grad.reshape(flat, c.cs), s.pq[2 * k + 1]))

        grad_q(k)

        @pl.loop(0, G)
        def _(g):
            up = rs_take(2 + (1 - k), g, k) * s.d2[k, group(g)]
            s.t1[group(g)] = up
            back_out(k, 2, g, up)

        @pl.loop(0, G)
        def _(g):
            mine = shard(k, me_p)
            s.da2[k, mine, group(g)] = back_in(k, 2, g, s.t1[group(g)])
            ag_send(4 + side, g, s.da2.at[k], mine)

        need_back(k)
        grad_w(k)

        @pl.loop(0, G)
        def _(g):
            up = conv_back(k, ag_take(4 + side, g, s.da2.at[k])) * s.d1[k, group(g)]
            s.t1[group(g)] = up
            back_out(k, 1, g, up)

        @pl.loop(0, G)
        def _(g):
            mine = shard(k, me_p)
            s.da1[k, mine, group(g)] = back_in(k, 1, g, s.t1[group(g)])
            ag_send(5 + side, g, s.da1.at[k], mine)

        if k == 0:
            need_proj(0)
        if k == 1:
            need_proj(3) if False else None

        @pl.loop(0, G)
        def _(g):
            d = dot_nt(ag_take(5 + side, g, s.da1.at[k]), s.pq[2 * k])
            d = d.reshape(GM, R, c.cs) + s.e3[group(g)]
            if k == 1:
                e = d * s.d3[0, group(g)]
                s.e3[group(g)] = e
                back_out(0, 3, g, e)
            else:
                s.in_seg[group(g)] = d.astype(BF16)

        grad_p(k)

    in_copy = pltpu.make_async_copy(s.in_seg, ig_out, s.out_r.at[1])
    in_copy.start()
    view = s.norm_sum.at[me_p]
    for i in range(1, NP):
        remote(view, view, s.ns_s.at[0], s.ns_r.at[0], pipe_peer(i), me_d).start()

    if c.deep:
        order = (3, 5, 2, 1, 4, 0)
        for step in (job_core, job_spread, job_sum, job_plane, job_share):
            for job in order:
                step(job)

    take_recv(s.bank_got.at[pl.ds(0, ND - 1)], s.bank_s.at[0], s.bank_r.at[0])
    tot = s.bank_got[0]
    for d in range(1, ND):
        tot = tot + s.bank_got[d]
    mb_out[...] = tot
    take_recv(s.norm_sum.at[pl.ds(0, NP - 1)], s.ns_s.at[0], s.ns_r.at[0])
    per = c.mid // LANES
    wide = c.cs // LANES
    each = (2 * per + c.ch // LANES) // NP
    for k in range(2):
        for n in range(each):
            q = me_p * each + n
            in_one = q < per
            in_two = (q >= per) & (q < 2 * per)
            sh = jnp.where(in_one, q, q - per)
            half = lax.rem(sh + k, 2)
            small = 2 * half + lax.div(sh, 2)
            far = q - 2 * per
            p = jnp.where(q < 2 * per, small, lax.div(far, wide))
            chunk = jnp.where(in_one, 0, jnp.where(in_two, 1, 2 + lax.rem(far, wide)))
            ns_out[n, 2 * k : 2 * k + 2, :] = s.norm_sum[p, chunk, 2 * k : 2 * k + 2, :]

    if c.deep:
        for job in range(6):
            job_end(job)
        p_copy = pltpu.make_async_copy(s.p_out, gp_out, s.out_r.at[2])
        w_copy = pltpu.make_async_copy(s.w_out, gw_out, s.out_r.at[3])
    else:
        p_copy = pltpu.make_async_copy(s.gp, gp_out, s.out_r.at[2])
        w_copy = pltpu.make_async_copy(s.gw, gw_out, s.out_r.at[3])
    p_copy.start()
    w_copy.start()
    take_send(s.norm_sum.at[pl.ds(0, NP - 1)], s.ns_s.at[0], s.ns_r.at[0])
    take_send(s.bank_got.at[pl.ds(0, ND - 1)], s.bank_s.at[0], s.bank_r.at[0])
    front_send().wait_send()
    for i in range(1, NP):
        proj_send(i).wait_send()
        back_send(i).wait_send()

    @pl.loop(0, G)
    def _(g):
        for idx in range(12):
            take_send(ar_ref(idx).at[pl.ds(0, ND - 1), group(g)], s.ar_s.at[idx, g], s.ar_r.at[idx, g])
        for idx in range(8):
            take_send(s.h1.at[0, pl.ds(0, NP - 1), group(g)], s.ag_s.at[idx, g], s.ag_r.at[idx, g])
        for idx in range(1, 4):
            take_send(s.put.at[idx, pl.ds(0, NP - 1), group(g)], s.rs_s.at[idx, g], s.rs_r.at[idx, g])

        @pl.when(me_p == 0)
        def _():
            take_send(s.put.at[0, pl.ds(0, NP - 1), group(g)], s.rs_s.at[0, g], s.rs_r.at[0, g])

    out_copy.wait()
    in_copy.wait()
    p_copy.wait()
    w_copy.wait()


def on_device(mesh, block_input, proj_weight, spatial_weight, norm_gain, norm_shift, output_grad, image_ids):
    bank = 8
    c = Sizes(mesh, block_input, proj_weight, spatial_weight, bank)
    extra = ((0, 0), (0, c.pad - c.rows), (0, 0))
    u = jnp.pad(block_input, extra)
    go = jnp.pad(output_grad, extra)
    sw = spatial_weight.reshape(TAPS, c.mid, spatial_weight.shape[2])
    ids = jnp.broadcast_to(image_ids.reshape(-1, 1), (image_ids.size, LANES))
    items = scratch_list(c)
    names = [n for n, _ in items]
    anyspec = pl.BlockSpec(memory_space=pl.ANY)
    vspec = pl.BlockSpec(memory_space=pltpu.VMEM)
    if c.deep:
        gp_shape, gw_shape = (c.ch, c.mid), (TAPS * c.mid, 2 * LANES)
    else:
        gp_shape, gw_shape = (c.pipes, c.cs, c.mid), (2, TAPS * c.mid, LANES)
    each = (2 * c.mid + c.ch) // LANES // c.pipes
    outs = pl.pallas_call(
        functools.partial(body, c, names),
        out_shape=(
            jax.ShapeDtypeStruct((c.micro, c.pad, c.cs), BF16),
            jax.ShapeDtypeStruct((c.micro, c.pad, c.cs), BF16),
            jax.ShapeDtypeStruct(gp_shape, BF16),
            jax.ShapeDtypeStruct(gw_shape, BF16),
            jax.ShapeDtypeStruct((each, 4, LANES), F32),
            jax.ShapeDtypeStruct((bank, c.cs), F32),
        ),
        in_specs=[anyspec] * 4 + [vspec] * 3,
        out_specs=(anyspec, anyspec, anyspec, anyspec, vspec, vspec),
        scratch_shapes=[v for _, v in items],
        compiler_params=pltpu.CompilerParams(collective_id=0, has_side_effects=True, vmem_limit_bytes=60 << 20),
    )(u, go, proj_weight[0], sw, norm_gain, norm_shift, ids)
    bo, ig, gp, gw, ns, mb = outs
    if not c.deep:
        gp = lax.psum(gp.astype(F32), "dp")
        gw = lax.psum(gw.astype(F32), "dp")
        gp = lax.all_to_all(gp, "pipe", 0, 0, tiled=True).reshape(c.ch, c.mid)
        gw = lax.all_gather(gw, "pipe")
        me = lax.axis_index("pipe")
        y, x = me // 2, me % 2
        near = lax.dynamic_index_in_dim(gw, me, 0, keepdims=False)
        far = lax.dynamic_index_in_dim(gw, 2 * (1 - y) + x, 0, keepdims=False)
        gw = jnp.concatenate(
            [lax.dynamic_index_in_dim(near, y, 0, keepdims=False), lax.dynamic_index_in_dim(far, y, 0, keepdims=False)],
            axis=1,
        )
    ns = jnp.transpose(ns.reshape(each, 2, 2, LANES), (2, 1, 0, 3)).reshape(2, 2, each * LANES)
    return (
        bo[:, : c.rows],
        ig[:, : c.rows],
        gp.astype(F32)[None],
        gw.astype(F32)[None],
        ns[0],
        ns[1],
        mb,
    )


def solution(mesh):
    return jax.shard_map(
        functools.partial(on_device, mesh),
        mesh=mesh,
        in_specs=(
            P(None, "dp", None),
            P("pipe", None, None),
            P("pipe", None, None),
            P(),
            P(),
            P(None, "dp", None),
            P(None, "dp"),
        ),
        out_specs=(
            P(None, "dp", "pipe"),
            P(None, "dp", "pipe"),
            P("pipe", None, None),
            P("pipe", None, None),
            P(None, "pipe"),
            P(None, "pipe"),
            P("dp", "pipe"),
        ),
        check_vma=False,
    )
```

```python
import functools
import math
import types

import jax
import jax.numpy as jnp
from jax import lax
from jax.experimental import pallas as pl
from jax.experimental.pallas import tpu as pltpu
from jax.sharding import PartitionSpec as P

SIDE = 7
TAPS = 9
EPS = 1e-05
LANES = 128
GROUPS = 4
W_PIECES = 3
P_PIECES = 2
POINTS = (
    (0,),
    (0,),
    (1, 2, 3),
    (0, 1, 2, 3),
    (0,),
    (4, 0, 1),
    (5, 4, 0, 1, 2),
    (5, 1, 2, 3),
    (6, 7, 8, 4, 0, 1, 2, 3),
    (5, 6, 7, 8, 4, 2, 3),
    (9, 10, 5, 4, 1, 3),
    (9, 10, 6, 5, 4, 2),
)
LAST = (5, 6, 4, 3, 7, 9, 8, 10)
MESH = pl.DeviceIdType.MESH
F32 = jnp.float32
BF16 = jnp.bfloat16


def gelu_pair(v):
    c0 = math.sqrt(2.0 / math.pi)
    c1 = 0.044715
    sq = v * v
    t = jnp.tanh(c0 * v * (1.0 + c1 * sq))
    half = 0.5 + 0.5 * t
    slope = half + (0.5 * c0) * v * (1.0 - t * t) * (1.0 + (3.0 * c1) * sq)
    return v * half, slope


def dot(a, b):
    return jnp.dot(a, b, preferred_element_type=F32)


def dot_nt(a, b):
    return lax.dot_general(a, b, (((1,), (1,)), ((), ())), preferred_element_type=F32)


def dot_tn(a, b):
    return lax.dot_general(a, b, (((0,), (0,)), ((), ())), preferred_element_type=F32)


class Sizes:
    def __init__(self, mesh, block_input, proj, spatial, bank_rows):
        self.pipes = mesh.shape["pipe"]
        self.dps = mesh.shape["dp"]
        self.micro = block_input.shape[0]
        self.rows = block_input.shape[1]
        self.pad = -(-self.rows // 16) * 16
        self.ch = block_input.shape[2]
        self.mid = proj.shape[2]
        self.images = self.rows // (SIDE * SIDE)
        self.cs = self.ch // self.pipes
        self.msd = self.mid // self.pipes
        self.groups = GROUPS
        self.gm = self.micro // self.groups
        self.zs = self.dps // 2
        self.total = self.rows * self.dps
        self.bank = bank_rows
        self.deep = self.zs == 4
        self.jobs = {}
        taps = TAPS // W_PIECES
        for k in (1, 0):
            self.jobs[len(self.jobs)] = ("q", k, self.cs // 2, 0, 1 - k)
            for i in range(W_PIECES):
                self.jobs[len(self.jobs)] = ("w", k, taps * self.mid // 2, i * taps * self.mid, (1 - k) * W_PIECES + i)
            if k == 1:
                self.jobs[len(self.jobs)] = ("p", k, self.cs // 2, 0, 2)
        for i in range(P_PIECES):
            self.jobs[len(self.jobs)] = ("0", 0, self.ch // P_PIECES // 2, i * self.ch // P_PIECES, i)


def scratch_list(c):
    full = (c.micro, c.pad)
    seg = (c.pipes, c.micro, c.pad, LANES)
    items = [
        ("u_all", pltpu.VMEM(full + (c.ch,), BF16)),
        ("u_seg", pltpu.VMEM((2,) + full + (c.cs,), BF16)),
        ("g_seg", pltpu.VMEM(full + (c.cs,), BF16)),
        ("p_own", pltpu.VMEM((c.ch, c.mid), BF16)),
        ("pq", pltpu.VMEM((c.pipes, c.cs, c.mid), BF16)),
        ("wf", pltpu.VMEM((2, TAPS, c.mid, LANES), BF16)),
        ("wb", pltpu.VMEM((2, 4, TAPS, LANES, LANES), BF16)),
        ("sw", pltpu.VMEM((2, TAPS, c.mid, LANES), BF16)),
        ("mask", pltpu.VMEM((TAPS, c.pad, LANES), F32)),
        ("z1", pltpu.VMEM((2,) + full + (LANES,), F32)),
        ("d1", pltpu.VMEM((2,) + full + (LANES,), F32)),
        ("z2", pltpu.VMEM((2,) + full + (LANES,), F32)),
        ("d2", pltpu.VMEM((2,) + full + (LANES,), F32)),
        ("z3", pltpu.VMEM((2,) + full + (c.cs,), F32)),
        ("d3", pltpu.VMEM((2,) + full + (c.cs,), F32)),
        ("e3", pltpu.VMEM(full + (c.cs,), F32)),
        ("t1", pltpu.VMEM(full + (LANES,), F32)),
        ("gr1", pltpu.VMEM((2, c.micro, 1, LANES), F32)),
        ("gr2", pltpu.VMEM((2, c.micro, 1, LANES), F32)),
        ("gr3", pltpu.VMEM((2, c.micro, 1, c.cs), F32)),
        ("h1", pltpu.VMEM((2,) + seg, BF16)),
        ("h2", pltpu.VMEM((2,) + seg, BF16)),
        ("da3", pltpu.VMEM((2,) + full + (c.cs,), BF16)),
        ("da2", pltpu.VMEM((2,) + seg, BF16)),
        ("da1", pltpu.VMEM((2,) + seg, BF16)),
        ("first", pltpu.VMEM(full + (LANES,), BF16)),
        ("put", pltpu.VMEM((4,) + seg, BF16)),
        ("got", pltpu.VMEM((4,) + seg, BF16)),
        ("out_seg", pltpu.VMEM(full + (c.cs,), BF16)),
        ("in_seg", pltpu.VMEM(full + (c.cs,), BF16)),
        ("ar_small", pltpu.VMEM((8, c.dps, c.micro, 2, LANES), F32)),
        ("ar_wide", pltpu.VMEM((4, c.dps, c.micro, 2, c.cs), F32)),
        ("pool", pltpu.VMEM((c.micro * c.images, 1, c.cs), F32)),
        ("bank_put", pltpu.VMEM((c.dps, c.bank, c.cs), F32)),
        ("bank_got", pltpu.VMEM((c.dps, c.bank, c.cs), F32)),
        ("norm_sum", pltpu.VMEM((c.pipes, 6, 8, LANES), F32)),
        ("gp", pltpu.VMEM((c.pipes, c.cs, c.mid), BF16)),
        ("g0", pltpu.VMEM((c.ch, LANES), BF16)),
        ("gw", pltpu.VMEM((2, TAPS * c.mid, LANES), BF16)),
        ("ar_s", pltpu.SemaphoreType.DMA((12, c.groups))),
        ("ar_r", pltpu.SemaphoreType.DMA((12, c.groups))),
        ("ag_s", pltpu.SemaphoreType.DMA((8, c.groups))),
        ("ag_r", pltpu.SemaphoreType.DMA((8, c.groups))),
        ("rs_s", pltpu.SemaphoreType.DMA((4, c.groups))),
        ("rs_r", pltpu.SemaphoreType.DMA((4, c.groups))),
        ("w_s", pltpu.SemaphoreType.DMA((3, c.pipes))),
        ("pass_s", pltpu.SemaphoreType.DMA((3, c.pipes))),
        ("pq_r", pltpu.SemaphoreType.DMA((c.pipes,))),
        ("pq_q", pltpu.SemaphoreType.DMA((c.pipes,))),
        ("wf_r", pltpu.SemaphoreType.DMA((2,))),
        ("wf_q", pltpu.SemaphoreType.DMA((2,))),
        ("wb_r", pltpu.SemaphoreType.DMA((2, 2))),
        ("wb_q", pltpu.SemaphoreType.DMA((2, 2))),
        ("bank_s", pltpu.SemaphoreType.DMA((1,))),
        ("bank_r", pltpu.SemaphoreType.DMA((1,))),
        ("ns_s", pltpu.SemaphoreType.DMA((1,))),
        ("ns_r", pltpu.SemaphoreType.DMA((1,))),
        ("in_r", pltpu.SemaphoreType.DMA((6,))),
        ("out_r", pltpu.SemaphoreType.DMA((4 + c.pipes,))),
    ]
    if c.deep:
        for name, width in (("p", c.mid), ("w", LANES), ("0", LANES)):
            of = [job for job in c.jobs.values() if job[0] in {"p": "pq"}.get(name, name)]
            lead, n = len(of), of[0][2]
            items += [(key + name, pltpu.VMEM((lead, n // (1 + (key == "jd")), width), BF16)) for key in ("ja", "jb", "jc", "jd", "je")]
        count = len(c.jobs)
        items += [
            ("p_out", pltpu.VMEM((c.ch, c.mid), BF16)),
            ("p0_out", pltpu.VMEM((c.pipes, c.ch, LANES), BF16)),
            ("w_out", pltpu.VMEM((2, TAPS * c.mid, LANES), BF16)),
            ("gs", pltpu.SemaphoreType.DMA((count, 7))),
            ("gr", pltpu.SemaphoreType.DMA((count, 6))),
            ("own_s", pltpu.SemaphoreType.DMA((count,))),
            ("fin_s", pltpu.SemaphoreType.DMA((count,))),
            ("fin_r", pltpu.SemaphoreType.DMA((count,))),
        ]
    return items


def body(c, names, *refs):
    (u_hbm, go_hbm, pw_hbm, sw_hbm, gain_ref, shift_ref, ids_ref) = refs[:7]
    (bo_out, ig_out, gp_out, gw_out, ns_out, mb_out) = refs[7:13]
    s = types.SimpleNamespace(**dict(zip(names, refs[13:])))
    me_p = lax.axis_index("pipe")
    me_d = lax.axis_index("dp")
    me_x = lax.rem(me_p, 2)
    me_y = lax.div(me_p, 2)
    NP, ND, M, GM, G, R = c.pipes, c.dps, c.micro, c.gm, c.groups, c.pad
    flat = GM * R
    count = float(c.total)

    def shard(k, p):
        half = lax.div(p, 2)
        return 2 * lax.rem(p, 2) + (half if k == 0 else 1 - half)

    def pipe_peer(i):
        return lax.rem(me_p + i, NP)

    def dp_peer(i):
        return lax.rem(me_d + i, ND)

    def remote(src, dst, ss, rs, p, d):
        return pltpu.make_async_remote_copy(
            src_ref=src, dst_ref=dst, send_sem=ss, recv_sem=rs, device_id=(p, d), device_id_type=MESH
        )

    def take_recv(view, ss, rs):
        remote(view, view, ss, rs, me_p, me_d).wait_recv()

    def take_send(view, ss, rs):
        remote(view, view, ss, rs, me_p, me_d).wait_send()

    def group(g):
        return pl.ds(g * GM, GM)

    owed, due = {}, {}

    lane0 = pl.multiple_of(me_p * c.cs, LANES)
    seg_cols = pl.ds(lane0, c.cs)
    load_u = pltpu.make_async_copy(u_hbm.at[:, :, seg_cols], s.u_seg.at[0], s.in_r.at[0])
    load_g = pltpu.make_async_copy(go_hbm.at[:, :, seg_cols], s.g_seg, s.in_r.at[1])
    load_all = pltpu.make_async_copy(u_hbm, s.u_all, s.in_r.at[2])
    load_p = pltpu.make_async_copy(pw_hbm, s.p_own, s.in_r.at[3])
    load_w = [
        pltpu.make_async_copy(sw_hbm.at[:, :, pl.ds(h * LANES, LANES)], s.sw.at[h], s.in_r.at[4 + h]) for h in range(2)
    ]
    load_all.start()

    @pl.when(me_p == 0)
    def _():
        load_p.start()

    for load in load_w:
        load.start()
    load_u.start()
    load_g.start()

    barrier = pltpu.get_barrier_semaphore()
    for i in range(1, NP):
        pl.semaphore_signal(barrier, inc=1, device_id=(pipe_peer(i), me_d), device_id_type=MESH)

    @pl.loop(1, ND)
    def _(i):
        pl.semaphore_signal(barrier, inc=1, device_id=(me_p, dp_peer(i)), device_id_type=MESH)

    row = lax.broadcasted_iota(jnp.int32, (R, LANES), 0)
    image = jnp.zeros_like(row)
    for n in range(1, c.images):
        image = image + (row >= n * SIDE * SIDE).astype(jnp.int32)
    pixel = row - image * (SIDE * SIDE)
    up = jnp.zeros_like(row)
    for n in range(1, SIDE):
        up = up + (pixel >= n * SIDE).astype(jnp.int32)
    across = pixel - up * SIDE
    for t in range(TAPS):
        i, j = t // 3 - 1, t % 3 - 1
        ok = (up + i >= 0) & (up + i < SIDE) & (across + j >= 0) & (across + j < SIDE) & (row < c.rows)
        s.mask[t] = ok.astype(F32)
    s.norm_sum[...] = jnp.zeros_like(s.norm_sum)

    pl.semaphore_wait(barrier, NP - 1 + ND - 1)

    me_c = lax.rem(me_d, 2)
    me_z = lax.div(me_d, 2)
    sib = me_d + 1 - 2 * me_c

    def rows_of(p):
        return pl.ds(pl.multiple_of(p * c.cs, 16), c.cs)

    def half_of(n, which):
        return pl.ds(pl.multiple_of(which * (n // 2), 16), n // 2)

    def proj_half(i, core):
        return s.pq.at[i, half_of(c.cs, core)]

    def proj_send(i):
        p = pipe_peer(i)
        src = pw_hbm.at[pl.ds(pl.multiple_of(p * c.cs + me_c * (c.cs // 2), 16), c.cs // 2)]
        return remote(src, proj_half(me_p, me_c), s.w_s.at[0, i], s.pq_r.at[me_p], p, me_d)

    def proj_pass(i):
        view = proj_half(i, me_c)
        return remote(view, view, s.pass_s.at[0, i], s.pq_q.at[i], me_p, sib)

    def pass_proj(i):
        @pl.when(me_p != i)
        def _():
            take_recv(proj_half(i, me_c), s.pass_s.at[0, i], s.pq_r.at[i])
            proj_pass(i).start()

    def need_proj(i):
        @pl.when(me_p != i)
        def _():
            take_recv(proj_half(i, 1 - me_c), s.pass_s.at[0, i], s.pq_q.at[i])

        @pl.when(me_p == i)
        def _():
            pltpu.make_async_copy(s.pq.at[i], s.pq.at[i], s.pq_r.at[i]).wait()

    def end_proj(i):
        @pl.when(me_p != i)
        def _():
            proj_pass(i).wait_send()

    def front_half(k, core):
        return s.wf.at[k, :, half_of(c.mid, core)]

    def front_send():
        return remote(
            s.sw.at[1, :, half_of(c.mid, me_c)],
            front_half(me_y, me_c),
            s.w_s.at[1, 0],
            s.wf_r.at[me_y],
            lax.rem(me_p + 2, NP),
            me_d,
        )

    def front_pass(k):
        view = front_half(k, me_c)
        return remote(view, view, s.pass_s.at[1, k], s.wf_q.at[k], me_p, sib)

    def pass_front(k):
        @pl.when(me_y != k)
        def _():
            take_recv(front_half(k, me_c), s.pass_s.at[1, k], s.wf_r.at[k])
            front_pass(k).start()

    def need_front(k):
        @pl.when(me_y != k)
        def _():
            take_recv(front_half(k, 1 - me_c), s.pass_s.at[1, k], s.wf_q.at[k])

        @pl.when(me_y == k)
        def _():
            pltpu.make_async_copy(s.wf.at[k], s.wf.at[k], s.wf_r.at[k]).wait()

    def end_front(k):
        @pl.when(me_y != k)
        def _():
            front_pass(k).wait_send()

    def back_rows(p):
        sh = 2 * lax.rem(p, 2) + lax.rem(lax.div(p, 2) + me_y, 2)
        return pl.ds(pl.multiple_of(sh * LANES, LANES), LANES)

    def back_send(i):
        p = pipe_peer(i)
        return remote(
            s.sw.at[me_c, :, back_rows(p)],
            s.wb.at[me_y, 2 * me_x + me_c],
            s.w_s.at[2, i],
            s.wb_r.at[me_y, me_x],
            p,
            me_d,
        )

    def back_pass(k, e):
        view = s.wb.at[k, 2 * e + me_c]
        return remote(view, view, s.pass_s.at[2, 2 * k + e], s.wb_q.at[k, e], me_p, sib)

    def pass_back(k):
        for e in range(2):

            @pl.when(me_p != 2 * k + e)
            def _():
                take_recv(s.wb.at[k, 2 * e + me_c], s.pass_s.at[2, 2 * k + e], s.wb_r.at[k, e])
                back_pass(k, e).start()

    def need_back(k):
        for e in range(2):

            @pl.when(me_p != 2 * k + e)
            def _():
                take_recv(s.wb.at[k, 2 * e + 1 - me_c], s.pass_s.at[2, 2 * k + e], s.wb_q.at[k, e])

            @pl.when(me_p == 2 * k + e)
            def _():
                view = s.wb.at[k, pl.ds(2 * e, 2)]
                pltpu.make_async_copy(view, view, s.wb_r.at[k, e]).wait()

    def end_back(k):
        for e in range(2):

            @pl.when(me_p != 2 * k + e)
            def _():
                back_pass(k, e).wait_send()

    for load in load_w:
        load.wait()
    front_send().start()
    pltpu.make_async_copy(pw_hbm.at[rows_of(me_p)], s.pq.at[me_p], s.pq_r.at[me_p]).start()
    pltpu.make_async_copy(s.sw.at[0], s.wf.at[me_y], s.wf_r.at[me_y]).start()
    pltpu.make_async_copy(
        s.sw.at[:, :, back_rows(me_p)], s.wb.at[me_y, pl.ds(2 * me_x, 2)], s.wb_r.at[me_y, me_x]
    ).start()

    def note(kind, idx, view, ss, rs):
        owed[kind, idx] = lambda g: take_send(view(g), ss.at[idx, g], rs.at[idx, g])
        due[kind, idx] = lambda g: take_recv(view(g), ss.at[idx, g], rs.at[idx, g])

    def grab(kind, idx, g):
        due.pop((kind, idx))(g)

    def ar_ref(idx):
        return s.ar_small.at[idx] if idx < 8 else s.ar_wide.at[idx - 8]

    def ar_send(idx, g, first, second):
        buf = ar_ref(idx)
        buf[me_d, group(g), 0:1, :] = first
        buf[me_d, group(g), 1:2, :] = second

        @pl.loop(1, ND)
        def _(i):
            view = buf.at[me_d, group(g)]
            remote(view, view, s.ar_s.at[idx, g], s.ar_r.at[idx, g], me_p, dp_peer(i)).start()

        note("ar", idx, lambda g: ar_ref(idx).at[pl.ds(0, ND - 1), group(g)], s.ar_s, s.ar_r)

    def ar_take(idx, g):
        buf = ar_ref(idx)
        grab("ar", idx, g)
        tot = buf[0, group(g)]
        for d in range(1, ND):
            tot = tot + buf[d, group(g)]
        return tot[:, 0:1, :], tot[:, 1:2, :]

    def ag_send(idx, g, buf, slot):
        view = buf.at[slot, group(g)]
        for i in range(1, NP):
            remote(view, view, s.ag_s.at[idx, g], s.ag_r.at[idx, g], pipe_peer(i), me_d).start()
        note("ag", idx, lambda g: s.h1.at[0, pl.ds(0, NP - 1), group(g)], s.ag_s, s.ag_r)

    def ag_take(idx, g, buf):
        grab("ag", idx, g)
        return jnp.concatenate([buf[j, group(g)].reshape(flat, LANES) for j in range(NP)], axis=1)

    def rs_send(idx, g, k, partial):
        for j in range(NP):
            s.put[idx, j, group(g)] = partial[:, j * LANES : (j + 1) * LANES].reshape(GM, R, LANES).astype(BF16)
        for i in range(1, NP):
            p = pipe_peer(i)
            remote(
                s.put.at[idx, shard(k, p), group(g)],
                s.got.at[idx, me_p, group(g)],
                s.rs_s.at[idx, g],
                s.rs_r.at[idx, g],
                p,
                me_d,
            ).start()
        note("rs", idx, lambda g: s.got.at[idx, pl.ds(0, NP - 1), group(g)], s.rs_s, s.rs_r)

    def rs_take(idx, g, k):
        grab("rs", idx, g)
        tot = s.put[idx, shard(k, me_p), group(g)].astype(F32)
        for i in range(1, NP):
            tot = tot + s.got[idx, pipe_peer(i), group(g)].astype(F32)
        return tot

    def shard_cols(base, k):
        return pl.ds(pl.multiple_of(base + shard(k, me_p) * LANES, LANES), LANES)

    def norm_cols(which, k):
        if which == 1:
            return shard_cols(0, k)
        if which == 2:
            return shard_cols(c.mid, k)
        return pl.ds(pl.multiple_of(2 * c.mid + me_p * c.cs, LANES), c.cs)

    def real_rows(width):
        return lax.broadcasted_iota(jnp.int32, (GM, R, width), 1) < c.rows

    ZD = {1: (s.z1, s.d1, s.gr1), 2: (s.z2, s.d2, s.gr2), 3: (s.z3, s.d3, s.gr3)}
    FWD = {(0, 1): 0, (0, 2): 1, (1, 1): 2, (1, 2): 3, (0, 3): 8, (1, 3): 9}
    BWD = {(1, 2): 4, (1, 1): 5, (0, 2): 6, (0, 1): 7, (1, 3): 10, (0, 3): 11}

    def stats_out(k, which, g, a):
        ZD[which][0][k, group(g)] = a
        ar_send(FWD[(k, which)], g, jnp.sum(a, axis=1, keepdims=True), jnp.sum(a * a, axis=1, keepdims=True))

    def normed(k, which, g):
        z_ref, _, gr_ref = ZD[which]
        one, two = ar_take(FWD[(k, which)], g)
        mean = one / count
        inv = lax.rsqrt(two / count - mean * mean + EPS)
        z = (z_ref[k, group(g)] - mean) * inv
        z_ref[k, group(g)] = z
        gain = gain_ref[k : k + 1, norm_cols(which, k)][None]
        gr_ref[k, group(g)] = gain * inv
        return z * gain + shift_ref[k : k + 1, norm_cols(which, k)][None]

    def hidden_out(k, which, g, idx, buf):
        act, slope = gelu_pair(normed(k, which, g))
        ZD[which][1][k, group(g)] = slope
        mine = shard(k, me_p)
        buf[k, mine, group(g)] = jnp.where(real_rows(LANES), act, 0.0).astype(BF16)
        ag_send(idx, g, buf.at[k], mine)

    def back_out(k, which, g, up):
        ar_send(
            BWD[(k, which)],
            g,
            jnp.sum(up, axis=1, keepdims=True),
            jnp.sum(up * ZD[which][0][k, group(g)], axis=1, keepdims=True),
        )

    def back_in(k, which, g, up):
        z_ref, _, gr_ref = ZD[which]
        one, two = ar_take(BWD[(k, which)], g)
        chunk0 = {1: 0, 2: 1, 3: 2}[which]
        for n in range(one.shape[-1] // LANES):
            lanes = slice(n * LANES, (n + 1) * LANES)
            s.norm_sum[me_p, chunk0 + n, 2 * k : 2 * k + 1, :] += jnp.sum(two[:, :, lanes], axis=0)
            s.norm_sum[me_p, chunk0 + n, 2 * k + 1 : 2 * k + 2, :] += jnp.sum(one[:, :, lanes], axis=0)
        grad = gr_ref[k, group(g)] * (up - one / count - z_ref[k, group(g)] * (two / count))
        return jnp.where(real_rows(grad.shape[-1]), grad, 0.0).astype(BF16)

    def shifted(v, by):
        by = by % flat
        return v if by == 0 else pltpu.roll(v, by, 0)

    def tap_shift(t):
        return SIDE * (t // 3 - 1) + (t % 3 - 1)

    def masked(v, t):
        return v.reshape(GM, R, LANES) * s.mask[t][None]

    def conv(k, h):
        acc = None
        for t0 in range(0, TAPS, 2):
            taps = [t for t in (t0, t0 + 1) if t < TAPS]
            w = s.wf[k, taps[0]] if len(taps) == 1 else jnp.concatenate([s.wf[k, t] for t in taps], axis=1)
            y = dot(h, w)
            for n, t in enumerate(taps):
                part = masked(shifted(y[:, n * LANES : (n + 1) * LANES], -tap_shift(t)), t)
                acc = part if acc is None else acc + part
        return acc

    def conv_back(k, d):
        acc = None
        for t0 in range(0, TAPS, 2):
            taps = [t for t in (t0, t0 + 1) if t < TAPS]
            w = [jnp.concatenate([s.wb[k, o, t] for o in range(4)], axis=1) for t in taps]
            w = w[0] if len(taps) == 1 else jnp.concatenate(w, axis=0)
            y = dot_nt(d, w)
            for n, t in enumerate(taps):
                part = masked(y[:, n * LANES : (n + 1) * LANES], t).reshape(flat, LANES)
                part = shifted(part, tap_shift(t))
                acc = part if acc is None else acc + part
        return acc.reshape(GM, R, LANES)

    tail, ends = [], []

    def work():
        load_all.wait()

        @pl.when(me_p == 0)
        def _():
            load_p.wait()

            @pl.loop(0, G)
            def _(g):
                a = dot(s.u_all[group(g)].reshape(flat, c.ch), s.p_own[...])
                for j in range(NP):
                    s.put[0, j, group(g)] = a[:, j * LANES : (j + 1) * LANES].reshape(GM, R, LANES).astype(BF16)
                s.first[group(g)] = s.put[0, 0, group(g)]
                for p in range(1, NP):
                    remote(
                        s.put.at[0, shard(0, jnp.int32(p)), group(g)], s.first.at[group(g)], s.rs_s.at[0, g], s.rs_r.at[0, g], p, me_d
                    ).start()

        for i in range(1, NP):
            proj_send(i).start()
            tail.append(proj_send(i).wait_send)

        for k in range(2):

            @pl.loop(0, G)
            def _(g):
                if k == 0:

                    @pl.when(me_p != 0)
                    def _():
                        take_recv(s.first.at[group(g)], s.rs_s.at[0, g], s.rs_r.at[0, g])

                    a = s.first[group(g)].astype(F32)
                else:
                    a = rs_take(1, g, 1)
                stats_out(k, 1, g, a)
            if k == 0:
                pass_front(0)

            @pl.loop(0, G)
            def _(g):
                hidden_out(k, 1, g, 2 * k, s.h1)

            if k == 1:
                pass_proj(3)
            need_front(k)

            @pl.loop(0, G)
            def _(g):
                stats_out(k, 2, g, conv(k, ag_take(2 * k, g, s.h1.at[k])))
            if k == 0:
                pass_proj(1)

            @pl.loop(0, G)
            def _(g):
                hidden_out(k, 2, g, 2 * k + 1, s.h2)
            if k == 1:
                for i in range(1, NP):
                    back_send(i).start()
                    tail.append(back_send(i).wait_send)

            need_proj(2 * k + 1)
            if k == 0:
                load_u.wait()
                pass_proj(2)

            @pl.loop(0, G)
            def _(g):
                a = dot_nt(ag_take(2 * k + 1, g, s.h2.at[k]), s.pq[2 * k + 1])
                stats_out(k, 3, g, a.reshape(GM, R, c.cs))

            if k == 0:
                need_proj(2)

                @pl.loop(0, G)
                def _(g):
                    v = normed(0, 3, g) + s.u_seg[0, group(g)].astype(F32)
                    act, slope = gelu_pair(v)
                    s.d3[0, group(g)] = slope
                    o = jnp.where(real_rows(c.cs), act, 0.0).astype(BF16)
                    s.u_seg[1, group(g)] = o
                    rs_send(1, g, 1, dot(o.reshape(flat, c.cs), s.pq[2]))
                pass_front(1)

        load_g.wait()

        @pl.loop(0, G)
        def _(g):
            v = normed(1, 3, g) + s.u_seg[1, group(g)].astype(F32)
            act, slope = gelu_pair(v)
            o = jnp.where(real_rows(c.cs), act, 0.0).astype(BF16)
            s.out_seg[group(g)] = o
            e = s.g_seg[group(g)].astype(F32) * slope
            s.e3[group(g)] = e
            back_out(1, 3, g, e)
            o32 = o.astype(F32)
            place = lax.broadcasted_iota(jnp.int32, (GM, R, c.cs), 1)
            for n in range(c.images):
                here = (place >= n * SIDE * SIDE) & (place < (n + 1) * SIDE * SIDE)
                mean = jnp.sum(jnp.where(here, o32, 0.0), axis=1, keepdims=True) / float(SIDE * SIDE)
                for m in range(GM):
                    s.pool[(g * GM + m) * c.images + n] = mean[m]

        out_copy = pltpu.make_async_copy(s.out_seg, bo_out, s.out_r.at[0])
        out_copy.start()
        tail.append(out_copy.wait)

        banks = ND * c.bank
        which = lax.broadcasted_iota(jnp.int32, (banks, c.cs), 0)
        term = jnp.zeros((banks, c.cs), F32)
        for n in range(M * c.images):
            ids = jnp.concatenate([ids_ref[n : n + 1, :]] * (c.cs // LANES), axis=1)
            term = term + jnp.where(which == ids, s.pool[n], 0.0)
        s.bank_put[...] = term.reshape(ND, c.bank, c.cs)

        @pl.loop(1, ND)
        def _(i):
            d = dp_peer(i)
            remote(s.bank_put.at[d], s.bank_got.at[me_d], s.bank_s.at[0], s.bank_r.at[0], me_p, d).start()

        tail.append(lambda: take_send(s.bank_got.at[pl.ds(0, ND - 1)], s.bank_s.at[0], s.bank_r.at[0]))

        s.bank_got[me_d] = s.bank_put[me_d]

        def all_rows(ref):
            return ref[...].reshape(M * R, ref.shape[-1])

        def all_seg(ref):
            return jnp.concatenate([ref[j].reshape(M * R, LANES) for j in range(NP)], axis=1)

        def grad_q(k):
            h = all_seg(s.h2.at[k])
            s.gp[2 * k + 1] = dot_tn(all_rows(s.da3.at[k]), h).astype(BF16)

        def grad_p0():
            d = s.da1[0, shard(0, me_p)].reshape(M * R, LANES)
            s.g0[...] = dot_tn(all_rows(s.u_all), d).astype(BF16)

        def grad_p(k):
            d = all_seg(s.da1.at[k])
            s.gp[2 * k] = dot_tn(all_rows(s.u_seg.at[k]), d).astype(BF16)

        def grad_w(k):
            h = all_seg(s.h1.at[k])
            d = s.da2[k, shard(k, me_p)].astype(F32)
            for t0 in range(0, TAPS, 2):
                taps = [t for t in (t0, t0 + 1) if t < TAPS]
                cols = []
                for t in taps:
                    part = (d * s.mask[t][None]).reshape(M * R, LANES)
                    by = tap_shift(t) % (M * R)
                    cols.append((part if by == 0 else pltpu.roll(part, by, 0)).astype(BF16))
                v = dot_tn(h, cols[0] if len(cols) == 1 else jnp.concatenate(cols, axis=1))
                for n, t in enumerate(taps):
                    s.gw[k, t * c.mid : (t + 1) * c.mid, :] = v[:, n * LANES : (n + 1) * LANES].astype(BF16)

        def part(base, n):
            return pl.ds(pl.multiple_of(base, 16), n)

        inner = (me_z == 1) | (me_z == 2)
        z_side = lax.div(me_z, 2)
        outer_dev = 2 * (3 * z_side) + me_c
        inner_dev = 2 * (1 + z_side) + me_c
        across_dev = 2 * (2 - z_side) + me_c

        def job_own(job):
            kind, k, n, base, slot = c.jobs[job]
            ref = s.g0 if kind == "0" else s.gw.at[k] if kind == "w" else s.gp.at[2 * k + (kind == "q")]
            return ref, base

        def job_ref(name, job):
            kind, k, n, base, slot = c.jobs[job]
            return getattr(s, name + ("p" if kind in "pq" else kind)).at[slot]

        def job_core(job):
            own, base = job_own(job)
            n = c.jobs[job][2]
            view = own.at[part(base + (1 - me_c) * n, n)]
            remote(view, job_ref("ja", job), s.gs.at[job, 0], s.gr.at[job, 0], me_p, sib).start()

        def job_in(job):
            own, base = job_own(job)
            n = c.jobs[job][2]
            got, tot = job_ref("ja", job), job_ref("jb", job)
            take_recv(got, s.gs.at[job, 0], s.gr.at[job, 0])
            tot[...] = (got[...].astype(F32) + own[part(base + me_c * n, n), :].astype(F32)).astype(BF16)

            @pl.when(jnp.logical_not(inner))
            def _():
                remote(tot, job_ref("jc", job), s.gs.at[job, 1], s.gr.at[job, 1], me_p, inner_dev).start()

        def job_halve(job):
            n = c.jobs[job][2]
            got, tot, half = job_ref("jc", job), job_ref("jb", job), job_ref("jd", job)

            @pl.when(inner)
            def _():
                take_recv(got, s.gs.at[job, 1], s.gr.at[job, 1])
                tot[...] = (got[...].astype(F32) + tot[...].astype(F32)).astype(BF16)
                view = tot.at[part((1 - z_side) * (n // 2), n // 2)]
                remote(view, half, s.gs.at[job, 2], s.gr.at[job, 2], me_p, across_dev).start()

        def job_sum(job):
            n = c.jobs[job][2]
            tot, half, fin = job_ref("jb", job), job_ref("jd", job), job_ref("je", job)
            mine = part(z_side * (n // 2), n // 2)

            @pl.when(inner)
            def _():
                take_recv(half, s.gs.at[job, 2], s.gr.at[job, 2])
                fin[mine, :] = (half[...].astype(F32) + tot[mine, :].astype(F32)).astype(BF16)
                view = fin.at[mine]
                remote(view, view, s.gs.at[job, 3], s.gr.at[job, 3], me_p, across_dev).start()
                remote(view, view, s.gs.at[job, 4], s.gr.at[job, 3], me_p, outer_dev).start()

        def job_out(job):
            n = c.jobs[job][2]
            fin = job_ref("je", job)
            view = fin.at[part((1 - z_side) * (n // 2), n // 2)]

            @pl.when(inner)
            def _():
                take_recv(view, s.gs.at[job, 3], s.gr.at[job, 3])
                remote(view, view, s.gs.at[job, 5], s.gr.at[job, 4], me_p, outer_dev).start()

        def job_place(job, p, core):
            kind, k, n, base, slot = c.jobs[job]
            if kind == "0":
                return s.p0_out.at[shard(0, p), part(base + core * n, n)]
            if kind == "w":
                return s.w_out.at[lax.div(p, 2) if k == 0 else 1 - lax.div(p, 2), part(base + core * n, n)]
            return s.p_out.at[part(p * 2 * n + core * n, n)]

        def job_home(job, p):
            kind, k = c.jobs[job][:2]
            return 2 * k + lax.rem(p, 2) if kind == "w" else jnp.int32(2 * k + (kind == "q"))

        def job_holds(job):
            kind, k = c.jobs[job][:2]
            return me_y == k if kind == "w" else me_p == 2 * k + (kind == "q")

        def job_plane(job):
            n = c.jobs[job][2]
            fin = job_ref("je", job)

            @pl.when(jnp.logical_not(inner))
            def _():
                for step in (3, 4):
                    take_recv(fin.at[part(0, n // 2)], s.gs.at[job, step], s.gr.at[job, step])

            home = job_home(job, me_p)

            @pl.when(me_p != home)
            def _():
                remote(fin, job_place(job, me_p, me_c), s.gs.at[job, 6], s.gr.at[job, 5], home, me_d).start()

            @pl.when(me_p == home)
            def _():
                pltpu.make_async_copy(fin, job_place(job, me_p, me_c), s.own_s.at[job]).start()

        def job_many(job, count):
            kind, k, n, base, slot = c.jobs[job]
            if kind == "0":
                return s.p0_out.at[pl.ds(0, count), pl.ds(0, n)]
            return s.w_out.at[pl.ds(0, count), pl.ds(0, n)] if kind == "w" else s.p_out.at[pl.ds(0, n * count)]

        def job_share(job):
            fin = job_ref("je", job)
            from_pipes = [0, 2] if c.jobs[job][0] == "w" else [0, 1, 2, 3]

            @pl.when(job_holds(job))
            def _():
                pltpu.make_async_copy(fin, job_place(job, me_p, me_c), s.own_s.at[job]).wait()
                take_recv(job_many(job, len(from_pipes) - 1), s.gs.at[job, 6], s.gr.at[job, 5])
                for i in from_pipes:
                    view = job_place(job, pipe_peer(i), me_c)
                    remote(view, view, s.fin_s.at[job], s.fin_r.at[job], me_p, sib).start()

        def job_end(job):
            got, half, fin = job_ref("ja", job), job_ref("jd", job), job_ref("je", job)
            take_send(got, s.gs.at[job, 0], s.gr.at[job, 0])

            @pl.when(inner)
            def _():
                for step in (2, 3, 4, 5):
                    take_send(half, s.gs.at[job, step], s.gr.at[job, 2])

            @pl.when(jnp.logical_not(inner))
            def _():
                take_send(got, s.gs.at[job, 1], s.gr.at[job, 1])

            @pl.when(me_p != job_home(job, me_p))
            def _():
                take_send(fin, s.gs.at[job, 6], s.gr.at[job, 5])

            @pl.when(job_holds(job))
            def _():
                view = job_many(job, 2 if c.jobs[job][0] == "w" else NP)
                take_recv(view, s.fin_s.at[job], s.fin_r.at[job])
                take_send(view, s.fin_s.at[job], s.fin_r.at[job])

        steps = (job_core, job_in, job_halve, job_sum, job_out, job_plane, job_share)
        next_step = dict.fromkeys(c.jobs, 0)

        def advance(*jobs):
            if c.deep:
                for job in jobs:
                    if next_step[job] < len(steps):
                        steps[next_step[job]](job)
                        next_step[job] += 1

        def point(k, n):
            advance(*POINTS[(1 - k) * 6 + n])

        for k in (1, 0):
            side = 2 * (1 - k)

            @pl.loop(0, G)
            def _(g):
                grad = back_in(k, 3, g, s.e3[group(g)])
                s.da3[k, group(g)] = grad
                rs_send(2 + (1 - k), g, k, dot(grad.reshape(flat, c.cs), s.pq[2 * k + 1]))
            if k == 1:
                pass_back(1)
            else:
                pass_back(0)

            grad_q(k)
            if k == 1:
                pass_proj(0)
            point(k, 0)

            @pl.loop(0, G)
            def _(g):
                up = rs_take(2 + (1 - k), g, k) * s.d2[k, group(g)]
                s.t1[group(g)] = up
                back_out(k, 2, g, up)
            point(k, 1)

            @pl.loop(0, G)
            def _(g):
                mine = shard(k, me_p)
                s.da2[k, mine, group(g)] = back_in(k, 2, g, s.t1[group(g)])
                ag_send(4 + side, g, s.da2.at[k], mine)

            need_back(k)
            grad_w(k)
            point(k, 2)

            @pl.loop(0, G)
            def _(g):
                up = conv_back(k, ag_take(4 + side, g, s.da2.at[k])) * s.d1[k, group(g)]
                s.t1[group(g)] = up
                back_out(k, 1, g, up)
            point(k, 3)

            @pl.loop(0, G)
            def _(g):
                mine = shard(k, me_p)
                s.da1[k, mine, group(g)] = back_in(k, 1, g, s.t1[group(g)])
                ag_send(5 + side, g, s.da1.at[k], mine)
            if k == 0:
                grad_p0()
            point(k, 4)

            if k == 0:
                need_proj(0)
            @pl.loop(0, G)
            def _(g):
                d = dot_nt(ag_take(5 + side, g, s.da1.at[k]), s.pq[2 * k])
                d = d.reshape(GM, R, c.cs) + s.e3[group(g)]
                if k == 1:
                    e = d * s.d3[0, group(g)]
                    s.e3[group(g)] = e
                    back_out(0, 3, g, e)
                else:
                    s.in_seg[group(g)] = d.astype(BF16)

            if k == 1 or not c.deep:
                grad_p(k)
            point(k, 5)

        in_copy = pltpu.make_async_copy(s.in_seg, ig_out, s.out_r.at[1])
        in_copy.start()
        tail.append(in_copy.wait)
        view = s.norm_sum.at[me_p]
        for i in range(1, NP):
            remote(view, view, s.ns_s.at[0], s.ns_r.at[0], pipe_peer(i), me_d).start()
        tail.append(lambda: take_send(s.norm_sum.at[pl.ds(0, NP - 1)], s.ns_s.at[0], s.ns_r.at[0]))

        if c.deep:
            while min(next_step.values()) < len(steps):
                advance(*LAST)
            ends.extend(functools.partial(job_end, job) for job in c.jobs)

        take_recv(s.bank_got.at[pl.ds(0, ND - 1)], s.bank_s.at[0], s.bank_r.at[0])
        tot = s.bank_got[0]
        for d in range(1, ND):
            tot = tot + s.bank_got[d]
        mb_out[...] = tot
        take_recv(s.norm_sum.at[pl.ds(0, NP - 1)], s.ns_s.at[0], s.ns_r.at[0])
        per = c.mid // LANES
        wide = c.cs // LANES
        each = (2 * per + c.ch // LANES) // NP
        for k in range(2):
            for n in range(each):
                q = me_p * each + n
                in_one = q < per
                in_two = (q >= per) & (q < 2 * per)
                sh = jnp.where(in_one, q, q - per)
                half = lax.rem(sh + k, 2)
                small = 2 * half + lax.div(sh, 2)
                far = q - 2 * per
                p = jnp.where(q < 2 * per, small, lax.div(far, wide))
                chunk = jnp.where(in_one, 0, jnp.where(in_two, 1, 2 + lax.rem(far, wide)))
                ns_out[n, 2 * k : 2 * k + 2, :] = s.norm_sum[p, chunk, 2 * k : 2 * k + 2, :]

    work()

    for wait in ends:
        wait()
    if c.deep:
        copies = [
            pltpu.make_async_copy(s.w_out.at[h], gw_out.at[:, pl.ds(h * LANES, LANES)], s.out_r.at[2 + h]) for h in range(2)
        ]
        wide = [
            pltpu.make_async_copy(s.p0_out.at[j], gp_out.at[:, pl.ds(j * LANES, LANES)], s.out_r.at[4 + j])
            for j in range(NP)
        ]
        tall = pltpu.make_async_copy(s.p_out, gp_out, s.out_r.at[4])
        for copy in copies:
            copy.start()
        for act in ("start", "wait"):

            @pl.when(me_p == 0)
            def _():
                for copy in wide:
                    getattr(copy, act)()

            @pl.when(me_p != 0)
            def _():
                getattr(tall, act)()

    else:
        copies = [
            pltpu.make_async_copy(s.gp, gp_out, s.out_r.at[2]),
            pltpu.make_async_copy(s.gw, gw_out, s.out_r.at[3]),
        ]
        for copy in copies:
            copy.start()
    front_send().wait_send()
    for i in range(NP):
        end_proj(i)
    for k in range(2):
        end_front(k)
        end_back(k)

    @pl.loop(0, G)
    def _(g):
        for wait in [*due.values(), *owed.values()]:
            wait(g)

        @pl.when(me_p == 0)
        def _():
            take_send(s.put.at[0, pl.ds(0, NP - 1), group(g)], s.rs_s.at[0, g], s.rs_r.at[0, g])

    for wait in tail:
        wait()
    for copy in copies:
        copy.wait()


def on_device(mesh, block_input, proj_weight, spatial_weight, norm_gain, norm_shift, output_grad, image_ids):
    bank = 8
    c = Sizes(mesh, block_input, proj_weight, spatial_weight, bank)
    extra = ((0, 0), (0, c.pad - c.rows), (0, 0))
    u = jnp.pad(block_input, extra)
    go = jnp.pad(output_grad, extra)
    sw = spatial_weight.reshape(TAPS, c.mid, spatial_weight.shape[2])
    ids = jnp.broadcast_to(image_ids.reshape(-1, 1), (image_ids.size, LANES))
    items = scratch_list(c)
    names = [n for n, _ in items]
    anyspec = pl.BlockSpec(memory_space=pl.ANY)
    vspec = pl.BlockSpec(memory_space=pltpu.VMEM)
    if c.deep:
        gp_shape, gw_shape = (c.ch, c.mid), (TAPS * c.mid, 2 * LANES)
    else:
        gp_shape, gw_shape = (c.pipes, c.cs, c.mid), (2, TAPS * c.mid, LANES)
    each = (2 * c.mid + c.ch) // LANES // c.pipes
    outs = pl.pallas_call(
        functools.partial(body, c, names),
        out_shape=(
            jax.ShapeDtypeStruct((c.micro, c.pad, c.cs), BF16),
            jax.ShapeDtypeStruct((c.micro, c.pad, c.cs), BF16),
            jax.ShapeDtypeStruct(gp_shape, BF16),
            jax.ShapeDtypeStruct(gw_shape, BF16),
            jax.ShapeDtypeStruct((each, 4, LANES), F32),
            jax.ShapeDtypeStruct((bank, c.cs), F32),
        ),
        in_specs=[anyspec] * 4 + [vspec] * 3,
        out_specs=(anyspec, anyspec, anyspec, anyspec, vspec, vspec),
        scratch_shapes=[v for _, v in items],
        compiler_params=pltpu.CompilerParams(collective_id=0, has_side_effects=True, vmem_limit_bytes=60 << 20),
    )(u, go, proj_weight[0], sw, norm_gain, norm_shift, ids)
    bo, ig, gp, gw, ns, mb = outs
    if not c.deep:
        gp = lax.psum(gp.astype(F32), "dp")
        gw = lax.psum(gw.astype(F32), "dp")
        gp = lax.all_to_all(gp, "pipe", 0, 0, tiled=True).reshape(c.ch, c.mid)
        gw = lax.all_gather(gw, "pipe")
        me = lax.axis_index("pipe")
        y, x = me // 2, me % 2
        near = lax.dynamic_index_in_dim(gw, me, 0, keepdims=False)
        far = lax.dynamic_index_in_dim(gw, 2 * (1 - y) + x, 0, keepdims=False)
        gw = jnp.concatenate(
            [lax.dynamic_index_in_dim(near, y, 0, keepdims=False), lax.dynamic_index_in_dim(far, y, 0, keepdims=False)],
            axis=1,
        )
    ns = jnp.transpose(ns.reshape(each, 2, 2, LANES), (2, 1, 0, 3)).reshape(2, 2, each * LANES)
    return (
        bo[:, : c.rows],
        ig[:, : c.rows],
        gp.astype(F32)[None],
        gw.astype(F32)[None],
        ns[0],
        ns[1],
        mb,
    )


def solution(mesh):
    return jax.shard_map(
        functools.partial(on_device, mesh),
        mesh=mesh,
        in_specs=(
            P(None, "dp", None),
            P("pipe", None, None),
            P("pipe", None, None),
            P(),
            P(),
            P(None, "dp", None),
            P(None, "dp"),
        ),
        out_specs=(
            P(None, "dp", "pipe"),
            P(None, "dp", "pipe"),
            P("pipe", None, None),
            P("pipe", None, None),
            P(None, "pipe"),
            P(None, "pipe"),
            P("dp", "pipe"),
        ),
        check_vma=False,
    )
```

```python
import functools
import math
import types

import jax
import jax.numpy as jnp
from jax import lax
from jax.experimental import pallas as pl
from jax.experimental.pallas import tpu as pltpu
from jax.sharding import PartitionSpec as P

SIDE = 7
TAPS = 9
EPS = 1e-05
LANES = 128
GROUPS = 4
W_PIECES = 3
P_PIECES = 2
POINTS = (
    (0,),
    (0,),
    (0, 1, 2, 3),
    (0, 1, 2),
    (0, 1),
    (1, 2, 3, 4),
    (0, 1, 2, 3, 4, 5),
    (2, 3, 4, 5),
    (6, 7, 8, 1, 2, 3, 4, 5),
    (6, 7, 8, 5, 4),
    (9, 10, 6, 5, 3, 4),
    (9, 10, 6, 7, 8, 5),
)
LAST = (0, 1, 2, 5, 6, 7, 8, 9, 10, 4, 3)
MESH = pl.DeviceIdType.MESH
F32 = jnp.float32
BF16 = jnp.bfloat16


def gelu_pair(v):
    c0 = math.sqrt(2.0 / math.pi)
    c1 = 0.044715
    sq = v * v
    t = jnp.tanh(c0 * v * (1.0 + c1 * sq))
    half = 0.5 + 0.5 * t
    slope = half + (0.5 * c0) * v * (1.0 - t * t) * (1.0 + (3.0 * c1) * sq)
    return v * half, slope


def dot(a, b):
    return jnp.dot(a, b, preferred_element_type=F32)


def dot_nt(a, b):
    return lax.dot_general(a, b, (((1,), (1,)), ((), ())), preferred_element_type=F32)


def dot_tn(a, b):
    return lax.dot_general(a, b, (((0,), (0,)), ((), ())), preferred_element_type=F32)


class Sizes:
    def __init__(self, mesh, block_input, proj, spatial, bank_rows):
        self.pipes = mesh.shape["pipe"]
        self.dps = mesh.shape["dp"]
        self.micro = block_input.shape[0]
        self.rows = block_input.shape[1]
        self.pad = -(-self.rows // 16) * 16
        self.ch = block_input.shape[2]
        self.mid = proj.shape[2]
        self.images = self.rows // (SIDE * SIDE)
        self.cs = self.ch // self.pipes
        self.msd = self.mid // self.pipes
        self.groups = GROUPS
        self.gm = self.micro // self.groups
        self.zs = self.dps // 2
        self.total = self.rows * self.dps
        self.bank = bank_rows
        self.deep = self.zs == 4
        self.jobs = {}
        taps = TAPS // W_PIECES
        for k in (1, 0):
            self.jobs[len(self.jobs)] = ("q", k, self.cs // 2, 0, 1 - k)
            for i in range(W_PIECES):
                self.jobs[len(self.jobs)] = ("w", k, taps * self.mid // 2, i * taps * self.mid, (1 - k) * W_PIECES + i)
            if k == 1:
                self.jobs[len(self.jobs)] = ("p", k, self.cs // 2, 0, 2)
        for i in range(P_PIECES):
            self.jobs[len(self.jobs)] = ("0", 0, self.ch // P_PIECES // 2, i * self.ch // P_PIECES, i)


def scratch_list(c):
    full = (c.micro, c.pad)
    seg = (c.pipes, c.micro, c.pad, LANES)
    items = [
        ("u_all", pltpu.VMEM(full + (c.ch,), BF16)),
        ("u_seg", pltpu.VMEM((2,) + full + (c.cs,), BF16)),
        ("g_seg", pltpu.VMEM(full + (c.cs,), BF16)),
        ("p_own", pltpu.VMEM((c.ch, c.mid), BF16)),
        ("pq", pltpu.VMEM((c.pipes, c.cs, c.mid), BF16)),
        ("wf", pltpu.VMEM((2, TAPS, c.mid, LANES), BF16)),
        ("sw", pltpu.VMEM((2, TAPS, c.mid, LANES), BF16)),
        ("mask", pltpu.VMEM((TAPS, c.pad, LANES), F32)),
        ("z1", pltpu.VMEM((2,) + full + (LANES,), F32)),
        ("d1", pltpu.VMEM((2,) + full + (LANES,), F32)),
        ("z2", pltpu.VMEM((2,) + full + (LANES,), F32)),
        ("d2", pltpu.VMEM((2,) + full + (LANES,), F32)),
        ("z3", pltpu.VMEM((2,) + full + (c.cs,), F32)),
        ("d3", pltpu.VMEM((2,) + full + (c.cs,), F32)),
        ("e3", pltpu.VMEM(full + (c.cs,), F32)),
        ("t1", pltpu.VMEM(full + (LANES,), F32)),
        ("gr1", pltpu.VMEM((2, c.micro, 1, LANES), F32)),
        ("gr2", pltpu.VMEM((2, c.micro, 1, LANES), F32)),
        ("gr3", pltpu.VMEM((2, c.micro, 1, c.cs), F32)),
        ("h1", pltpu.VMEM((2,) + seg, BF16)),
        ("h2", pltpu.VMEM((2,) + seg, BF16)),
        ("da3", pltpu.VMEM((2,) + full + (c.cs,), BF16)),
        ("dcol", pltpu.VMEM((2,) + full + (TAPS * LANES,), BF16)),
        ("da1", pltpu.VMEM((2,) + seg, BF16)),
        ("first", pltpu.VMEM(full + (LANES,), BF16)),
        ("put", pltpu.VMEM((6,) + seg, BF16)),
        ("got", pltpu.VMEM((6,) + seg, BF16)),
        ("out_seg", pltpu.VMEM(full + (c.cs,), BF16)),
        ("in_seg", pltpu.VMEM(full + (c.cs,), BF16)),
        ("ar_small", pltpu.VMEM((8, c.dps, c.micro, 2, LANES), F32)),
        ("ar_wide", pltpu.VMEM((4, c.dps, c.micro, 2, c.cs), F32)),
        ("pool", pltpu.VMEM((c.micro * c.images, 1, c.cs), F32)),
        ("bank_put", pltpu.VMEM((c.dps, c.bank, c.cs), F32)),
        ("bank_got", pltpu.VMEM((c.dps, c.bank, c.cs), F32)),
        ("norm_sum", pltpu.VMEM((c.pipes, 6, 8, LANES), F32)),
        ("gp", pltpu.VMEM((c.pipes, c.cs, c.mid), BF16)),
        ("g0", pltpu.VMEM((c.ch, LANES), BF16)),
        ("gw", pltpu.VMEM((2, TAPS * c.mid, LANES), BF16)),
        ("ar_s", pltpu.SemaphoreType.DMA((12, c.groups))),
        ("ar_r", pltpu.SemaphoreType.DMA((12, c.groups))),
        ("ag_s", pltpu.SemaphoreType.DMA((8, c.groups))),
        ("ag_r", pltpu.SemaphoreType.DMA((8, c.groups))),
        ("rs_s", pltpu.SemaphoreType.DMA((6, c.groups))),
        ("rs_r", pltpu.SemaphoreType.DMA((6, c.groups))),
        ("w_s", pltpu.SemaphoreType.DMA((2, c.pipes))),
        ("pass_s", pltpu.SemaphoreType.DMA((6, 3))),
        ("w_r", pltpu.SemaphoreType.DMA((6,))),
        ("w_z", pltpu.SemaphoreType.DMA((6,))),
        ("w_q", pltpu.SemaphoreType.DMA((6,))),
        ("bank_s", pltpu.SemaphoreType.DMA((1,))),
        ("bank_r", pltpu.SemaphoreType.DMA((1,))),
        ("ns_s", pltpu.SemaphoreType.DMA((1,))),
        ("ns_r", pltpu.SemaphoreType.DMA((1,))),
        ("in_r", pltpu.SemaphoreType.DMA((6,))),
        ("out_r", pltpu.SemaphoreType.DMA((4 + c.pipes,))),
    ]
    if c.deep:
        for name, width in (("p", c.mid), ("w", LANES), ("0", LANES)):
            of = [job for job in c.jobs.values() if job[0] in {"p": "pq"}.get(name, name)]
            lead, n = len(of), of[0][2]
            items += [(key + name, pltpu.VMEM((lead, n // (1 + (key == "jd")), width), BF16)) for key in ("ja", "jb", "jc", "jd", "je")]
        count = len(c.jobs)
        items += [
            ("p_out", pltpu.VMEM((c.ch, c.mid), BF16)),
            ("p0_out", pltpu.VMEM((c.pipes, c.ch, LANES), BF16)),
            ("w_out", pltpu.VMEM((2, TAPS * c.mid, LANES), BF16)),
            ("gs", pltpu.SemaphoreType.DMA((count, 7))),
            ("gr", pltpu.SemaphoreType.DMA((count, 6))),
            ("own_s", pltpu.SemaphoreType.DMA((count,))),
            ("fin_s", pltpu.SemaphoreType.DMA((count,))),
            ("fin_r", pltpu.SemaphoreType.DMA((count,))),
        ]
    return items


def body(c, names, *refs):
    (u_hbm, go_hbm, pw_hbm, sw_hbm, gain_ref, shift_ref, ids_ref) = refs[:7]
    (bo_out, ig_out, gp_out, gw_out, ns_out, mb_out) = refs[7:13]
    s = types.SimpleNamespace(**dict(zip(names, refs[13:])))
    me_p = lax.axis_index("pipe")
    me_d = lax.axis_index("dp")
    me_x = lax.rem(me_p, 2)
    me_y = lax.div(me_p, 2)
    NP, ND, M, GM, G, R = c.pipes, c.dps, c.micro, c.gm, c.groups, c.pad
    flat = GM * R
    count = float(c.total)

    def shard(k, p):
        half = lax.div(p, 2)
        return 2 * lax.rem(p, 2) + (half if k == 0 else 1 - half)

    def pipe_peer(i):
        return lax.rem(me_p + i, NP)

    def dp_peer(i):
        return lax.rem(me_d + i, ND)

    def remote(src, dst, ss, rs, p, d):
        return pltpu.make_async_remote_copy(
            src_ref=src, dst_ref=dst, send_sem=ss, recv_sem=rs, device_id=(p, d), device_id_type=MESH
        )

    def take_recv(view, ss, rs):
        remote(view, view, ss, rs, me_p, me_d).wait_recv()

    def take_send(view, ss, rs):
        remote(view, view, ss, rs, me_p, me_d).wait_send()

    def group(g):
        return pl.ds(g * GM, GM)

    owed, due = {}, {}

    lane0 = pl.multiple_of(me_p * c.cs, LANES)
    seg_cols = pl.ds(lane0, c.cs)
    load_u = pltpu.make_async_copy(u_hbm.at[:, :, seg_cols], s.u_seg.at[0], s.in_r.at[0])
    load_g = pltpu.make_async_copy(go_hbm.at[:, :, seg_cols], s.g_seg, s.in_r.at[1])
    load_all = pltpu.make_async_copy(u_hbm, s.u_all, s.in_r.at[2])
    load_p = pltpu.make_async_copy(pw_hbm, s.p_own, s.in_r.at[3])
    load_w = [
        pltpu.make_async_copy(sw_hbm.at[:, :, pl.ds(h * LANES, LANES)], s.sw.at[h], s.in_r.at[4 + h]) for h in range(2)
    ]
    load_all.start()

    @pl.when(me_p == 0)
    def _():
        load_p.start()

    for load in load_w:
        load.start()
    load_u.start()
    load_g.start()

    barrier = pltpu.get_barrier_semaphore()
    for i in range(1, NP):
        pl.semaphore_signal(barrier, inc=1, device_id=(pipe_peer(i), me_d), device_id_type=MESH)

    @pl.loop(1, ND)
    def _(i):
        pl.semaphore_signal(barrier, inc=1, device_id=(me_p, dp_peer(i)), device_id_type=MESH)

    row = lax.broadcasted_iota(jnp.int32, (R, LANES), 0)
    image = jnp.zeros_like(row)
    for n in range(1, c.images):
        image = image + (row >= n * SIDE * SIDE).astype(jnp.int32)
    pixel = row - image * (SIDE * SIDE)
    up = jnp.zeros_like(row)
    for n in range(1, SIDE):
        up = up + (pixel >= n * SIDE).astype(jnp.int32)
    across = pixel - up * SIDE
    for t in range(TAPS):
        i, j = t // 3 - 1, t % 3 - 1
        ok = (up + i >= 0) & (up + i < SIDE) & (across + j >= 0) & (across + j < SIDE) & (row < c.rows)
        s.mask[t] = ok.astype(F32)
    s.norm_sum[...] = jnp.zeros_like(s.norm_sum)

    pl.semaphore_wait(barrier, NP - 1 + ND - 1)

    me_c = lax.rem(me_d, 2)
    me_z = lax.div(me_d, 2)
    sib = me_d + 1 - 2 * me_c

    def link_peer(i):
        flip = me_p + 1 - 2 * me_x
        return (None, flip, lax.rem(me_p + 2, NP), lax.rem(flip + 2, NP))[i]

    def on_pipes(*pipes):
        here = me_p == pipes[0]
        for p in pipes[1:]:
            here = here | (me_p == p)
        return pl.when(here)

    me_l = lax.rem(me_z, 2)
    low = 2 * (me_z + 1 - 2 * me_l) + me_c

    def quarter(part, core, z):
        if part < 4:
            return s.pq.at[part, pl.ds(pl.multiple_of((2 * core + z) * (c.cs // 4), 16), c.cs // 4)]
        return s.wf.at[part - 4, :, pl.ds(pl.multiple_of((2 * core + z) * (c.mid // 4), 16), c.mid // 4)]

    def whole_part(part, core):
        if part < 4:
            return s.pq.at[part] if core is None else s.pq.at[part, pl.ds(pl.multiple_of(core * (c.cs // 2), 16), c.cs // 2)]
        rows = pl.ds(0, c.mid) if core is None else pl.ds(pl.multiple_of(core * (c.mid // 2), 16), c.mid // 2)
        return s.wf.at[part - 4, :, rows]

    def here_already(part):
        return me_p == part if part < 4 else me_y == part - 4

    def proj_send(i):
        p = link_peer(i)
        n = c.cs // 4
        base = (2 * me_c + me_l) * n
        src = pw_hbm.at[pl.ds(pl.multiple_of(p * c.cs + base, 16), n)]
        dst = s.pq.at[me_p, pl.ds(pl.multiple_of(base, 16), n)]
        return remote(src, dst, s.w_s.at[0, i], s.w_r.at[me_p], p, me_d)

    def front_send():
        rows = pl.ds(pl.multiple_of((2 * me_c + me_l) * (c.mid // 4), 16), c.mid // 4)
        return remote(s.sw.at[1, :, rows], s.wf.at[me_y, :, rows], s.w_s.at[1, 0], s.w_r.at[4 + me_y], link_peer(2), me_d)

    def pass_copies(part):
        near, far = quarter(part, me_c, me_l), quarter(part, me_c, 1 - me_l)
        return (
            remote(near, near, s.pass_s.at[part, 0], s.w_z.at[part], me_p, low),
            remote(near, near, s.pass_s.at[part, 1], s.w_q.at[part], me_p, sib),
            remote(far, far, s.pass_s.at[part, 2], s.w_q.at[part], me_p, sib),
        )

    def pass_one(*parts):
        for part in parts:

            @pl.when(jnp.logical_not(here_already(part)))
            def _():
                take_recv(quarter(part, me_c, me_l), s.pass_s.at[part, 0], s.w_r.at[part])
                for copy in pass_copies(part)[:2]:
                    copy.start()

    def pass_two(*parts):
        for part in parts:

            @pl.when(jnp.logical_not(here_already(part)))
            def _():
                take_recv(quarter(part, me_c, 1 - me_l), s.pass_s.at[part, 0], s.w_z.at[part])
                pass_copies(part)[2].start()

    def need(*parts):
        for part in parts:

            @pl.when(jnp.logical_not(here_already(part)))
            def _():
                take_recv(whole_part(part, 1 - me_c), s.pass_s.at[part, 0], s.w_q.at[part])

            @pl.when(here_already(part))
            def _():
                pltpu.make_async_copy(whole_part(part, None), whole_part(part, None), s.w_r.at[part]).wait()

    def end_part(part):
        @pl.when(jnp.logical_not(here_already(part)))
        def _():
            for copy in pass_copies(part):
                copy.wait_send()

    for load in load_w:
        load.wait()

    @on_pipes(1)
    def _():
        front_send().start()

    @on_pipes(2)
    def _():
        for i in range(1, NP):
            proj_send(i).start()

    own_rows = pl.ds(pl.multiple_of(me_p * c.cs, 16), c.cs)
    pltpu.make_async_copy(pw_hbm.at[own_rows], s.pq.at[me_p], s.w_r.at[me_p]).start()
    pltpu.make_async_copy(s.sw.at[0], s.wf.at[me_y], s.w_r.at[4 + me_y]).start()

    def note(kind, idx, view, ss, rs):
        owed[kind, idx] = lambda g: take_send(view(g), ss.at[idx, g], rs.at[idx, g])
        due[kind, idx] = lambda g: take_recv(view(g), ss.at[idx, g], rs.at[idx, g])

    def grab(kind, idx, g):
        due.pop((kind, idx))(g)

    def ar_ref(idx):
        return s.ar_small.at[idx] if idx < 8 else s.ar_wide.at[idx - 8]

    def ar_send(idx, g, first, second):
        buf = ar_ref(idx)
        buf[me_d, group(g), 0:1, :] = first
        buf[me_d, group(g), 1:2, :] = second

        @pl.loop(1, ND)
        def _(i):
            view = buf.at[me_d, group(g)]
            remote(view, view, s.ar_s.at[idx, g], s.ar_r.at[idx, g], me_p, dp_peer(i)).start()

        note("ar", idx, lambda g: ar_ref(idx).at[pl.ds(0, ND - 1), group(g)], s.ar_s, s.ar_r)

    def ar_take(idx, g):
        buf = ar_ref(idx)
        grab("ar", idx, g)
        tot = buf[0, group(g)]
        for d in range(1, ND):
            tot = tot + buf[d, group(g)]
        return tot[:, 0:1, :], tot[:, 1:2, :]

    def ag_send(idx, g, buf, slot):
        view = buf.at[slot, group(g)]
        for i in range(1, NP):
            remote(view, view, s.ag_s.at[idx, g], s.ag_r.at[idx, g], pipe_peer(i), me_d).start()
        note("ag", idx, lambda g: s.h1.at[0, pl.ds(0, NP - 1), group(g)], s.ag_s, s.ag_r)

    def ag_take(idx, g, buf):
        grab("ag", idx, g)
        return jnp.concatenate([buf[j, group(g)].reshape(flat, LANES) for j in range(NP)], axis=1)

    def rs_send(idx, g, k, partial):
        for j in range(NP):
            s.put[idx, j, group(g)] = partial[:, j * LANES : (j + 1) * LANES].reshape(GM, R, LANES).astype(BF16)
        for i in range(1, NP):
            p = pipe_peer(i)
            remote(
                s.put.at[idx, shard(k, p), group(g)],
                s.got.at[idx, me_p, group(g)],
                s.rs_s.at[idx, g],
                s.rs_r.at[idx, g],
                p,
                me_d,
            ).start()
        note("rs", idx, lambda g: s.got.at[idx, pl.ds(0, NP - 1), group(g)], s.rs_s, s.rs_r)

    def rs_take(idx, g, k):
        grab("rs", idx, g)
        tot = s.put[idx, shard(k, me_p), group(g)].astype(F32)
        for i in range(1, NP):
            tot = tot + s.got[idx, pipe_peer(i), group(g)].astype(F32)
        return tot

    def shard_cols(base, k):
        return pl.ds(pl.multiple_of(base + shard(k, me_p) * LANES, LANES), LANES)

    def norm_cols(which, k):
        if which == 1:
            return shard_cols(0, k)
        if which == 2:
            return shard_cols(c.mid, k)
        return pl.ds(pl.multiple_of(2 * c.mid + me_p * c.cs, LANES), c.cs)

    def real_rows(width):
        return lax.broadcasted_iota(jnp.int32, (GM, R, width), 1) < c.rows

    ZD = {1: (s.z1, s.d1, s.gr1), 2: (s.z2, s.d2, s.gr2), 3: (s.z3, s.d3, s.gr3)}
    FWD = {(0, 1): 0, (0, 2): 1, (1, 1): 2, (1, 2): 3, (0, 3): 8, (1, 3): 9}
    BWD = {(1, 2): 4, (1, 1): 5, (0, 2): 6, (0, 1): 7, (1, 3): 10, (0, 3): 11}

    def stats_out(k, which, g, a):
        ZD[which][0][k, group(g)] = a
        ar_send(FWD[(k, which)], g, jnp.sum(a, axis=1, keepdims=True), jnp.sum(a * a, axis=1, keepdims=True))

    def normed(k, which, g):
        z_ref, _, gr_ref = ZD[which]
        one, two = ar_take(FWD[(k, which)], g)
        mean = one / count
        inv = lax.rsqrt(two / count - mean * mean + EPS)
        z = (z_ref[k, group(g)] - mean) * inv
        z_ref[k, group(g)] = z
        gain = gain_ref[k : k + 1, norm_cols(which, k)][None]
        gr_ref[k, group(g)] = gain * inv
        return z * gain + shift_ref[k : k + 1, norm_cols(which, k)][None]

    def hidden_out(k, which, g, idx, buf):
        act, slope = gelu_pair(normed(k, which, g))
        ZD[which][1][k, group(g)] = slope
        mine = shard(k, me_p)
        buf[k, mine, group(g)] = jnp.where(real_rows(LANES), act, 0.0).astype(BF16)
        ag_send(idx, g, buf.at[k], mine)

    def back_out(k, which, g, up):
        ar_send(
            BWD[(k, which)],
            g,
            jnp.sum(up, axis=1, keepdims=True),
            jnp.sum(up * ZD[which][0][k, group(g)], axis=1, keepdims=True),
        )

    def back_in(k, which, g, up):
        z_ref, _, gr_ref = ZD[which]
        one, two = ar_take(BWD[(k, which)], g)
        chunk0 = {1: 0, 2: 1, 3: 2}[which]
        for n in range(one.shape[-1] // LANES):
            lanes = slice(n * LANES, (n + 1) * LANES)
            s.norm_sum[me_p, chunk0 + n, 2 * k : 2 * k + 1, :] += jnp.sum(two[:, :, lanes], axis=0)
            s.norm_sum[me_p, chunk0 + n, 2 * k + 1 : 2 * k + 2, :] += jnp.sum(one[:, :, lanes], axis=0)
        grad = gr_ref[k, group(g)] * (up - one / count - z_ref[k, group(g)] * (two / count))
        return jnp.where(real_rows(grad.shape[-1]), grad, 0.0).astype(BF16)

    def shifted(v, by):
        by = by % flat
        return v if by == 0 else pltpu.roll(v, by, 0)

    def tap_shift(t):
        return SIDE * (t // 3 - 1) + (t % 3 - 1)

    def masked(v, t):
        return v.reshape(GM, R, LANES) * s.mask[t][None]

    def conv(k, h):
        acc = None
        for t0 in range(0, TAPS, 2):
            taps = [t for t in (t0, t0 + 1) if t < TAPS]
            w = s.wf[k, taps[0]] if len(taps) == 1 else jnp.concatenate([s.wf[k, t] for t in taps], axis=1)
            y = dot(h, w)
            for n, t in enumerate(taps):
                part = masked(shifted(y[:, n * LANES : (n + 1) * LANES], -tap_shift(t)), t)
                acc = part if acc is None else acc + part
        return acc

    def conv_back(k, g, d):
        flat_d = d.astype(F32)
        for t in range(TAPS):
            part = shifted((flat_d * s.mask[t][None]).reshape(flat, LANES), tap_shift(t))
            s.dcol[k, group(g), :, t * LANES : (t + 1) * LANES] = part.astype(BF16).reshape(GM, R, LANES)
        w = jnp.concatenate([s.wf[k, t] for t in range(TAPS)], axis=1)
        return dot_nt(s.dcol[k, group(g)].reshape(flat, TAPS * LANES), w)

    tail, ends = [], []

    def work():
        load_all.wait()

        @pl.when(me_p == 0)
        def _():
            load_p.wait()

            @pl.loop(0, G)
            def _(g):
                a = dot(s.u_all[group(g)].reshape(flat, c.ch), s.p_own[...])
                for j in range(NP):
                    s.put[0, j, group(g)] = a[:, j * LANES : (j + 1) * LANES].reshape(GM, R, LANES).astype(BF16)
                s.first[group(g)] = s.put[0, 0, group(g)]
                for p in range(1, NP):
                    remote(
                        s.put.at[0, shard(0, jnp.int32(p)), group(g)], s.first.at[group(g)], s.rs_s.at[0, g], s.rs_r.at[0, g], p, me_d
                    ).start()

        @on_pipes(0)
        def _():
            front_send().start()


        for k in range(2):

            @pl.loop(0, G)
            def _(g):
                if k == 0:

                    @pl.when(me_p != 0)
                    def _():
                        take_recv(s.first.at[group(g)], s.rs_s.at[0, g], s.rs_r.at[0, g])

                    a = s.first[group(g)].astype(F32)
                else:
                    a = rs_take(1, g, 1)
                stats_out(k, 1, g, a)
            pass_one(4 if k == 0 else 3)

            @pl.loop(0, G)
            def _(g):
                hidden_out(k, 1, g, 2 * k, s.h1)
            if k == 0:

                @on_pipes(2, 3)
                def _():
                    front_send().start()

                @on_pipes(1)
                def _():
                    for i in range(1, NP):
                        proj_send(i).start()

            else:
                pass_two(3)


            if k == 0:
                pass_two(4)
            need(4 + k)

            @pl.loop(0, G)
            def _(g):
                stats_out(k, 2, g, conv(k, ag_take(2 * k, g, s.h1.at[k])))
            if k == 0:
                pass_one(1, 2)

            @pl.loop(0, G)
            def _(g):
                hidden_out(k, 2, g, 2 * k + 1, s.h2)
            if k == 0:
                pass_two(1, 2)

                @on_pipes(3)
                def _():
                    for i in range(1, NP):
                        proj_send(i).start()


            need(2 * k + 1)
            if k == 0:
                load_u.wait()

            @pl.loop(0, G)
            def _(g):
                a = dot_nt(ag_take(2 * k + 1, g, s.h2.at[k]), s.pq[2 * k + 1])
                stats_out(k, 3, g, a.reshape(GM, R, c.cs))
            if k == 0:
                pass_one(5)

            if k == 0:
                need(2)

                @pl.loop(0, G)
                def _(g):
                    v = normed(0, 3, g) + s.u_seg[0, group(g)].astype(F32)
                    act, slope = gelu_pair(v)
                    s.d3[0, group(g)] = slope
                    o = jnp.where(real_rows(c.cs), act, 0.0).astype(BF16)
                    s.u_seg[1, group(g)] = o
                    rs_send(1, g, 1, dot(o.reshape(flat, c.cs), s.pq[2]))
                pass_two(5)

        load_g.wait()

        @pl.loop(0, G)
        def _(g):
            v = normed(1, 3, g) + s.u_seg[1, group(g)].astype(F32)
            act, slope = gelu_pair(v)
            o = jnp.where(real_rows(c.cs), act, 0.0).astype(BF16)
            s.out_seg[group(g)] = o
            e = s.g_seg[group(g)].astype(F32) * slope
            s.e3[group(g)] = e
            back_out(1, 3, g, e)
            o32 = o.astype(F32)
            place = lax.broadcasted_iota(jnp.int32, (GM, R, c.cs), 1)
            for n in range(c.images):
                here = (place >= n * SIDE * SIDE) & (place < (n + 1) * SIDE * SIDE)
                mean = jnp.sum(jnp.where(here, o32, 0.0), axis=1, keepdims=True) / float(SIDE * SIDE)
                for m in range(GM):
                    s.pool[(g * GM + m) * c.images + n] = mean[m]

        out_copy = pltpu.make_async_copy(s.out_seg, bo_out, s.out_r.at[0])
        out_copy.start()
        tail.append(out_copy.wait)

        banks = ND * c.bank
        which = lax.broadcasted_iota(jnp.int32, (banks, c.cs), 0)
        term = jnp.zeros((banks, c.cs), F32)
        for n in range(M * c.images):
            ids = jnp.concatenate([ids_ref[n : n + 1, :]] * (c.cs // LANES), axis=1)
            term = term + jnp.where(which == ids, s.pool[n], 0.0)
        s.bank_put[...] = term.reshape(ND, c.bank, c.cs)

        @pl.loop(1, ND)
        def _(i):
            d = dp_peer(i)
            remote(s.bank_put.at[d], s.bank_got.at[me_d], s.bank_s.at[0], s.bank_r.at[0], me_p, d).start()

        tail.append(lambda: take_send(s.bank_got.at[pl.ds(0, ND - 1)], s.bank_s.at[0], s.bank_r.at[0]))

        s.bank_got[me_d] = s.bank_put[me_d]

        def all_rows(ref):
            return ref[...].reshape(M * R, ref.shape[-1])

        def all_seg(ref):
            return jnp.concatenate([ref[j].reshape(M * R, LANES) for j in range(NP)], axis=1)

        def grad_q(k):
            h = all_seg(s.h2.at[k])
            s.gp[2 * k + 1] = dot_tn(all_rows(s.da3.at[k]), h).astype(BF16)

        def grad_p0():
            d = s.da1[0, shard(0, me_p)].reshape(M * R, LANES)
            s.g0[...] = dot_tn(all_rows(s.u_all), d).astype(BF16)

        def grad_p(k):
            d = all_seg(s.da1.at[k])
            s.gp[2 * k] = dot_tn(all_rows(s.u_seg.at[k]), d).astype(BF16)

        def grad_w(k):
            h = all_seg(s.h1.at[k])
            for t0 in range(0, TAPS, 2):
                taps = [t for t in (t0, t0 + 1) if t < TAPS]
                d = s.dcol[k, :, :, t0 * LANES : (t0 + len(taps)) * LANES].reshape(M * R, len(taps) * LANES)
                v = dot_tn(h, d)
                for n, t in enumerate(taps):
                    s.gw[k, t * c.mid : (t + 1) * c.mid, :] = v[:, n * LANES : (n + 1) * LANES].astype(BF16)

        def part(base, n):
            return pl.ds(pl.multiple_of(base, 16), n)

        inner = (me_z == 1) | (me_z == 2)
        z_side = lax.div(me_z, 2)
        outer_dev = 2 * (3 * z_side) + me_c
        inner_dev = 2 * (1 + z_side) + me_c
        across_dev = 2 * (2 - z_side) + me_c
        high_dev = 2 * lax.rem(me_z + 2, 4) + me_c

        def halving(job):
            return c.jobs[job][1] == 0

        def job_own(job):
            kind, k, n, base, slot = c.jobs[job]
            ref = s.g0 if kind == "0" else s.gw.at[k] if kind == "w" else s.gp.at[2 * k + (kind == "q")]
            return ref, base

        def job_ref(name, job):
            kind, k, n, base, slot = c.jobs[job]
            return getattr(s, name + ("p" if kind in "pq" else kind)).at[slot]

        def job_core(job):
            own, base = job_own(job)
            n = c.jobs[job][2]
            view = own.at[part(base + (1 - me_c) * n, n)]
            remote(view, job_ref("ja", job), s.gs.at[job, 0], s.gr.at[job, 0], me_p, sib).start()

        def job_in(job):
            own, base = job_own(job)
            n = c.jobs[job][2]
            got, tot = job_ref("ja", job), job_ref("jb", job)
            take_recv(got, s.gs.at[job, 0], s.gr.at[job, 0])
            tot[...] = (got[...].astype(F32) + own[part(base + me_c * n, n), :].astype(F32)).astype(BF16)
            if halving(job):
                view = tot.at[part((1 - me_l) * (n // 2), n // 2)]
                remote(view, job_ref("jc", job).at[0 : n // 2], s.gs.at[job, 1], s.gr.at[job, 1], me_p, low).start()
                return

            @pl.when(jnp.logical_not(inner))
            def _():
                remote(tot, job_ref("jc", job), s.gs.at[job, 1], s.gr.at[job, 1], me_p, inner_dev).start()

        def job_halve(job):
            n = c.jobs[job][2]
            got, tot, half = job_ref("jc", job), job_ref("jb", job), job_ref("jd", job)
            if halving(job):
                got, half = got.at[0 : n // 2], half.at[0 : n // 4]
                take_recv(got, s.gs.at[job, 1], s.gr.at[job, 1])
                mine = part(me_l * (n // 2), n // 2)
                tot[mine, :] = (got[...].astype(F32) + tot[mine, :].astype(F32)).astype(BF16)
                view = tot.at[part(me_l * (n // 2) + (1 - z_side) * (n // 4), n // 4)]
                remote(view, half, s.gs.at[job, 2], s.gr.at[job, 2], me_p, high_dev).start()
                return

            @pl.when(inner)
            def _():
                take_recv(got, s.gs.at[job, 1], s.gr.at[job, 1])
                tot[...] = (got[...].astype(F32) + tot[...].astype(F32)).astype(BF16)
                view = tot.at[part((1 - z_side) * (n // 2), n // 2)]
                remote(view, half, s.gs.at[job, 2], s.gr.at[job, 2], me_p, across_dev).start()

        def job_sum(job):
            n = c.jobs[job][2]
            tot, half, fin = job_ref("jb", job), job_ref("jd", job), job_ref("je", job)
            if halving(job):
                half = half.at[0 : n // 4]
                take_recv(half, s.gs.at[job, 2], s.gr.at[job, 2])
                mine = part(me_l * (n // 2) + z_side * (n // 4), n // 4)
                fin[mine, :] = (half[...].astype(F32) + tot[mine, :].astype(F32)).astype(BF16)
                remote(fin.at[mine], fin.at[mine], s.gs.at[job, 3], s.gr.at[job, 3], me_p, high_dev).start()
                return
            mine = part(z_side * (n // 2), n // 2)

            @pl.when(inner)
            def _():
                take_recv(half, s.gs.at[job, 2], s.gr.at[job, 2])
                fin[mine, :] = (half[...].astype(F32) + tot[mine, :].astype(F32)).astype(BF16)
                view = fin.at[mine]
                remote(view, view, s.gs.at[job, 3], s.gr.at[job, 3], me_p, across_dev).start()
                remote(view, view, s.gs.at[job, 4], s.gr.at[job, 3], me_p, outer_dev).start()

        def job_out(job):
            n = c.jobs[job][2]
            fin = job_ref("je", job)
            if halving(job):
                take_recv(fin.at[0 : n // 4], s.gs.at[job, 3], s.gr.at[job, 3])
                view = fin.at[part(me_l * (n // 2), n // 2)]
                remote(view, view, s.gs.at[job, 4], s.gr.at[job, 4], me_p, low).start()
                return
            view = fin.at[part((1 - z_side) * (n // 2), n // 2)]

            @pl.when(inner)
            def _():
                take_recv(view, s.gs.at[job, 3], s.gr.at[job, 3])
                remote(view, view, s.gs.at[job, 5], s.gr.at[job, 4], me_p, outer_dev).start()

        def job_place(job, p, core):
            kind, k, n, base, slot = c.jobs[job]
            if kind == "0":
                return s.p0_out.at[shard(0, p), part(base + core * n, n)]
            if kind == "w":
                return s.w_out.at[lax.div(p, 2) if k == 0 else 1 - lax.div(p, 2), part(base + core * n, n)]
            return s.p_out.at[part(p * 2 * n + core * n, n)]

        def job_home(job, p):
            kind, k = c.jobs[job][:2]
            return 2 * k + lax.rem(p, 2) if kind == "w" else jnp.int32(2 * k + (kind == "q"))

        def job_holds(job):
            kind, k = c.jobs[job][:2]
            return me_y == k if kind == "w" else me_p == 2 * k + (kind == "q")

        def job_plane(job):
            n = c.jobs[job][2]
            fin = job_ref("je", job)

            if halving(job):
                take_recv(fin.at[0 : n // 2], s.gs.at[job, 4], s.gr.at[job, 4])
            else:

                @pl.when(jnp.logical_not(inner))
                def _():
                    for step in (3, 4):
                        take_recv(fin.at[0 : n // 2], s.gs.at[job, step], s.gr.at[job, step])

            home = job_home(job, me_p)

            @pl.when(me_p != home)
            def _():
                remote(fin, job_place(job, me_p, me_c), s.gs.at[job, 6], s.gr.at[job, 5], home, me_d).start()

            @pl.when(me_p == home)
            def _():
                pltpu.make_async_copy(fin, job_place(job, me_p, me_c), s.own_s.at[job]).start()

        def job_many(job, count):
            kind, k, n, base, slot = c.jobs[job]
            if kind == "0":
                return s.p0_out.at[pl.ds(0, count), pl.ds(0, n)]
            return s.w_out.at[pl.ds(0, count), pl.ds(0, n)] if kind == "w" else s.p_out.at[pl.ds(0, n * count)]

        def job_share(job):
            fin = job_ref("je", job)
            from_pipes = [0, 2] if c.jobs[job][0] == "w" else [0, 1, 2, 3]

            @pl.when(job_holds(job))
            def _():
                pltpu.make_async_copy(fin, job_place(job, me_p, me_c), s.own_s.at[job]).wait()
                take_recv(job_many(job, len(from_pipes) - 1), s.gs.at[job, 6], s.gr.at[job, 5])
                for i in from_pipes:
                    view = job_place(job, pipe_peer(i), me_c)
                    remote(view, view, s.fin_s.at[job], s.fin_r.at[job], me_p, sib).start()

        def job_end(job):
            got, half, fin = job_ref("ja", job), job_ref("jd", job), job_ref("je", job)
            n = c.jobs[job][2]
            take_send(got, s.gs.at[job, 0], s.gr.at[job, 0])
            if halving(job):
                for step, rows in ((1, n // 2), (2, n // 4), (3, n // 4), (4, n // 2)):
                    take_send(fin.at[0:rows], s.gs.at[job, step], s.gr.at[job, step])
            else:

                @pl.when(inner)
                def _():
                    for step in (2, 3, 4, 5):
                        take_send(half, s.gs.at[job, step], s.gr.at[job, 2])

                @pl.when(jnp.logical_not(inner))
                def _():
                    take_send(got, s.gs.at[job, 1], s.gr.at[job, 1])

            @pl.when(me_p != job_home(job, me_p))
            def _():
                take_send(fin, s.gs.at[job, 6], s.gr.at[job, 5])

            @pl.when(job_holds(job))
            def _():
                view = job_many(job, 2 if c.jobs[job][0] == "w" else NP)
                take_recv(view, s.fin_s.at[job], s.fin_r.at[job])
                take_send(view, s.fin_s.at[job], s.fin_r.at[job])

        steps = (job_core, job_in, job_halve, job_sum, job_out, job_plane, job_share)
        next_step = dict.fromkeys(c.jobs, 0)

        def advance(*jobs):
            if c.deep:
                for job in jobs:
                    if next_step[job] < len(steps):
                        steps[next_step[job]](job)
                        next_step[job] += 1

        def point(k, n):
            advance(*POINTS[(1 - k) * 6 + n])

        for k in (1, 0):
            side = 2 * (1 - k)

            @pl.loop(0, G)
            def _(g):
                grad = back_in(k, 3, g, s.e3[group(g)])
                s.da3[k, group(g)] = grad
                rs_send(2 + (1 - k), g, k, dot(grad.reshape(flat, c.cs), s.pq[2 * k + 1]))

            grad_q(k)
            if k == 1:

                @on_pipes(0)
                def _():
                    for i in range(1, NP):
                        proj_send(i).start()

            point(k, 0)

            @pl.loop(0, G)
            def _(g):
                up = rs_take(2 + (1 - k), g, k) * s.d2[k, group(g)]
                s.t1[group(g)] = up
                back_out(k, 2, g, up)
            if k == 0:
                pass_two(0)
            point(k, 1)

            @pl.loop(0, G)
            def _(g):
                rs_send(5 - k, g, k, conv_back(k, g, back_in(k, 2, g, s.t1[group(g)])))

            grad_w(k)
            point(k, 2)

            @pl.loop(0, G)
            def _(g):
                up = rs_take(5 - k, g, k) * s.d1[k, group(g)]
                s.t1[group(g)] = up
                back_out(k, 1, g, up)
            point(k, 3)

            @pl.loop(0, G)
            def _(g):
                mine = shard(k, me_p)
                s.da1[k, mine, group(g)] = back_in(k, 1, g, s.t1[group(g)])
                ag_send(5 + side, g, s.da1.at[k], mine)
            if k == 0:
                grad_p0()
            point(k, 4)

            if k == 0:
                need(0)
            @pl.loop(0, G)
            def _(g):
                d = dot_nt(ag_take(5 + side, g, s.da1.at[k]), s.pq[2 * k])
                d = d.reshape(GM, R, c.cs) + s.e3[group(g)]
                if k == 1:
                    e = d * s.d3[0, group(g)]
                    s.e3[group(g)] = e
                    back_out(0, 3, g, e)
                else:
                    s.in_seg[group(g)] = d.astype(BF16)

            if k == 1 or not c.deep:
                grad_p(k)
            if k == 1:
                pass_one(0)
            point(k, 5)

        in_copy = pltpu.make_async_copy(s.in_seg, ig_out, s.out_r.at[1])
        in_copy.start()
        tail.append(in_copy.wait)
        view = s.norm_sum.at[me_p]
        for i in range(1, NP):
            remote(view, view, s.ns_s.at[0], s.ns_r.at[0], pipe_peer(i), me_d).start()
        tail.append(lambda: take_send(s.norm_sum.at[pl.ds(0, NP - 1)], s.ns_s.at[0], s.ns_r.at[0]))

        if c.deep:
            for stop in (len(steps) - 1, len(steps)):
                while min(next_step.values()) < stop:
                    advance(*[job for job in LAST if next_step[job] < stop])
            ends.extend(functools.partial(job_end, job) for job in c.jobs)

        take_recv(s.bank_got.at[pl.ds(0, ND - 1)], s.bank_s.at[0], s.bank_r.at[0])
        tot = s.bank_got[0]
        for d in range(1, ND):
            tot = tot + s.bank_got[d]
        mb_out[...] = tot
        take_recv(s.norm_sum.at[pl.ds(0, NP - 1)], s.ns_s.at[0], s.ns_r.at[0])
        per = c.mid // LANES
        wide = c.cs // LANES
        each = (2 * per + c.ch // LANES) // NP
        for k in range(2):
            for n in range(each):
                q = me_p * each + n
                in_one = q < per
                in_two = (q >= per) & (q < 2 * per)
                sh = jnp.where(in_one, q, q - per)
                half = lax.rem(sh + k, 2)
                small = 2 * half + lax.div(sh, 2)
                far = q - 2 * per
                p = jnp.where(q < 2 * per, small, lax.div(far, wide))
                chunk = jnp.where(in_one, 0, jnp.where(in_two, 1, 2 + lax.rem(far, wide)))
                ns_out[n, 2 * k : 2 * k + 2, :] = s.norm_sum[p, chunk, 2 * k : 2 * k + 2, :]

    work()

    for wait in ends:
        wait()
    if c.deep:
        copies = [
            pltpu.make_async_copy(s.w_out.at[h], gw_out.at[:, pl.ds(h * LANES, LANES)], s.out_r.at[2 + h]) for h in range(2)
        ]
        wide = [
            pltpu.make_async_copy(s.p0_out.at[j], gp_out.at[:, pl.ds(j * LANES, LANES)], s.out_r.at[4 + j])
            for j in range(NP)
        ]
        tall = pltpu.make_async_copy(s.p_out, gp_out, s.out_r.at[4])
        for copy in copies:
            copy.start()
        for act in ("start", "wait"):

            @pl.when(me_p == 0)
            def _():
                for copy in wide:
                    getattr(copy, act)()

            @pl.when(me_p != 0)
            def _():
                getattr(tall, act)()

    else:
        copies = [
            pltpu.make_async_copy(s.gp, gp_out, s.out_r.at[2]),
            pltpu.make_async_copy(s.gw, gw_out, s.out_r.at[3]),
        ]
        for copy in copies:
            copy.start()
    front_send().wait_send()
    for i in range(1, NP):
        proj_send(i).wait_send()
    for n in range(6):
        end_part(n)

    @pl.loop(0, G)
    def _(g):
        for wait in [*due.values(), *owed.values()]:
            wait(g)

        @pl.when(me_p == 0)
        def _():
            take_send(s.put.at[0, pl.ds(0, NP - 1), group(g)], s.rs_s.at[0, g], s.rs_r.at[0, g])

    for wait in tail:
        wait()
    for copy in copies:
        copy.wait()


def on_device(mesh, block_input, proj_weight, spatial_weight, norm_gain, norm_shift, output_grad, image_ids):
    bank = 8
    c = Sizes(mesh, block_input, proj_weight, spatial_weight, bank)
    extra = ((0, 0), (0, c.pad - c.rows), (0, 0))
    u = jnp.pad(block_input, extra)
    go = jnp.pad(output_grad, extra)
    sw = spatial_weight.reshape(TAPS, c.mid, spatial_weight.shape[2])
    ids = jnp.broadcast_to(image_ids.reshape(-1, 1), (image_ids.size, LANES))
    items = scratch_list(c)
    names = [n for n, _ in items]
    anyspec = pl.BlockSpec(memory_space=pl.ANY)
    vspec = pl.BlockSpec(memory_space=pltpu.VMEM)
    if c.deep:
        gp_shape, gw_shape = (c.ch, c.mid), (TAPS * c.mid, 2 * LANES)
    else:
        gp_shape, gw_shape = (c.pipes, c.cs, c.mid), (2, TAPS * c.mid, LANES)
    each = (2 * c.mid + c.ch) // LANES // c.pipes
    outs = pl.pallas_call(
        functools.partial(body, c, names),
        out_shape=(
            jax.ShapeDtypeStruct((c.micro, c.pad, c.cs), BF16),
            jax.ShapeDtypeStruct((c.micro, c.pad, c.cs), BF16),
            jax.ShapeDtypeStruct(gp_shape, BF16),
            jax.ShapeDtypeStruct(gw_shape, BF16),
            jax.ShapeDtypeStruct((each, 4, LANES), F32),
            jax.ShapeDtypeStruct((bank, c.cs), F32),
        ),
        in_specs=[anyspec] * 4 + [vspec] * 3,
        out_specs=(anyspec, anyspec, anyspec, anyspec, vspec, vspec),
        scratch_shapes=[v for _, v in items],
        compiler_params=pltpu.CompilerParams(collective_id=0, has_side_effects=True, vmem_limit_bytes=60 << 20),
    )(u, go, proj_weight[0], sw, norm_gain, norm_shift, ids)
    bo, ig, gp, gw, ns, mb = outs
    if not c.deep:
        gp = lax.psum(gp.astype(F32), "dp")
        gw = lax.psum(gw.astype(F32), "dp")
        gp = lax.all_to_all(gp, "pipe", 0, 0, tiled=True).reshape(c.ch, c.mid)
        gw = lax.all_gather(gw, "pipe")
        me = lax.axis_index("pipe")
        y, x = me // 2, me % 2
        near = lax.dynamic_index_in_dim(gw, me, 0, keepdims=False)
        far = lax.dynamic_index_in_dim(gw, 2 * (1 - y) + x, 0, keepdims=False)
        gw = jnp.concatenate(
            [lax.dynamic_index_in_dim(near, y, 0, keepdims=False), lax.dynamic_index_in_dim(far, y, 0, keepdims=False)],
            axis=1,
        )
    ns = jnp.transpose(ns.reshape(each, 2, 2, LANES), (2, 1, 0, 3)).reshape(2, 2, each * LANES)
    return (
        bo[:, : c.rows],
        ig[:, : c.rows],
        gp.astype(F32)[None],
        gw.astype(F32)[None],
        ns[0],
        ns[1],
        mb,
    )


def solution(mesh):
    return jax.shard_map(
        functools.partial(on_device, mesh),
        mesh=mesh,
        in_specs=(
            P(None, "dp", None),
            P("pipe", None, None),
            P("pipe", None, None),
            P(),
            P(),
            P(None, "dp", None),
            P(None, "dp"),
        ),
        out_specs=(
            P(None, "dp", "pipe"),
            P(None, "dp", "pipe"),
            P("pipe", None, None),
            P("pipe", None, None),
            P(None, "pipe"),
            P(None, "pipe"),
            P("dp", "pipe"),
        ),
        check_vma=False,
    )
```

```python
import functools
import math
import types

import jax
import jax.numpy as jnp
from jax import lax
from jax.experimental import pallas as pl
from jax.experimental.pallas import tpu as pltpu
from jax.sharding import PartitionSpec as P

SIDE = 7
TAPS = 9
EPS = 1e-05
LANES = 128
GROUPS = 4
W_PIECES = 3
P_PIECES = 2
POINTS = (
    (0,),
    (0,),
    (0, 1, 2, 3),
    (0, 1, 2),
    (0, 1),
    (1, 2, 3, 4),
    (0, 1, 2, 3, 4, 5),
    (2, 3, 4, 5),
    (6, 7, 8, 1, 2, 3, 4, 5),
    (6, 7, 8, 5, 4),
    (9, 10, 6, 5),
    (9, 10, 6, 7, 8, 5, 3, 4),
)
LAST = (6, 7, 8, 9, 10, 5, 4, 3, 0, 1, 2)
MESH = pl.DeviceIdType.MESH
F32 = jnp.float32
BF16 = jnp.bfloat16


def gelu_pair(v):
    c0 = math.sqrt(2.0 / math.pi)
    c1 = 0.044715
    sq = v * v
    t = jnp.tanh(c0 * v * (1.0 + c1 * sq))
    half = 0.5 + 0.5 * t
    slope = half + (0.5 * c0) * v * (1.0 - t * t) * (1.0 + (3.0 * c1) * sq)
    return v * half, slope


def dot(a, b):
    return jnp.dot(a, b, preferred_element_type=F32)


def dot_nt(a, b):
    return lax.dot_general(a, b, (((1,), (1,)), ((), ())), preferred_element_type=F32)


def dot_tn(a, b):
    return lax.dot_general(a, b, (((0,), (0,)), ((), ())), preferred_element_type=F32)


class Sizes:
    def __init__(self, mesh, block_input, proj, spatial, bank_rows):
        self.pipes = mesh.shape["pipe"]
        self.dps = mesh.shape["dp"]
        self.micro = block_input.shape[0]
        self.rows = block_input.shape[1]
        self.pad = -(-self.rows // 16) * 16
        self.ch = block_input.shape[2]
        self.mid = proj.shape[2]
        self.images = self.rows // (SIDE * SIDE)
        self.cs = self.ch // self.pipes
        self.msd = self.mid // self.pipes
        self.groups = GROUPS
        self.gm = self.micro // self.groups
        self.zs = self.dps // 2
        self.total = self.rows * self.dps
        self.bank = bank_rows
        self.deep = self.zs == 4
        self.jobs = {}
        taps = TAPS // W_PIECES
        for k in (1, 0):
            self.jobs[len(self.jobs)] = ("q", k, self.cs // 2, 0, 1 - k)
            for i in range(W_PIECES):
                self.jobs[len(self.jobs)] = ("w", k, taps * self.mid // 2, i * taps * self.mid, (1 - k) * W_PIECES + i)
            if k == 1:
                self.jobs[len(self.jobs)] = ("p", k, self.cs // 2, 0, 2)
        for i in range(P_PIECES):
            self.jobs[len(self.jobs)] = ("0", 0, self.ch // P_PIECES // 2, i * self.ch // P_PIECES, i)


def scratch_list(c):
    full = (c.micro, c.pad)
    seg = (c.pipes, c.micro, c.pad, LANES)
    items = [
        ("u_all", pltpu.VMEM(full + (c.ch,), BF16)),
        ("u_seg", pltpu.VMEM((2,) + full + (c.cs,), BF16)),
        ("g_seg", pltpu.VMEM(full + (c.cs,), BF16)),
        ("p_own", pltpu.VMEM((c.ch, c.mid), BF16)),
        ("pq", pltpu.VMEM((c.pipes, c.cs, c.mid), BF16)),
        ("wf", pltpu.VMEM((2, TAPS, c.mid, LANES), BF16)),
        ("sw", pltpu.VMEM((2, TAPS, c.mid, LANES), BF16)),
        ("mask", pltpu.VMEM((TAPS, c.pad, LANES), F32)),
        ("z1", pltpu.VMEM((2,) + full + (LANES,), F32)),
        ("d1", pltpu.VMEM((2,) + full + (LANES,), F32)),
        ("z2", pltpu.VMEM((2,) + full + (LANES,), F32)),
        ("d2", pltpu.VMEM((2,) + full + (LANES,), F32)),
        ("z3", pltpu.VMEM((2,) + full + (c.cs,), F32)),
        ("d3", pltpu.VMEM((2,) + full + (c.cs,), F32)),
        ("e3", pltpu.VMEM(full + (c.cs,), F32)),
        ("t1", pltpu.VMEM(full + (LANES,), F32)),
        ("gr1", pltpu.VMEM((2, c.micro, 1, LANES), F32)),
        ("gr2", pltpu.VMEM((2, c.micro, 1, LANES), F32)),
        ("gr3", pltpu.VMEM((2, c.micro, 1, c.cs), F32)),
        ("h1", pltpu.VMEM((2,) + seg, BF16)),
        ("h2", pltpu.VMEM((2,) + seg, BF16)),
        ("da3", pltpu.VMEM((2,) + full + (c.cs,), BF16)),
        ("dcol", pltpu.VMEM((2,) + full + (TAPS * LANES,), BF16)),
        ("da1", pltpu.VMEM((2,) + seg, BF16)),
        ("first", pltpu.VMEM(full + (LANES,), BF16)),
        ("put", pltpu.VMEM((6,) + seg, BF16)),
        ("got", pltpu.VMEM((6,) + seg, BF16)),
        ("out_seg", pltpu.VMEM(full + (c.cs,), BF16)),
        ("in_seg", pltpu.VMEM(full + (c.cs,), BF16)),
        ("ar_small", pltpu.VMEM((8, c.dps, c.micro, 2, LANES), F32)),
        ("ar_wide", pltpu.VMEM((4, c.dps, c.micro, 2, c.cs), F32)),
        ("pool", pltpu.VMEM((c.micro * c.images, 1, c.cs), F32)),
        ("bank_put", pltpu.VMEM((c.dps, c.bank, c.cs), F32)),
        ("bank_got", pltpu.VMEM((c.dps, c.bank, c.cs), F32)),
        ("norm_sum", pltpu.VMEM((c.pipes, 6, 8, LANES), F32)),
        ("gp", pltpu.VMEM((c.pipes, c.cs, c.mid), BF16)),
        ("g0", pltpu.VMEM((c.ch, LANES), BF16)),
        ("gw", pltpu.VMEM((2, TAPS * c.mid, LANES), BF16)),
        ("ar_s", pltpu.SemaphoreType.DMA((12, c.groups))),
        ("ar_r", pltpu.SemaphoreType.DMA((12, c.groups))),
        ("ag_s", pltpu.SemaphoreType.DMA((8, c.groups))),
        ("ag_r", pltpu.SemaphoreType.DMA((8, c.groups))),
        ("rs_s", pltpu.SemaphoreType.DMA((6, c.groups))),
        ("rs_r", pltpu.SemaphoreType.DMA((6, c.groups))),
        ("w_s", pltpu.SemaphoreType.DMA((2, c.pipes))),
        ("pass_s", pltpu.SemaphoreType.DMA((6, 3))),
        ("w_r", pltpu.SemaphoreType.DMA((6,))),
        ("w_z", pltpu.SemaphoreType.DMA((6,))),
        ("w_q", pltpu.SemaphoreType.DMA((6,))),
        ("bank_s", pltpu.SemaphoreType.DMA((1,))),
        ("bank_r", pltpu.SemaphoreType.DMA((1,))),
        ("ns_s", pltpu.SemaphoreType.DMA((1,))),
        ("ns_r", pltpu.SemaphoreType.DMA((1,))),
        ("in_r", pltpu.SemaphoreType.DMA((6,))),
        ("out_r", pltpu.SemaphoreType.DMA((4 + c.pipes,))),
    ]
    if c.deep:
        for name, width in (("p", c.mid), ("w", LANES), ("0", LANES)):
            of = [job for job in c.jobs.values() if job[0] in {"p": "pq"}.get(name, name)]
            lead, n = len(of), of[0][2]
            items += [(key + name, pltpu.VMEM((lead, n // (1 + (key == "jd")), width), BF16)) for key in ("ja", "jb", "jc", "jd", "je")]
        count = len(c.jobs)
        items += [
            ("p_out", pltpu.VMEM((c.ch, c.mid), BF16)),
            ("p0_out", pltpu.VMEM((c.pipes, c.ch, LANES), BF16)),
            ("w_out", pltpu.VMEM((2, TAPS * c.mid, LANES), BF16)),
            ("gs", pltpu.SemaphoreType.DMA((count, 7))),
            ("gr", pltpu.SemaphoreType.DMA((count, 6))),
            ("own_s", pltpu.SemaphoreType.DMA((count,))),
            ("fin_s", pltpu.SemaphoreType.DMA((count,))),
            ("fin_r", pltpu.SemaphoreType.DMA((count,))),
        ]
    return items


def body(c, names, *refs):
    (u_hbm, go_hbm, pw_hbm, sw_hbm, gain_ref, shift_ref, ids_ref) = refs[:7]
    (bo_out, ig_out, gp_out, gw_out, ns_out, mb_out) = refs[7:13]
    s = types.SimpleNamespace(**dict(zip(names, refs[13:])))
    me_p = lax.axis_index("pipe")
    me_d = lax.axis_index("dp")
    me_x = lax.rem(me_p, 2)
    me_y = lax.div(me_p, 2)
    NP, ND, M, GM, G, R = c.pipes, c.dps, c.micro, c.gm, c.groups, c.pad
    flat = GM * R
    count = float(c.total)

    def shard(k, p):
        half = lax.div(p, 2)
        return 2 * lax.rem(p, 2) + (half if k == 0 else 1 - half)

    def pipe_peer(i):
        return lax.rem(me_p + i, NP)

    def dp_peer(i):
        return lax.rem(me_d + i, ND)

    def remote(src, dst, ss, rs, p, d):
        return pltpu.make_async_remote_copy(
            src_ref=src, dst_ref=dst, send_sem=ss, recv_sem=rs, device_id=(p, d), device_id_type=MESH
        )

    def take_recv(view, ss, rs):
        remote(view, view, ss, rs, me_p, me_d).wait_recv()

    def take_send(view, ss, rs):
        remote(view, view, ss, rs, me_p, me_d).wait_send()

    def group(g):
        return pl.ds(g * GM, GM)

    owed, due = {}, {}

    lane0 = pl.multiple_of(me_p * c.cs, LANES)
    seg_cols = pl.ds(lane0, c.cs)
    load_u = pltpu.make_async_copy(u_hbm.at[:, :, seg_cols], s.u_seg.at[0], s.in_r.at[0])
    load_g = pltpu.make_async_copy(go_hbm.at[:, :, seg_cols], s.g_seg, s.in_r.at[1])
    load_all = pltpu.make_async_copy(u_hbm, s.u_all, s.in_r.at[2])
    load_p = pltpu.make_async_copy(pw_hbm, s.p_own, s.in_r.at[3])
    load_w = [
        pltpu.make_async_copy(sw_hbm.at[:, :, pl.ds(h * LANES, LANES)], s.sw.at[h], s.in_r.at[4 + h]) for h in range(2)
    ]
    load_all.start()

    @pl.when(me_p == 0)
    def _():
        load_p.start()

    for load in load_w:
        load.start()
    load_u.start()
    load_g.start()

    barrier = pltpu.get_barrier_semaphore()
    for i in range(1, NP):
        pl.semaphore_signal(barrier, inc=1, device_id=(pipe_peer(i), me_d), device_id_type=MESH)

    @pl.loop(1, ND)
    def _(i):
        pl.semaphore_signal(barrier, inc=1, device_id=(me_p, dp_peer(i)), device_id_type=MESH)

    row = lax.broadcasted_iota(jnp.int32, (R, LANES), 0)
    image = jnp.zeros_like(row)
    for n in range(1, c.images):
        image = image + (row >= n * SIDE * SIDE).astype(jnp.int32)
    pixel = row - image * (SIDE * SIDE)
    up = jnp.zeros_like(row)
    for n in range(1, SIDE):
        up = up + (pixel >= n * SIDE).astype(jnp.int32)
    across = pixel - up * SIDE
    for t in range(TAPS):
        i, j = t // 3 - 1, t % 3 - 1
        ok = (up + i >= 0) & (up + i < SIDE) & (across + j >= 0) & (across + j < SIDE) & (row < c.rows)
        s.mask[t] = ok.astype(F32)
    s.norm_sum[...] = jnp.zeros_like(s.norm_sum)

    pl.semaphore_wait(barrier, NP - 1 + ND - 1)

    me_c = lax.rem(me_d, 2)
    me_z = lax.div(me_d, 2)
    sib = me_d + 1 - 2 * me_c

    def link_peer(i):
        flip = me_p + 1 - 2 * me_x
        return (None, flip, lax.rem(me_p + 2, NP), lax.rem(flip + 2, NP))[i]

    def on_pipes(*pipes):
        here = me_p == pipes[0]
        for p in pipes[1:]:
            here = here | (me_p == p)
        return pl.when(here)

    me_l = lax.rem(me_z, 2)
    low = 2 * (me_z + 1 - 2 * me_l) + me_c

    def quarter(part, core, z):
        if part < 4:
            return s.pq.at[part, pl.ds(pl.multiple_of((2 * core + z) * (c.cs // 4), 16), c.cs // 4)]
        return s.wf.at[part - 4, :, pl.ds(pl.multiple_of((2 * core + z) * (c.mid // 4), 16), c.mid // 4)]

    def whole_part(part, core):
        if part < 4:
            return s.pq.at[part] if core is None else s.pq.at[part, pl.ds(pl.multiple_of(core * (c.cs // 2), 16), c.cs // 2)]
        rows = pl.ds(0, c.mid) if core is None else pl.ds(pl.multiple_of(core * (c.mid // 2), 16), c.mid // 2)
        return s.wf.at[part - 4, :, rows]

    def here_already(part):
        return me_p == part if part < 4 else me_y == part - 4

    def proj_send(i):
        p = link_peer(i)
        n = c.cs // 4
        base = (2 * me_c + me_l) * n
        src = pw_hbm.at[pl.ds(pl.multiple_of(p * c.cs + base, 16), n)]
        dst = s.pq.at[me_p, pl.ds(pl.multiple_of(base, 16), n)]
        return remote(src, dst, s.w_s.at[0, i], s.w_r.at[me_p], p, me_d)

    def front_send():
        rows = pl.ds(pl.multiple_of((2 * me_c + me_l) * (c.mid // 4), 16), c.mid // 4)
        return remote(s.sw.at[1, :, rows], s.wf.at[me_y, :, rows], s.w_s.at[1, 0], s.w_r.at[4 + me_y], link_peer(2), me_d)

    def pass_copies(part):
        near, far = quarter(part, me_c, me_l), quarter(part, me_c, 1 - me_l)
        return (
            remote(near, near, s.pass_s.at[part, 0], s.w_z.at[part], me_p, low),
            remote(near, near, s.pass_s.at[part, 1], s.w_q.at[part], me_p, sib),
            remote(far, far, s.pass_s.at[part, 2], s.w_q.at[part], me_p, sib),
        )

    def pass_one(*parts):
        for part in parts:

            @pl.when(jnp.logical_not(here_already(part)))
            def _():
                take_recv(quarter(part, me_c, me_l), s.pass_s.at[part, 0], s.w_r.at[part])
                for copy in pass_copies(part)[:2]:
                    copy.start()

    def pass_two(*parts):
        for part in parts:

            @pl.when(jnp.logical_not(here_already(part)))
            def _():
                take_recv(quarter(part, me_c, 1 - me_l), s.pass_s.at[part, 0], s.w_z.at[part])
                pass_copies(part)[2].start()

    def need(*parts):
        for part in parts:

            @pl.when(jnp.logical_not(here_already(part)))
            def _():
                take_recv(whole_part(part, 1 - me_c), s.pass_s.at[part, 0], s.w_q.at[part])

            @pl.when(here_already(part))
            def _():
                pltpu.make_async_copy(whole_part(part, None), whole_part(part, None), s.w_r.at[part]).wait()

    def end_part(part):
        @pl.when(jnp.logical_not(here_already(part)))
        def _():
            for copy in pass_copies(part):
                copy.wait_send()

    for load in load_w:
        load.wait()

    front_send().start()

    @on_pipes(2)
    def _():
        for i in range(1, NP):
            proj_send(i).start()

    own_rows = pl.ds(pl.multiple_of(me_p * c.cs, 16), c.cs)
    pltpu.make_async_copy(pw_hbm.at[own_rows], s.pq.at[me_p], s.w_r.at[me_p]).start()
    pltpu.make_async_copy(s.sw.at[0], s.wf.at[me_y], s.w_r.at[4 + me_y]).start()

    def note(kind, idx, view, ss, rs):
        owed[kind, idx] = lambda g: take_send(view(g), ss.at[idx, g], rs.at[idx, g])
        due[kind, idx] = lambda g: take_recv(view(g), ss.at[idx, g], rs.at[idx, g])

    def grab(kind, idx, g):
        due.pop((kind, idx))(g)

    def ar_ref(idx):
        return s.ar_small.at[idx] if idx < 8 else s.ar_wide.at[idx - 8]

    def ar_send(idx, g, first, second):
        buf = ar_ref(idx)
        buf[me_d, group(g), 0:1, :] = first
        buf[me_d, group(g), 1:2, :] = second

        @pl.loop(1, ND)
        def _(i):
            view = buf.at[me_d, group(g)]
            remote(view, view, s.ar_s.at[idx, g], s.ar_r.at[idx, g], me_p, dp_peer(i)).start()

        note("ar", idx, lambda g: ar_ref(idx).at[pl.ds(0, ND - 1), group(g)], s.ar_s, s.ar_r)

    def ar_take(idx, g):
        buf = ar_ref(idx)
        grab("ar", idx, g)
        tot = buf[0, group(g)]
        for d in range(1, ND):
            tot = tot + buf[d, group(g)]
        return tot[:, 0:1, :], tot[:, 1:2, :]

    def ag_send(idx, g, buf, slot):
        view = buf.at[slot, group(g)]
        for i in range(1, NP):
            remote(view, view, s.ag_s.at[idx, g], s.ag_r.at[idx, g], pipe_peer(i), me_d).start()
        note("ag", idx, lambda g: s.h1.at[0, pl.ds(0, NP - 1), group(g)], s.ag_s, s.ag_r)

    def ag_take(idx, g, buf):
        grab("ag", idx, g)
        return jnp.concatenate([buf[j, group(g)].reshape(flat, LANES) for j in range(NP)], axis=1)

    def rs_send(idx, g, k, partial):
        for j in range(NP):
            s.put[idx, j, group(g)] = partial[:, j * LANES : (j + 1) * LANES].reshape(GM, R, LANES).astype(BF16)
        for i in range(1, NP):
            p = pipe_peer(i)
            remote(
                s.put.at[idx, shard(k, p), group(g)],
                s.got.at[idx, me_p, group(g)],
                s.rs_s.at[idx, g],
                s.rs_r.at[idx, g],
                p,
                me_d,
            ).start()
        note("rs", idx, lambda g: s.got.at[idx, pl.ds(0, NP - 1), group(g)], s.rs_s, s.rs_r)

    def rs_take(idx, g, k):
        grab("rs", idx, g)
        tot = s.put[idx, shard(k, me_p), group(g)].astype(F32)
        for i in range(1, NP):
            tot = tot + s.got[idx, pipe_peer(i), group(g)].astype(F32)
        return tot

    def shard_cols(base, k):
        return pl.ds(pl.multiple_of(base + shard(k, me_p) * LANES, LANES), LANES)

    def norm_cols(which, k):
        if which == 1:
            return shard_cols(0, k)
        if which == 2:
            return shard_cols(c.mid, k)
        return pl.ds(pl.multiple_of(2 * c.mid + me_p * c.cs, LANES), c.cs)

    def real_rows(width):
        return lax.broadcasted_iota(jnp.int32, (GM, R, width), 1) < c.rows

    ZD = {1: (s.z1, s.d1, s.gr1), 2: (s.z2, s.d2, s.gr2), 3: (s.z3, s.d3, s.gr3)}
    FWD = {(0, 1): 0, (0, 2): 1, (1, 1): 2, (1, 2): 3, (0, 3): 8, (1, 3): 9}
    BWD = {(1, 2): 4, (1, 1): 5, (0, 2): 6, (0, 1): 7, (1, 3): 10, (0, 3): 11}

    def stats_out(k, which, g, a):
        ZD[which][0][k, group(g)] = a
        ar_send(FWD[(k, which)], g, jnp.sum(a, axis=1, keepdims=True), jnp.sum(a * a, axis=1, keepdims=True))

    def normed(k, which, g):
        z_ref, _, gr_ref = ZD[which]
        one, two = ar_take(FWD[(k, which)], g)
        mean = one / count
        inv = lax.rsqrt(two / count - mean * mean + EPS)
        z = (z_ref[k, group(g)] - mean) * inv
        z_ref[k, group(g)] = z
        gain = gain_ref[k : k + 1, norm_cols(which, k)][None]
        gr_ref[k, group(g)] = gain * inv
        return z * gain + shift_ref[k : k + 1, norm_cols(which, k)][None]

    def hidden_out(k, which, g, idx, buf):
        act, slope = gelu_pair(normed(k, which, g))
        ZD[which][1][k, group(g)] = slope
        mine = shard(k, me_p)
        buf[k, mine, group(g)] = jnp.where(real_rows(LANES), act, 0.0).astype(BF16)
        ag_send(idx, g, buf.at[k], mine)

    def back_out(k, which, g, up):
        ar_send(
            BWD[(k, which)],
            g,
            jnp.sum(up, axis=1, keepdims=True),
            jnp.sum(up * ZD[which][0][k, group(g)], axis=1, keepdims=True),
        )

    def back_in(k, which, g, up):
        z_ref, _, gr_ref = ZD[which]
        one, two = ar_take(BWD[(k, which)], g)
        chunk0 = {1: 0, 2: 1, 3: 2}[which]
        for n in range(one.shape[-1] // LANES):
            lanes = slice(n * LANES, (n + 1) * LANES)
            s.norm_sum[me_p, chunk0 + n, 2 * k : 2 * k + 1, :] += jnp.sum(two[:, :, lanes], axis=0)
            s.norm_sum[me_p, chunk0 + n, 2 * k + 1 : 2 * k + 2, :] += jnp.sum(one[:, :, lanes], axis=0)
        grad = gr_ref[k, group(g)] * (up - one / count - z_ref[k, group(g)] * (two / count))
        return jnp.where(real_rows(grad.shape[-1]), grad, 0.0).astype(BF16)

    def shifted(v, by):
        by = by % flat
        return v if by == 0 else pltpu.roll(v, by, 0)

    def tap_shift(t):
        return SIDE * (t // 3 - 1) + (t % 3 - 1)

    def masked(v, t):
        return v.reshape(GM, R, LANES) * s.mask[t][None]

    def conv(k, h):
        acc = None
        for t0 in range(0, TAPS, 2):
            taps = [t for t in (t0, t0 + 1) if t < TAPS]
            w = s.wf[k, taps[0]] if len(taps) == 1 else jnp.concatenate([s.wf[k, t] for t in taps], axis=1)
            y = dot(h, w)
            for n, t in enumerate(taps):
                part = masked(shifted(y[:, n * LANES : (n + 1) * LANES], -tap_shift(t)), t)
                acc = part if acc is None else acc + part
        return acc

    def conv_back(k, g, d):
        flat_d = d.astype(F32)
        for t in range(TAPS):
            part = shifted((flat_d * s.mask[t][None]).reshape(flat, LANES), tap_shift(t))
            s.dcol[k, group(g), :, t * LANES : (t + 1) * LANES] = part.astype(BF16).reshape(GM, R, LANES)
        w = jnp.concatenate([s.wf[k, t] for t in range(TAPS)], axis=1)
        return dot_nt(s.dcol[k, group(g)].reshape(flat, TAPS * LANES), w)

    tail, ends = [], []

    def work():
        load_all.wait()

        @pl.when(me_p == 0)
        def _():
            load_p.wait()

            @pl.loop(0, G)
            def _(g):
                a = dot(s.u_all[group(g)].reshape(flat, c.ch), s.p_own[...])
                for j in range(NP):
                    s.put[0, j, group(g)] = a[:, j * LANES : (j + 1) * LANES].reshape(GM, R, LANES).astype(BF16)
                s.first[group(g)] = s.put[0, 0, group(g)]
                for p in range(1, NP):
                    remote(
                        s.put.at[0, shard(0, jnp.int32(p)), group(g)], s.first.at[group(g)], s.rs_s.at[0, g], s.rs_r.at[0, g], p, me_d
                    ).start()


        for k in range(2):

            @pl.loop(0, G)
            def _(g):
                if k == 0:

                    @pl.when(me_p != 0)
                    def _():
                        take_recv(s.first.at[group(g)], s.rs_s.at[0, g], s.rs_r.at[0, g])

                    a = s.first[group(g)].astype(F32)
                else:
                    a = rs_take(1, g, 1)
                stats_out(k, 1, g, a)
            pass_one(*((4, 5) if k == 0 else (3,)))

            @pl.loop(0, G)
            def _(g):
                hidden_out(k, 1, g, 2 * k, s.h1)
            if k == 0:

                @on_pipes(1)
                def _():
                    for i in range(1, NP):
                        proj_send(i).start()

            else:
                pass_two(3)


            if k == 0:
                pass_two(4, 5)
            need(4 + k)

            @pl.loop(0, G)
            def _(g):
                stats_out(k, 2, g, conv(k, ag_take(2 * k, g, s.h1.at[k])))
            if k == 0:
                pass_one(1, 2)

            @pl.loop(0, G)
            def _(g):
                hidden_out(k, 2, g, 2 * k + 1, s.h2)
            if k == 0:
                pass_two(1, 2)

                @on_pipes(3)
                def _():
                    for i in range(1, NP):
                        proj_send(i).start()


            need(2 * k + 1)
            if k == 0:
                load_u.wait()

            @pl.loop(0, G)
            def _(g):
                a = dot_nt(ag_take(2 * k + 1, g, s.h2.at[k]), s.pq[2 * k + 1])
                stats_out(k, 3, g, a.reshape(GM, R, c.cs))

            if k == 0:
                need(2)

                @pl.loop(0, G)
                def _(g):
                    v = normed(0, 3, g) + s.u_seg[0, group(g)].astype(F32)
                    act, slope = gelu_pair(v)
                    s.d3[0, group(g)] = slope
                    o = jnp.where(real_rows(c.cs), act, 0.0).astype(BF16)
                    s.u_seg[1, group(g)] = o
                    rs_send(1, g, 1, dot(o.reshape(flat, c.cs), s.pq[2]))

        load_g.wait()

        @pl.loop(0, G)
        def _(g):
            v = normed(1, 3, g) + s.u_seg[1, group(g)].astype(F32)
            act, slope = gelu_pair(v)
            o = jnp.where(real_rows(c.cs), act, 0.0).astype(BF16)
            s.out_seg[group(g)] = o
            e = s.g_seg[group(g)].astype(F32) * slope
            s.e3[group(g)] = e
            back_out(1, 3, g, e)
            o32 = o.astype(F32)
            place = lax.broadcasted_iota(jnp.int32, (GM, R, c.cs), 1)
            for n in range(c.images):
                here = (place >= n * SIDE * SIDE) & (place < (n + 1) * SIDE * SIDE)
                mean = jnp.sum(jnp.where(here, o32, 0.0), axis=1, keepdims=True) / float(SIDE * SIDE)
                for m in range(GM):
                    s.pool[(g * GM + m) * c.images + n] = mean[m]

        out_copy = pltpu.make_async_copy(s.out_seg, bo_out, s.out_r.at[0])
        out_copy.start()
        tail.append(out_copy.wait)

        banks = ND * c.bank
        which = lax.broadcasted_iota(jnp.int32, (banks, c.cs), 0)
        term = jnp.zeros((banks, c.cs), F32)
        for n in range(M * c.images):
            ids = jnp.concatenate([ids_ref[n : n + 1, :]] * (c.cs // LANES), axis=1)
            term = term + jnp.where(which == ids, s.pool[n], 0.0)
        s.bank_put[...] = term.reshape(ND, c.bank, c.cs)

        @pl.loop(1, ND)
        def _(i):
            d = dp_peer(i)
            remote(s.bank_put.at[d], s.bank_got.at[me_d], s.bank_s.at[0], s.bank_r.at[0], me_p, d).start()

        tail.append(lambda: take_send(s.bank_got.at[pl.ds(0, ND - 1)], s.bank_s.at[0], s.bank_r.at[0]))

        s.bank_got[me_d] = s.bank_put[me_d]

        def all_rows(ref):
            return ref[...].reshape(M * R, ref.shape[-1])

        def all_seg(ref):
            return jnp.concatenate([ref[j].reshape(M * R, LANES) for j in range(NP)], axis=1)

        def grad_q(k):
            h = all_seg(s.h2.at[k])
            s.gp[2 * k + 1] = dot_tn(all_rows(s.da3.at[k]), h).astype(BF16)

        def grad_p0():
            d = s.da1[0, shard(0, me_p)].reshape(M * R, LANES)
            s.g0[...] = dot_tn(all_rows(s.u_all), d).astype(BF16)

        def grad_p(k):
            d = all_seg(s.da1.at[k])
            s.gp[2 * k] = dot_tn(all_rows(s.u_seg.at[k]), d).astype(BF16)

        def grad_w(k):
            h = all_seg(s.h1.at[k])
            for t0 in range(0, TAPS, 2):
                taps = [t for t in (t0, t0 + 1) if t < TAPS]
                d = s.dcol[k, :, :, t0 * LANES : (t0 + len(taps)) * LANES].reshape(M * R, len(taps) * LANES)
                v = dot_tn(h, d)
                for n, t in enumerate(taps):
                    s.gw[k, t * c.mid : (t + 1) * c.mid, :] = v[:, n * LANES : (n + 1) * LANES].astype(BF16)

        def part(base, n):
            return pl.ds(pl.multiple_of(base, 16), n)

        inner = (me_z == 1) | (me_z == 2)
        z_side = lax.div(me_z, 2)
        outer_dev = 2 * (3 * z_side) + me_c
        inner_dev = 2 * (1 + z_side) + me_c
        across_dev = 2 * (2 - z_side) + me_c

        def job_own(job):
            kind, k, n, base, slot = c.jobs[job]
            ref = s.g0 if kind == "0" else s.gw.at[k] if kind == "w" else s.gp.at[2 * k + (kind == "q")]
            return ref, base

        def job_ref(name, job):
            kind, k, n, base, slot = c.jobs[job]
            return getattr(s, name + ("p" if kind in "pq" else kind)).at[slot]

        def job_core(job):
            own, base = job_own(job)
            n = c.jobs[job][2]
            view = own.at[part(base + (1 - me_c) * n, n)]
            remote(view, job_ref("ja", job), s.gs.at[job, 0], s.gr.at[job, 0], me_p, sib).start()

        def job_in(job):
            own, base = job_own(job)
            n = c.jobs[job][2]
            got, tot = job_ref("ja", job), job_ref("jb", job)
            take_recv(got, s.gs.at[job, 0], s.gr.at[job, 0])
            tot[...] = (got[...].astype(F32) + own[part(base + me_c * n, n), :].astype(F32)).astype(BF16)
            @pl.when(jnp.logical_not(inner))
            def _():
                remote(tot, job_ref("jc", job), s.gs.at[job, 1], s.gr.at[job, 1], me_p, inner_dev).start()

        def job_halve(job):
            n = c.jobs[job][2]
            got, tot, half = job_ref("jc", job), job_ref("jb", job), job_ref("jd", job)

            @pl.when(inner)
            def _():
                take_recv(got, s.gs.at[job, 1], s.gr.at[job, 1])
                tot[...] = (got[...].astype(F32) + tot[...].astype(F32)).astype(BF16)
                view = tot.at[part((1 - z_side) * (n // 2), n // 2)]
                remote(view, half, s.gs.at[job, 2], s.gr.at[job, 2], me_p, across_dev).start()

        def job_sum(job):
            n = c.jobs[job][2]
            tot, half, fin = job_ref("jb", job), job_ref("jd", job), job_ref("je", job)
            mine = part(z_side * (n // 2), n // 2)

            @pl.when(inner)
            def _():
                take_recv(half, s.gs.at[job, 2], s.gr.at[job, 2])
                fin[mine, :] = (half[...].astype(F32) + tot[mine, :].astype(F32)).astype(BF16)
                view = fin.at[mine]
                remote(view, view, s.gs.at[job, 3], s.gr.at[job, 3], me_p, across_dev).start()
                remote(view, view, s.gs.at[job, 4], s.gr.at[job, 3], me_p, outer_dev).start()

        def job_out(job):
            n = c.jobs[job][2]
            fin = job_ref("je", job)
            view = fin.at[part((1 - z_side) * (n // 2), n // 2)]

            @pl.when(inner)
            def _():
                take_recv(view, s.gs.at[job, 3], s.gr.at[job, 3])
                remote(view, view, s.gs.at[job, 5], s.gr.at[job, 4], me_p, outer_dev).start()

        def job_place(job, p, core):
            kind, k, n, base, slot = c.jobs[job]
            if kind == "0":
                return s.p0_out.at[shard(0, p), part(base + core * n, n)]
            if kind == "w":
                return s.w_out.at[lax.div(p, 2) if k == 0 else 1 - lax.div(p, 2), part(base + core * n, n)]
            return s.p_out.at[part(p * 2 * n + core * n, n)]

        def job_home(job, p):
            kind, k = c.jobs[job][:2]
            return 2 * k + lax.rem(p, 2) if kind == "w" else jnp.int32(2 * k + (kind == "q"))

        def job_holds(job):
            kind, k = c.jobs[job][:2]
            return me_y == k if kind == "w" else me_p == 2 * k + (kind == "q")

        def job_plane(job):
            n = c.jobs[job][2]
            fin = job_ref("je", job)

            @pl.when(jnp.logical_not(inner))
            def _():
                for step in (3, 4):
                    take_recv(fin.at[0 : n // 2], s.gs.at[job, step], s.gr.at[job, step])

            home = job_home(job, me_p)

            @pl.when(me_p != home)
            def _():
                remote(fin, job_place(job, me_p, me_c), s.gs.at[job, 6], s.gr.at[job, 5], home, me_d).start()

            @pl.when(me_p == home)
            def _():
                pltpu.make_async_copy(fin, job_place(job, me_p, me_c), s.own_s.at[job]).start()

        def job_many(job, count):
            kind, k, n, base, slot = c.jobs[job]
            if kind == "0":
                return s.p0_out.at[pl.ds(0, count), pl.ds(0, n)]
            return s.w_out.at[pl.ds(0, count), pl.ds(0, n)] if kind == "w" else s.p_out.at[pl.ds(0, n * count)]

        def job_share(job):
            fin = job_ref("je", job)
            from_pipes = [0, 2] if c.jobs[job][0] == "w" else [0, 1, 2, 3]

            @pl.when(job_holds(job))
            def _():
                pltpu.make_async_copy(fin, job_place(job, me_p, me_c), s.own_s.at[job]).wait()
                take_recv(job_many(job, len(from_pipes) - 1), s.gs.at[job, 6], s.gr.at[job, 5])
                for i in from_pipes:
                    view = job_place(job, pipe_peer(i), me_c)
                    remote(view, view, s.fin_s.at[job], s.fin_r.at[job], me_p, sib).start()

        def job_end(job):
            got, half, fin = job_ref("ja", job), job_ref("jd", job), job_ref("je", job)
            take_send(got, s.gs.at[job, 0], s.gr.at[job, 0])

            @pl.when(inner)
            def _():
                for step in (2, 3, 4, 5):
                    take_send(half, s.gs.at[job, step], s.gr.at[job, 2])

            @pl.when(jnp.logical_not(inner))
            def _():
                take_send(got, s.gs.at[job, 1], s.gr.at[job, 1])

            @pl.when(me_p != job_home(job, me_p))
            def _():
                take_send(fin, s.gs.at[job, 6], s.gr.at[job, 5])

            @pl.when(job_holds(job))
            def _():
                view = job_many(job, 2 if c.jobs[job][0] == "w" else NP)
                take_recv(view, s.fin_s.at[job], s.fin_r.at[job])
                take_send(view, s.fin_s.at[job], s.fin_r.at[job])

        steps = (job_core, job_in, job_halve, job_sum, job_out, job_plane, job_share)
        next_step = dict.fromkeys(c.jobs, 0)

        def advance(*jobs):
            if c.deep:
                for job in jobs:
                    if next_step[job] < len(steps):
                        steps[next_step[job]](job)
                        next_step[job] += 1

        def point(k, n):
            advance(*POINTS[(1 - k) * 6 + n])

        for k in (1, 0):
            side = 2 * (1 - k)

            @pl.loop(0, G)
            def _(g):
                grad = back_in(k, 3, g, s.e3[group(g)])
                s.da3[k, group(g)] = grad
                rs_send(2 + (1 - k), g, k, dot(grad.reshape(flat, c.cs), s.pq[2 * k + 1]))

            grad_q(k)
            if k == 1:

                @on_pipes(0)
                def _():
                    for i in range(1, NP):
                        proj_send(i).start()

            point(k, 0)

            @pl.loop(0, G)
            def _(g):
                up = rs_take(2 + (1 - k), g, k) * s.d2[k, group(g)]
                s.t1[group(g)] = up
                back_out(k, 2, g, up)
            if k == 0:
                pass_two(0)
            point(k, 1)

            @pl.loop(0, G)
            def _(g):
                rs_send(5 - k, g, k, conv_back(k, g, back_in(k, 2, g, s.t1[group(g)])))

            grad_w(k)
            point(k, 2)

            @pl.loop(0, G)
            def _(g):
                up = rs_take(5 - k, g, k) * s.d1[k, group(g)]
                s.t1[group(g)] = up
                back_out(k, 1, g, up)
            point(k, 3)

            @pl.loop(0, G)
            def _(g):
                mine = shard(k, me_p)
                s.da1[k, mine, group(g)] = back_in(k, 1, g, s.t1[group(g)])
                ag_send(5 + side, g, s.da1.at[k], mine)
            if k == 0:
                grad_p0()
            point(k, 4)

            if k == 0:
                need(0)
            @pl.loop(0, G)
            def _(g):
                d = dot_nt(ag_take(5 + side, g, s.da1.at[k]), s.pq[2 * k])
                d = d.reshape(GM, R, c.cs) + s.e3[group(g)]
                if k == 1:
                    e = d * s.d3[0, group(g)]
                    s.e3[group(g)] = e
                    back_out(0, 3, g, e)
                else:
                    s.in_seg[group(g)] = d.astype(BF16)

            if k == 1 or not c.deep:
                grad_p(k)
            if k == 1:
                pass_one(0)
            point(k, 5)

        in_copy = pltpu.make_async_copy(s.in_seg, ig_out, s.out_r.at[1])
        in_copy.start()
        tail.append(in_copy.wait)
        view = s.norm_sum.at[me_p]
        for i in range(1, NP):
            remote(view, view, s.ns_s.at[0], s.ns_r.at[0], pipe_peer(i), me_d).start()
        tail.append(lambda: take_send(s.norm_sum.at[pl.ds(0, NP - 1)], s.ns_s.at[0], s.ns_r.at[0]))

        if c.deep:
            for stop in (len(steps) - 1, len(steps)):
                while min(next_step.values()) < stop:
                    advance(*[job for job in LAST if next_step[job] < stop])
            ends.extend(functools.partial(job_end, job) for job in c.jobs)

        take_recv(s.bank_got.at[pl.ds(0, ND - 1)], s.bank_s.at[0], s.bank_r.at[0])
        tot = s.bank_got[0]
        for d in range(1, ND):
            tot = tot + s.bank_got[d]
        mb_out[...] = tot
        take_recv(s.norm_sum.at[pl.ds(0, NP - 1)], s.ns_s.at[0], s.ns_r.at[0])
        per = c.mid // LANES
        wide = c.cs // LANES
        each = (2 * per + c.ch // LANES) // NP
        for k in range(2):
            for n in range(each):
                q = me_p * each + n
                in_one = q < per
                in_two = (q >= per) & (q < 2 * per)
                sh = jnp.where(in_one, q, q - per)
                half = lax.rem(sh + k, 2)
                small = 2 * half + lax.div(sh, 2)
                far = q - 2 * per
                p = jnp.where(q < 2 * per, small, lax.div(far, wide))
                chunk = jnp.where(in_one, 0, jnp.where(in_two, 1, 2 + lax.rem(far, wide)))
                ns_out[n, 2 * k : 2 * k + 2, :] = s.norm_sum[p, chunk, 2 * k : 2 * k + 2, :]

    work()

    for wait in ends:
        wait()
    if c.deep:
        copies = [
            pltpu.make_async_copy(s.w_out.at[h], gw_out.at[:, pl.ds(h * LANES, LANES)], s.out_r.at[2 + h]) for h in range(2)
        ]
        wide = [
            pltpu.make_async_copy(s.p0_out.at[j], gp_out.at[:, pl.ds(j * LANES, LANES)], s.out_r.at[4 + j])
            for j in range(NP)
        ]
        tall = pltpu.make_async_copy(s.p_out, gp_out, s.out_r.at[4])
        for copy in copies:
            copy.start()
        for act in ("start", "wait"):

            @pl.when(me_p == 0)
            def _():
                for copy in wide:
                    getattr(copy, act)()

            @pl.when(me_p != 0)
            def _():
                getattr(tall, act)()

    else:
        copies = [
            pltpu.make_async_copy(s.gp, gp_out, s.out_r.at[2]),
            pltpu.make_async_copy(s.gw, gw_out, s.out_r.at[3]),
        ]
        for copy in copies:
            copy.start()
    front_send().wait_send()
    for i in range(1, NP):
        proj_send(i).wait_send()
    for n in range(6):
        end_part(n)

    @pl.loop(0, G)
    def _(g):
        for wait in [*due.values(), *owed.values()]:
            wait(g)

        @pl.when(me_p == 0)
        def _():
            take_send(s.put.at[0, pl.ds(0, NP - 1), group(g)], s.rs_s.at[0, g], s.rs_r.at[0, g])

    for wait in tail:
        wait()
    for copy in copies:
        copy.wait()


def on_device(mesh, block_input, proj_weight, spatial_weight, norm_gain, norm_shift, output_grad, image_ids):
    bank = 8
    c = Sizes(mesh, block_input, proj_weight, spatial_weight, bank)
    extra = ((0, 0), (0, c.pad - c.rows), (0, 0))
    u = jnp.pad(block_input, extra)
    go = jnp.pad(output_grad, extra)
    sw = spatial_weight.reshape(TAPS, c.mid, spatial_weight.shape[2])
    ids = jnp.broadcast_to(image_ids.reshape(-1, 1), (image_ids.size, LANES))
    items = scratch_list(c)
    names = [n for n, _ in items]
    anyspec = pl.BlockSpec(memory_space=pl.ANY)
    vspec = pl.BlockSpec(memory_space=pltpu.VMEM)
    if c.deep:
        gp_shape, gw_shape = (c.ch, c.mid), (TAPS * c.mid, 2 * LANES)
    else:
        gp_shape, gw_shape = (c.pipes, c.cs, c.mid), (2, TAPS * c.mid, LANES)
    each = (2 * c.mid + c.ch) // LANES // c.pipes
    outs = pl.pallas_call(
        functools.partial(body, c, names),
        out_shape=(
            jax.ShapeDtypeStruct((c.micro, c.pad, c.cs), BF16),
            jax.ShapeDtypeStruct((c.micro, c.pad, c.cs), BF16),
            jax.ShapeDtypeStruct(gp_shape, BF16),
            jax.ShapeDtypeStruct(gw_shape, BF16),
            jax.ShapeDtypeStruct((each, 4, LANES), F32),
            jax.ShapeDtypeStruct((bank, c.cs), F32),
        ),
        in_specs=[anyspec] * 4 + [vspec] * 3,
        out_specs=(anyspec, anyspec, anyspec, anyspec, vspec, vspec),
        scratch_shapes=[v for _, v in items],
        compiler_params=pltpu.CompilerParams(collective_id=0, has_side_effects=True, vmem_limit_bytes=60 << 20),
    )(u, go, proj_weight[0], sw, norm_gain, norm_shift, ids)
    bo, ig, gp, gw, ns, mb = outs
    if not c.deep:
        gp = lax.psum(gp.astype(F32), "dp")
        gw = lax.psum(gw.astype(F32), "dp")
        gp = lax.all_to_all(gp, "pipe", 0, 0, tiled=True).reshape(c.ch, c.mid)
        gw = lax.all_gather(gw, "pipe")
        me = lax.axis_index("pipe")
        y, x = me // 2, me % 2
        near = lax.dynamic_index_in_dim(gw, me, 0, keepdims=False)
        far = lax.dynamic_index_in_dim(gw, 2 * (1 - y) + x, 0, keepdims=False)
        gw = jnp.concatenate(
            [lax.dynamic_index_in_dim(near, y, 0, keepdims=False), lax.dynamic_index_in_dim(far, y, 0, keepdims=False)],
            axis=1,
        )
    ns = jnp.transpose(ns.reshape(each, 2, 2, LANES), (2, 1, 0, 3)).reshape(2, 2, each * LANES)
    return (
        bo[:, : c.rows],
        ig[:, : c.rows],
        gp.astype(F32)[None],
        gw.astype(F32)[None],
        ns[0],
        ns[1],
        mb,
    )


def solution(mesh):
    return jax.shard_map(
        functools.partial(on_device, mesh),
        mesh=mesh,
        in_specs=(
            P(None, "dp", None),
            P("pipe", None, None),
            P("pipe", None, None),
            P(),
            P(),
            P(None, "dp", None),
            P(None, "dp"),
        ),
        out_specs=(
            P(None, "dp", "pipe"),
            P(None, "dp", "pipe"),
            P("pipe", None, None),
            P("pipe", None, None),
            P(None, "pipe"),
            P(None, "pipe"),
            P("dp", "pipe"),
        ),
        check_vma=False,
    )
```

```python
import functools
import math
import types

import jax
import jax.numpy as jnp
from jax import lax
from jax.experimental import pallas as pl
from jax.experimental.pallas import tpu as pltpu
from jax.sharding import PartitionSpec as P

SIDE = 7
TAPS = 9
EPS = 1e-05
LANES = 128
GROUPS = 4
W_PIECES = 3
P_PIECES = 2
POINTS = (
    (0,),
    (0,),
    (0, 1, 2, 3),
    (0, 1, 2),
    (0, 1),
    (1, 2, 3, 4),
    (0, 1, 2, 3, 4, 5),
    (2, 3, 4, 5),
    (6, 7, 8, 1, 2, 3, 4, 5),
    (6, 7, 8, 5, 4),
    (9, 10, 6, 5),
    (9, 10, 6, 7, 8, 5, 3, 4),
)
LAST = (6, 7, 8, 9, 10, 5, 4, 3, 0, 1, 2)
MESH = pl.DeviceIdType.MESH
F32 = jnp.float32
BF16 = jnp.bfloat16


def gelu_pair(v):
    c0 = math.sqrt(2.0 / math.pi)
    c1 = 0.044715
    sq = v * v
    t = jnp.tanh(c0 * v * (1.0 + c1 * sq))
    half = 0.5 + 0.5 * t
    slope = half + (0.5 * c0) * v * (1.0 - t * t) * (1.0 + (3.0 * c1) * sq)
    return v * half, slope


def dot(a, b):
    return jnp.dot(a, b, preferred_element_type=F32)


def dot_nt(a, b):
    return lax.dot_general(a, b, (((1,), (1,)), ((), ())), preferred_element_type=F32)


def dot_tn(a, b):
    return lax.dot_general(a, b, (((0,), (0,)), ((), ())), preferred_element_type=F32)


class Sizes:
    def __init__(self, mesh, block_input, proj, spatial, bank_rows):
        self.pipes = mesh.shape["pipe"]
        self.dps = mesh.shape["dp"]
        self.micro = block_input.shape[0]
        self.rows = block_input.shape[1]
        self.pad = -(-self.rows // 16) * 16
        self.ch = block_input.shape[2]
        self.mid = proj.shape[2]
        self.images = self.rows // (SIDE * SIDE)
        self.cs = self.ch // self.pipes
        self.msd = self.mid // self.pipes
        self.groups = GROUPS
        self.gm = self.micro // self.groups
        self.zs = self.dps // 2
        self.total = self.rows * self.dps
        self.bank = bank_rows
        self.deep = self.zs == 4
        self.jobs = {}
        taps = TAPS // W_PIECES
        for k in (1, 0):
            self.jobs[len(self.jobs)] = ("q", k, self.cs // 2, 0, 1 - k)
            for i in range(W_PIECES):
                self.jobs[len(self.jobs)] = ("w", k, taps * self.mid // 2, i * taps * self.mid, (1 - k) * W_PIECES + i)
            if k == 1:
                self.jobs[len(self.jobs)] = ("p", k, self.cs // 2, 0, 2)
        for i in range(P_PIECES):
            self.jobs[len(self.jobs)] = ("0", 0, self.ch // P_PIECES // 2, i * self.ch // P_PIECES, i)


def scratch_list(c):
    full = (c.micro, c.pad)
    seg = (c.pipes, c.micro, c.pad, LANES)
    items = [
        ("u_all", pltpu.VMEM(full + (c.ch,), BF16)),
        ("u_seg", pltpu.VMEM((2,) + full + (c.cs,), BF16)),
        ("g_seg", pltpu.VMEM(full + (c.cs,), BF16)),
        ("p_own", pltpu.VMEM((c.ch, c.mid), BF16)),
        ("pq", pltpu.VMEM((c.pipes, c.cs, c.mid), BF16)),
        ("wf", pltpu.VMEM((2, TAPS, c.mid, LANES), BF16)),
        ("sw", pltpu.VMEM((2, TAPS, c.mid, LANES), BF16)),
        ("mask", pltpu.VMEM((TAPS, c.pad, LANES), F32)),
        ("z1", pltpu.VMEM((2,) + full + (LANES,), F32)),
        ("d1", pltpu.VMEM((2,) + full + (LANES,), F32)),
        ("z2", pltpu.VMEM((2,) + full + (LANES,), F32)),
        ("d2", pltpu.VMEM((2,) + full + (LANES,), F32)),
        ("z3", pltpu.VMEM((2,) + full + (c.cs,), F32)),
        ("d3", pltpu.VMEM((2,) + full + (c.cs,), F32)),
        ("e3", pltpu.VMEM(full + (c.cs,), F32)),
        ("t1", pltpu.VMEM(full + (LANES,), F32)),
        ("gr1", pltpu.VMEM((2, c.micro, 1, LANES), F32)),
        ("gr2", pltpu.VMEM((2, c.micro, 1, LANES), F32)),
        ("gr3", pltpu.VMEM((2, c.micro, 1, c.cs), F32)),
        ("h1", pltpu.VMEM((2,) + seg, BF16)),
        ("h2", pltpu.VMEM((2,) + seg, BF16)),
        ("da3", pltpu.VMEM((2,) + full + (c.cs,), BF16)),
        ("dcol", pltpu.VMEM((2,) + full + (TAPS * LANES,), BF16)),
        ("da1", pltpu.VMEM((2,) + seg, BF16)),
        ("first", pltpu.VMEM(full + (LANES,), BF16)),
        ("put", pltpu.VMEM((6,) + seg, BF16)),
        ("got", pltpu.VMEM((6,) + seg, BF16)),
        ("out_seg", pltpu.VMEM(full + (c.cs,), BF16)),
        ("in_seg", pltpu.VMEM(full + (c.cs,), BF16)),
        ("ar_small", pltpu.VMEM((8, c.dps, c.micro, 2, LANES), F32)),
        ("ar_wide", pltpu.VMEM((4, c.dps, c.micro, 2, c.cs), F32)),
        ("pool", pltpu.VMEM((c.micro * c.images, 1, c.cs), F32)),
        ("bank_put", pltpu.VMEM((c.dps, c.bank, c.cs), F32)),
        ("bank_got", pltpu.VMEM((c.dps, c.bank, c.cs), F32)),
        ("norm_sum", pltpu.VMEM((c.pipes, 6, 8, LANES), F32)),
        ("gp", pltpu.VMEM((c.pipes, c.cs, c.mid), BF16)),
        ("g0", pltpu.VMEM((c.ch, LANES), BF16)),
        ("gw", pltpu.VMEM((2, TAPS * c.mid, LANES), BF16)),
        ("ar_s", pltpu.SemaphoreType.DMA((12, c.groups))),
        ("ar_r", pltpu.SemaphoreType.DMA((12, c.groups))),
        ("ag_s", pltpu.SemaphoreType.DMA((8, c.groups))),
        ("ag_r", pltpu.SemaphoreType.DMA((8, c.groups))),
        ("rs_s", pltpu.SemaphoreType.DMA((6, c.groups))),
        ("rs_r", pltpu.SemaphoreType.DMA((6, c.groups))),
        ("w_s", pltpu.SemaphoreType.DMA((2, c.pipes))),
        ("pass_s", pltpu.SemaphoreType.DMA((6, 3))),
        ("w_r", pltpu.SemaphoreType.DMA((6,))),
        ("w_z", pltpu.SemaphoreType.DMA((6,))),
        ("w_q", pltpu.SemaphoreType.DMA((6,))),
        ("bank_s", pltpu.SemaphoreType.DMA((1,))),
        ("bank_r", pltpu.SemaphoreType.DMA((1,))),
        ("ns_s", pltpu.SemaphoreType.DMA((1,))),
        ("ns_r", pltpu.SemaphoreType.DMA((1,))),
        ("in_r", pltpu.SemaphoreType.DMA((6,))),
        ("out_r", pltpu.SemaphoreType.DMA((4 + c.pipes,))),
    ]
    if c.deep:
        for name, width in (("p", c.mid), ("w", LANES), ("0", LANES)):
            of = [job for job in c.jobs.values() if job[0] in {"p": "pq"}.get(name, name)]
            lead, n = len(of), of[0][2]
            items += [(key + name, pltpu.VMEM((lead, n // (1 + (key == "jd")), width), BF16)) for key in ("ja", "jb", "jc", "jd", "je")]
        count = len(c.jobs)
        items += [
            ("p_out", pltpu.VMEM((c.ch, c.mid), BF16)),
            ("p0_out", pltpu.VMEM((c.pipes, c.ch, LANES), BF16)),
            ("w_out", pltpu.VMEM((2, TAPS * c.mid, LANES), BF16)),
            ("gs", pltpu.SemaphoreType.DMA((count, 7))),
            ("gr", pltpu.SemaphoreType.DMA((count, 6))),
            ("own_s", pltpu.SemaphoreType.DMA((count,))),
            ("store", pltpu.SemaphoreType.DMA((count, c.pipes))),
            ("fin_s", pltpu.SemaphoreType.DMA((count,))),
            ("fin_r", pltpu.SemaphoreType.DMA((count,))),
        ]
    return items


def body(c, names, *refs):
    (u_hbm, go_hbm, pw_hbm, sw_hbm, gain_ref, shift_ref, ids_ref) = refs[:7]
    (bo_out, ig_out, gp_out, gw_out, ns_out, mb_out) = refs[7:13]
    s = types.SimpleNamespace(**dict(zip(names, refs[13:])))
    me_p = lax.axis_index("pipe")
    me_d = lax.axis_index("dp")
    me_x = lax.rem(me_p, 2)
    me_y = lax.div(me_p, 2)
    NP, ND, M, GM, G, R = c.pipes, c.dps, c.micro, c.gm, c.groups, c.pad
    flat = GM * R
    count = float(c.total)

    def shard(k, p):
        half = lax.div(p, 2)
        return 2 * lax.rem(p, 2) + (half if k == 0 else 1 - half)

    def pipe_peer(i):
        return lax.rem(me_p + i, NP)

    def dp_peer(i):
        return lax.rem(me_d + i, ND)

    def remote(src, dst, ss, rs, p, d):
        return pltpu.make_async_remote_copy(
            src_ref=src, dst_ref=dst, send_sem=ss, recv_sem=rs, device_id=(p, d), device_id_type=MESH
        )

    def take_recv(view, ss, rs):
        remote(view, view, ss, rs, me_p, me_d).wait_recv()

    def take_send(view, ss, rs):
        remote(view, view, ss, rs, me_p, me_d).wait_send()

    def group(g):
        return pl.ds(g * GM, GM)

    owed, due = {}, {}

    lane0 = pl.multiple_of(me_p * c.cs, LANES)
    seg_cols = pl.ds(lane0, c.cs)
    load_u = pltpu.make_async_copy(u_hbm.at[:, :, seg_cols], s.u_seg.at[0], s.in_r.at[0])
    load_g = pltpu.make_async_copy(go_hbm, s.g_seg, s.in_r.at[1])
    load_all = pltpu.make_async_copy(u_hbm, s.u_all, s.in_r.at[2])
    load_p = pltpu.make_async_copy(pw_hbm, s.p_own, s.in_r.at[3])
    load_w = [
        pltpu.make_async_copy(sw_hbm.at[:, :, pl.ds(h * LANES, LANES)], s.sw.at[h], s.in_r.at[4 + h]) for h in range(2)
    ]
    load_all.start()

    @pl.when(me_p == 0)
    def _():
        load_p.start()

    for load in load_w:
        load.start()
    load_u.start()
    load_g.start()

    barrier = pltpu.get_barrier_semaphore()
    for i in range(1, NP):
        pl.semaphore_signal(barrier, inc=1, device_id=(pipe_peer(i), me_d), device_id_type=MESH)

    @pl.loop(1, ND)
    def _(i):
        pl.semaphore_signal(barrier, inc=1, device_id=(me_p, dp_peer(i)), device_id_type=MESH)

    row = lax.broadcasted_iota(jnp.int32, (R, LANES), 0)
    image = jnp.zeros_like(row)
    for n in range(1, c.images):
        image = image + (row >= n * SIDE * SIDE).astype(jnp.int32)
    pixel = row - image * (SIDE * SIDE)
    up = jnp.zeros_like(row)
    for n in range(1, SIDE):
        up = up + (pixel >= n * SIDE).astype(jnp.int32)
    across = pixel - up * SIDE
    for t in range(TAPS):
        i, j = t // 3 - 1, t % 3 - 1
        ok = (up + i >= 0) & (up + i < SIDE) & (across + j >= 0) & (across + j < SIDE) & (row < c.rows)
        s.mask[t] = ok.astype(F32)
    s.norm_sum[...] = jnp.zeros_like(s.norm_sum)

    pl.semaphore_wait(barrier, NP - 1 + ND - 1)

    me_c = lax.rem(me_d, 2)
    me_z = lax.div(me_d, 2)
    sib = me_d + 1 - 2 * me_c

    def link_peer(i):
        flip = me_p + 1 - 2 * me_x
        return (None, flip, lax.rem(me_p + 2, NP), lax.rem(flip + 2, NP))[i]

    def on_pipes(*pipes):
        here = me_p == pipes[0]
        for p in pipes[1:]:
            here = here | (me_p == p)
        return pl.when(here)

    me_l = lax.rem(me_z, 2)
    low = 2 * (me_z + 1 - 2 * me_l) + me_c

    def quarter(part, core, z):
        if part < 4:
            return s.pq.at[part, pl.ds(pl.multiple_of((2 * core + z) * (c.cs // 4), 16), c.cs // 4)]
        return s.wf.at[part - 4, :, pl.ds(pl.multiple_of((2 * core + z) * (c.mid // 4), 16), c.mid // 4)]

    def whole_part(part, core):
        if part < 4:
            return s.pq.at[part] if core is None else s.pq.at[part, pl.ds(pl.multiple_of(core * (c.cs // 2), 16), c.cs // 2)]
        rows = pl.ds(0, c.mid) if core is None else pl.ds(pl.multiple_of(core * (c.mid // 2), 16), c.mid // 2)
        return s.wf.at[part - 4, :, rows]

    def here_already(part):
        return me_p == part if part < 4 else me_y == part - 4

    def proj_send(i):
        p = link_peer(i)
        n = c.cs // 4
        base = (2 * me_c + me_l) * n
        src = pw_hbm.at[pl.ds(pl.multiple_of(p * c.cs + base, 16), n)]
        dst = s.pq.at[me_p, pl.ds(pl.multiple_of(base, 16), n)]
        return remote(src, dst, s.w_s.at[0, i], s.w_r.at[me_p], p, me_d)

    def front_send():
        rows = pl.ds(pl.multiple_of((2 * me_c + me_l) * (c.mid // 4), 16), c.mid // 4)
        return remote(s.sw.at[1, :, rows], s.wf.at[me_y, :, rows], s.w_s.at[1, 0], s.w_r.at[4 + me_y], link_peer(2), me_d)

    def pass_copies(part):
        near, far = quarter(part, me_c, me_l), quarter(part, me_c, 1 - me_l)
        return (
            remote(near, near, s.pass_s.at[part, 0], s.w_z.at[part], me_p, low),
            remote(near, near, s.pass_s.at[part, 1], s.w_q.at[part], me_p, sib),
            remote(far, far, s.pass_s.at[part, 2], s.w_q.at[part], me_p, sib),
        )

    def pass_one(*parts):
        for part in parts:

            @pl.when(jnp.logical_not(here_already(part)))
            def _():
                take_recv(quarter(part, me_c, me_l), s.pass_s.at[part, 0], s.w_r.at[part])
                for copy in pass_copies(part)[:2]:
                    copy.start()

    def pass_two(*parts):
        for part in parts:

            @pl.when(jnp.logical_not(here_already(part)))
            def _():
                take_recv(quarter(part, me_c, 1 - me_l), s.pass_s.at[part, 0], s.w_z.at[part])
                pass_copies(part)[2].start()

    def need(*parts):
        for part in parts:

            @pl.when(jnp.logical_not(here_already(part)))
            def _():
                take_recv(whole_part(part, 1 - me_c), s.pass_s.at[part, 0], s.w_q.at[part])

            @pl.when(here_already(part))
            def _():
                pltpu.make_async_copy(whole_part(part, None), whole_part(part, None), s.w_r.at[part]).wait()

    def end_part(part):
        @pl.when(jnp.logical_not(here_already(part)))
        def _():
            for copy in pass_copies(part):
                copy.wait_send()

    for load in load_w:
        load.wait()

    front_send().start()

    @on_pipes(2)
    def _():
        for i in range(1, NP):
            proj_send(i).start()

    own_rows = pl.ds(pl.multiple_of(me_p * c.cs, 16), c.cs)
    pltpu.make_async_copy(pw_hbm.at[own_rows], s.pq.at[me_p], s.w_r.at[me_p]).start()
    pltpu.make_async_copy(s.sw.at[0], s.wf.at[me_y], s.w_r.at[4 + me_y]).start()

    def note(kind, idx, view, ss, rs):
        owed[kind, idx] = lambda g: take_send(view(g), ss.at[idx, g], rs.at[idx, g])
        due[kind, idx] = lambda g: take_recv(view(g), ss.at[idx, g], rs.at[idx, g])

    def grab(kind, idx, g):
        due.pop((kind, idx))(g)

    def ar_ref(idx):
        return s.ar_small.at[idx] if idx < 8 else s.ar_wide.at[idx - 8]

    def ar_send(idx, g, first, second):
        buf = ar_ref(idx)
        buf[me_d, group(g), 0:1, :] = first
        buf[me_d, group(g), 1:2, :] = second

        @pl.loop(1, ND)
        def _(i):
            view = buf.at[me_d, group(g)]
            remote(view, view, s.ar_s.at[idx, g], s.ar_r.at[idx, g], me_p, dp_peer(i)).start()

        note("ar", idx, lambda g: ar_ref(idx).at[pl.ds(0, ND - 1), group(g)], s.ar_s, s.ar_r)

    def ar_take(idx, g):
        buf = ar_ref(idx)
        grab("ar", idx, g)
        tot = buf[0, group(g)]
        for d in range(1, ND):
            tot = tot + buf[d, group(g)]
        return tot[:, 0:1, :], tot[:, 1:2, :]

    def ag_send(idx, g, buf, slot):
        view = buf.at[slot, group(g)]
        for i in range(1, NP):
            remote(view, view, s.ag_s.at[idx, g], s.ag_r.at[idx, g], pipe_peer(i), me_d).start()
        note("ag", idx, lambda g: s.h1.at[0, pl.ds(0, NP - 1), group(g)], s.ag_s, s.ag_r)

    def ag_take(idx, g, buf):
        grab("ag", idx, g)
        return jnp.concatenate([buf[j, group(g)].reshape(flat, LANES) for j in range(NP)], axis=1)

    def rs_send(idx, g, k, partial):
        for j in range(NP):
            s.put[idx, j, group(g)] = partial[:, j * LANES : (j + 1) * LANES].reshape(GM, R, LANES).astype(BF16)
        for i in range(1, NP):
            p = pipe_peer(i)
            remote(
                s.put.at[idx, shard(k, p), group(g)],
                s.got.at[idx, me_p, group(g)],
                s.rs_s.at[idx, g],
                s.rs_r.at[idx, g],
                p,
                me_d,
            ).start()
        note("rs", idx, lambda g: s.got.at[idx, pl.ds(0, NP - 1), group(g)], s.rs_s, s.rs_r)

    def rs_take(idx, g, k):
        grab("rs", idx, g)
        tot = s.put[idx, shard(k, me_p), group(g)].astype(F32)
        for i in range(1, NP):
            tot = tot + s.got[idx, pipe_peer(i), group(g)].astype(F32)
        return tot

    def shard_cols(base, k):
        return pl.ds(pl.multiple_of(base + shard(k, me_p) * LANES, LANES), LANES)

    def norm_cols(which, k):
        if which == 1:
            return shard_cols(0, k)
        if which == 2:
            return shard_cols(c.mid, k)
        return pl.ds(pl.multiple_of(2 * c.mid + me_p * c.cs, LANES), c.cs)

    def real_rows(width):
        return lax.broadcasted_iota(jnp.int32, (GM, R, width), 1) < c.rows

    ZD = {1: (s.z1, s.d1, s.gr1), 2: (s.z2, s.d2, s.gr2), 3: (s.z3, s.d3, s.gr3)}
    FWD = {(0, 1): 0, (0, 2): 1, (1, 1): 2, (1, 2): 3, (0, 3): 8, (1, 3): 9}
    BWD = {(1, 2): 4, (1, 1): 5, (0, 2): 6, (0, 1): 7, (1, 3): 10, (0, 3): 11}

    def stats_out(k, which, g, a):
        ZD[which][0][k, group(g)] = a
        ar_send(FWD[(k, which)], g, jnp.sum(a, axis=1, keepdims=True), jnp.sum(a * a, axis=1, keepdims=True))

    def normed(k, which, g):
        z_ref, _, gr_ref = ZD[which]
        one, two = ar_take(FWD[(k, which)], g)
        mean = one / count
        inv = lax.rsqrt(two / count - mean * mean + EPS)
        z = (z_ref[k, group(g)] - mean) * inv
        z_ref[k, group(g)] = z
        gain = gain_ref[k : k + 1, norm_cols(which, k)][None]
        gr_ref[k, group(g)] = gain * inv
        return z * gain + shift_ref[k : k + 1, norm_cols(which, k)][None]

    def hidden_out(k, which, g, idx, buf):
        act, slope = gelu_pair(normed(k, which, g))
        ZD[which][1][k, group(g)] = slope
        mine = shard(k, me_p)
        buf[k, mine, group(g)] = jnp.where(real_rows(LANES), act, 0.0).astype(BF16)
        ag_send(idx, g, buf.at[k], mine)

    def back_out(k, which, g, up):
        ar_send(
            BWD[(k, which)],
            g,
            jnp.sum(up, axis=1, keepdims=True),
            jnp.sum(up * ZD[which][0][k, group(g)], axis=1, keepdims=True),
        )

    def back_in(k, which, g, up):
        z_ref, _, gr_ref = ZD[which]
        one, two = ar_take(BWD[(k, which)], g)
        chunk0 = {1: 0, 2: 1, 3: 2}[which]
        for n in range(one.shape[-1] // LANES):
            lanes = slice(n * LANES, (n + 1) * LANES)
            s.norm_sum[me_p, chunk0 + n, 2 * k : 2 * k + 1, :] += jnp.sum(two[:, :, lanes], axis=0)
            s.norm_sum[me_p, chunk0 + n, 2 * k + 1 : 2 * k + 2, :] += jnp.sum(one[:, :, lanes], axis=0)
        grad = gr_ref[k, group(g)] * (up - one / count - z_ref[k, group(g)] * (two / count))
        return jnp.where(real_rows(grad.shape[-1]), grad, 0.0).astype(BF16)

    def shifted(v, by):
        by = by % flat
        return v if by == 0 else pltpu.roll(v, by, 0)

    def tap_shift(t):
        return SIDE * (t // 3 - 1) + (t % 3 - 1)

    def masked(v, t):
        return v.reshape(GM, R, LANES) * s.mask[t][None]

    def conv(k, h):
        acc = None
        for t0 in range(0, TAPS, 2):
            taps = [t for t in (t0, t0 + 1) if t < TAPS]
            w = s.wf[k, taps[0]] if len(taps) == 1 else jnp.concatenate([s.wf[k, t] for t in taps], axis=1)
            y = dot(h, w)
            for n, t in enumerate(taps):
                part = masked(shifted(y[:, n * LANES : (n + 1) * LANES], -tap_shift(t)), t)
                acc = part if acc is None else acc + part
        return acc

    def conv_back(k, g, d):
        flat_d = d.astype(F32)
        for t in range(TAPS):
            part = shifted((flat_d * s.mask[t][None]).reshape(flat, LANES), tap_shift(t))
            s.dcol[k, group(g), :, t * LANES : (t + 1) * LANES] = part.astype(BF16).reshape(GM, R, LANES)
        w = jnp.concatenate([s.wf[k, t] for t in range(TAPS)], axis=1)
        return dot_nt(s.dcol[k, group(g)].reshape(flat, TAPS * LANES), w)

    tail = []

    def work():
        load_all.wait()

        @pl.when(me_p == 0)
        def _():
            load_p.wait()

            @pl.loop(0, G)
            def _(g):
                a = dot(s.u_all[group(g)].reshape(flat, c.ch), s.p_own[...])
                for j in range(NP):
                    s.put[0, j, group(g)] = a[:, j * LANES : (j + 1) * LANES].reshape(GM, R, LANES).astype(BF16)
                s.first[group(g)] = s.put[0, 0, group(g)]
                for p in range(1, NP):
                    remote(
                        s.put.at[0, shard(0, jnp.int32(p)), group(g)], s.first.at[group(g)], s.rs_s.at[0, g], s.rs_r.at[0, g], p, me_d
                    ).start()


        for k in range(2):

            @pl.loop(0, G)
            def _(g):
                if k == 0:

                    @pl.when(me_p != 0)
                    def _():
                        take_recv(s.first.at[group(g)], s.rs_s.at[0, g], s.rs_r.at[0, g])

                    a = s.first[group(g)].astype(F32)
                else:
                    a = rs_take(1, g, 1)
                stats_out(k, 1, g, a)
            pass_one(*((4, 5) if k == 0 else (3,)))

            @pl.loop(0, G)
            def _(g):
                hidden_out(k, 1, g, 2 * k, s.h1)
            if k == 0:

                @on_pipes(1)
                def _():
                    for i in range(1, NP):
                        proj_send(i).start()

            else:
                pass_two(3)


            if k == 0:
                pass_two(4, 5)
            need(4 + k)

            @pl.loop(0, G)
            def _(g):
                stats_out(k, 2, g, conv(k, ag_take(2 * k, g, s.h1.at[k])))
            if k == 0:
                pass_one(1, 2)

            @pl.loop(0, G)
            def _(g):
                hidden_out(k, 2, g, 2 * k + 1, s.h2)
            if k == 0:
                pass_two(1, 2)

                @on_pipes(3)
                def _():
                    for i in range(1, NP):
                        proj_send(i).start()


            need(2 * k + 1)
            if k == 0:
                load_u.wait()

            @pl.loop(0, G)
            def _(g):
                a = dot_nt(ag_take(2 * k + 1, g, s.h2.at[k]), s.pq[2 * k + 1])
                stats_out(k, 3, g, a.reshape(GM, R, c.cs))

            if k == 0:
                need(2)

                @pl.loop(0, G)
                def _(g):
                    v = normed(0, 3, g) + s.u_seg[0, group(g)].astype(F32)
                    act, slope = gelu_pair(v)
                    s.d3[0, group(g)] = slope
                    o = jnp.where(real_rows(c.cs), act, 0.0).astype(BF16)
                    s.u_seg[1, group(g)] = o
                    rs_send(1, g, 1, dot(o.reshape(flat, c.cs), s.pq[2]))

        load_g.wait()

        @pl.loop(0, G)
        def _(g):
            v = normed(1, 3, g) + s.u_seg[1, group(g)].astype(F32)
            act, slope = gelu_pair(v)
            o = jnp.where(real_rows(c.cs), act, 0.0).astype(BF16)
            s.out_seg[group(g)] = o
            e = s.g_seg[group(g)].astype(F32) * slope
            s.e3[group(g)] = e
            back_out(1, 3, g, e)
            o32 = o.astype(F32)
            place = lax.broadcasted_iota(jnp.int32, (GM, R, c.cs), 1)
            for n in range(c.images):
                here = (place >= n * SIDE * SIDE) & (place < (n + 1) * SIDE * SIDE)
                mean = jnp.sum(jnp.where(here, o32, 0.0), axis=1, keepdims=True) / float(SIDE * SIDE)
                for m in range(GM):
                    s.pool[(g * GM + m) * c.images + n] = mean[m]

        out_copy = pltpu.make_async_copy(s.out_seg, bo_out, s.out_r.at[0])
        out_copy.start()
        tail.append(out_copy.wait)

        banks = ND * c.bank
        which = lax.broadcasted_iota(jnp.int32, (banks, c.cs), 0)
        term = jnp.zeros((banks, c.cs), F32)
        for n in range(M * c.images):
            ids = jnp.concatenate([ids_ref[n : n + 1, :]] * (c.cs // LANES), axis=1)
            term = term + jnp.where(which == ids, s.pool[n], 0.0)
        s.bank_put[...] = term.reshape(ND, c.bank, c.cs)

        @pl.loop(1, ND)
        def _(i):
            d = dp_peer(i)
            remote(s.bank_put.at[d], s.bank_got.at[me_d], s.bank_s.at[0], s.bank_r.at[0], me_p, d).start()

        tail.append(lambda: take_send(s.bank_got.at[pl.ds(0, ND - 1)], s.bank_s.at[0], s.bank_r.at[0]))

        s.bank_got[me_d] = s.bank_put[me_d]

        def all_rows(ref):
            return ref[...].reshape(M * R, ref.shape[-1])

        def all_seg(ref):
            return jnp.concatenate([ref[j].reshape(M * R, LANES) for j in range(NP)], axis=1)

        def grad_q(k):
            h = all_seg(s.h2.at[k])
            s.gp[2 * k + 1] = dot_tn(all_rows(s.da3.at[k]), h).astype(BF16)

        def grad_p0():
            d = s.da1[0, shard(0, me_p)].reshape(M * R, LANES)
            s.g0[...] = dot_tn(all_rows(s.u_all), d).astype(BF16)

        def grad_p(k):
            d = all_seg(s.da1.at[k])
            s.gp[2 * k] = dot_tn(all_rows(s.u_seg.at[k]), d).astype(BF16)

        def grad_w(k):
            h = all_seg(s.h1.at[k])
            for t0 in range(0, TAPS, 2):
                taps = [t for t in (t0, t0 + 1) if t < TAPS]
                d = s.dcol[k, :, :, t0 * LANES : (t0 + len(taps)) * LANES].reshape(M * R, len(taps) * LANES)
                v = dot_tn(h, d)
                for n, t in enumerate(taps):
                    s.gw[k, t * c.mid : (t + 1) * c.mid, :] = v[:, n * LANES : (n + 1) * LANES].astype(BF16)

        def part(base, n):
            return pl.ds(pl.multiple_of(base, 16), n)

        inner = (me_z == 1) | (me_z == 2)
        z_side = lax.div(me_z, 2)
        outer_dev = 2 * (3 * z_side) + me_c
        inner_dev = 2 * (1 + z_side) + me_c
        across_dev = 2 * (2 - z_side) + me_c

        def job_own(job):
            kind, k, n, base, slot = c.jobs[job]
            ref = s.g0 if kind == "0" else s.gw.at[k] if kind == "w" else s.gp.at[2 * k + (kind == "q")]
            return ref, base

        def job_ref(name, job):
            kind, k, n, base, slot = c.jobs[job]
            return getattr(s, name + ("p" if kind in "pq" else kind)).at[slot]

        def job_core(job):
            own, base = job_own(job)
            n = c.jobs[job][2]
            view = own.at[part(base + (1 - me_c) * n, n)]
            remote(view, job_ref("ja", job), s.gs.at[job, 0], s.gr.at[job, 0], me_p, sib).start()

        def job_in(job):
            own, base = job_own(job)
            n = c.jobs[job][2]
            got, tot = job_ref("ja", job), job_ref("jb", job)
            take_recv(got, s.gs.at[job, 0], s.gr.at[job, 0])
            tot[...] = (got[...].astype(F32) + own[part(base + me_c * n, n), :].astype(F32)).astype(BF16)
            @pl.when(jnp.logical_not(inner))
            def _():
                remote(tot, job_ref("jc", job), s.gs.at[job, 1], s.gr.at[job, 1], me_p, inner_dev).start()

        def job_halve(job):
            n = c.jobs[job][2]
            got, tot, half = job_ref("jc", job), job_ref("jb", job), job_ref("jd", job)

            @pl.when(inner)
            def _():
                take_recv(got, s.gs.at[job, 1], s.gr.at[job, 1])
                tot[...] = (got[...].astype(F32) + tot[...].astype(F32)).astype(BF16)
                view = tot.at[part((1 - z_side) * (n // 2), n // 2)]
                remote(view, half, s.gs.at[job, 2], s.gr.at[job, 2], me_p, across_dev).start()

        def job_sum(job):
            n = c.jobs[job][2]
            tot, half, fin = job_ref("jb", job), job_ref("jd", job), job_ref("je", job)
            mine = part(z_side * (n // 2), n // 2)

            @pl.when(inner)
            def _():
                take_recv(half, s.gs.at[job, 2], s.gr.at[job, 2])
                fin[mine, :] = (half[...].astype(F32) + tot[mine, :].astype(F32)).astype(BF16)
                view = fin.at[mine]
                remote(view, view, s.gs.at[job, 3], s.gr.at[job, 3], me_p, across_dev).start()
                remote(view, view, s.gs.at[job, 4], s.gr.at[job, 3], me_p, outer_dev).start()

        def job_out(job):
            n = c.jobs[job][2]
            fin = job_ref("je", job)
            view = fin.at[part((1 - z_side) * (n // 2), n // 2)]

            @pl.when(inner)
            def _():
                take_recv(view, s.gs.at[job, 3], s.gr.at[job, 3])
                remote(view, view, s.gs.at[job, 5], s.gr.at[job, 4], me_p, outer_dev).start()

        def job_place(job, p, core):
            kind, k, n, base, slot = c.jobs[job]
            if kind == "0":
                return s.p0_out.at[shard(0, p), part(base + core * n, n)]
            if kind == "w":
                return s.w_out.at[lax.div(p, 2) if k == 0 else 1 - lax.div(p, 2), part(base + core * n, n)]
            return s.p_out.at[part(p * 2 * n + core * n, n)]

        def job_home(job, p):
            kind, k = c.jobs[job][:2]
            return 2 * k + lax.rem(p, 2) if kind == "w" else jnp.int32(2 * k + (kind == "q"))

        def job_holds(job):
            kind, k = c.jobs[job][:2]
            return me_y == k if kind == "w" else me_p == 2 * k + (kind == "q")

        def job_plane(job):
            n = c.jobs[job][2]
            fin = job_ref("je", job)

            @pl.when(jnp.logical_not(inner))
            def _():
                for step in (3, 4):
                    take_recv(fin.at[0 : n // 2], s.gs.at[job, step], s.gr.at[job, step])

            home = job_home(job, me_p)

            @pl.when(me_p != home)
            def _():
                remote(fin, job_place(job, me_p, me_c), s.gs.at[job, 6], s.gr.at[job, 5], home, me_d).start()

            @pl.when(me_p == home)
            def _():
                pltpu.make_async_copy(fin, job_place(job, me_p, me_c), s.own_s.at[job]).start()

        def job_many(job, count):
            kind, k, n, base, slot = c.jobs[job]
            if kind == "0":
                return s.p0_out.at[pl.ds(0, count), pl.ds(0, n)]
            return s.w_out.at[pl.ds(0, count), pl.ds(0, n)] if kind == "w" else s.p_out.at[pl.ds(0, n * count)]

        def job_share(job):
            fin = job_ref("je", job)
            from_pipes = [0, 2] if c.jobs[job][0] == "w" else [0, 1, 2, 3]

            @pl.when(job_holds(job))
            def _():
                pltpu.make_async_copy(fin, job_place(job, me_p, me_c), s.own_s.at[job]).wait()
                take_recv(job_many(job, len(from_pipes) - 1), s.gs.at[job, 6], s.gr.at[job, 5])
                for i in from_pipes:
                    view = job_place(job, pipe_peer(i), me_c)
                    remote(view, view, s.fin_s.at[job], s.fin_r.at[job], me_p, sib).start()

        def job_end(job):
            got, half, fin = job_ref("ja", job), job_ref("jd", job), job_ref("je", job)
            take_send(got, s.gs.at[job, 0], s.gr.at[job, 0])

            @pl.when(inner)
            def _():
                for step in (2, 3, 4, 5):
                    take_send(half, s.gs.at[job, step], s.gr.at[job, 2])

            @pl.when(jnp.logical_not(inner))
            def _():
                take_send(got, s.gs.at[job, 1], s.gr.at[job, 1])

            @pl.when(me_p != job_home(job, me_p))
            def _():
                take_send(fin, s.gs.at[job, 6], s.gr.at[job, 5])

            @pl.when(job_holds(job))
            def _():
                view = job_many(job, 2 if c.jobs[job][0] == "w" else NP)
                take_recv(view, s.fin_s.at[job], s.fin_r.at[job])
                take_send(view, s.fin_s.at[job], s.fin_r.at[job])

        def job_store(job, act):
            kind, k, n, base, slot = c.jobs[job]
            rows = pl.ds(base, 2 * n)
            if kind == "0":
                parts = [(s.p0_out.at[j, rows], gp_out.at[rows, pl.ds(j * LANES, LANES)]) for j in range(NP)]
            elif kind == "w":
                parts = [(s.w_out.at[h, rows], gw_out.at[rows, pl.ds(h * LANES, LANES)]) for h in range(2)]
            else:
                parts = [(s.p_out, gp_out)]

            @pl.when(job_holds(job))
            def _():
                for i, (src, dst) in enumerate(parts):
                    getattr(pltpu.make_async_copy(src, dst, s.store.at[job, i]), act)()

        steps = (job_core, job_in, job_halve, job_sum, job_out, job_plane, job_share)
        next_step = dict.fromkeys(c.jobs, 0)

        def advance(*jobs):
            if c.deep:
                for job in jobs:
                    if next_step[job] < len(steps):
                        steps[next_step[job]](job)
                        next_step[job] += 1

        def point(k, n):
            advance(*POINTS[(1 - k) * 6 + n])

        for k in (1, 0):
            side = 2 * (1 - k)

            @pl.loop(0, G)
            def _(g):
                grad = back_in(k, 3, g, s.e3[group(g)])
                s.da3[k, group(g)] = grad
                rs_send(2 + (1 - k), g, k, dot(grad.reshape(flat, c.cs), s.pq[2 * k + 1]))

            grad_q(k)
            if k == 1:

                @on_pipes(0)
                def _():
                    for i in range(1, NP):
                        proj_send(i).start()

            point(k, 0)

            @pl.loop(0, G)
            def _(g):
                up = rs_take(2 + (1 - k), g, k) * s.d2[k, group(g)]
                s.t1[group(g)] = up
                back_out(k, 2, g, up)
            if k == 0:
                pass_two(0)
            point(k, 1)

            @pl.loop(0, G)
            def _(g):
                rs_send(5 - k, g, k, conv_back(k, g, back_in(k, 2, g, s.t1[group(g)])))

            grad_w(k)
            point(k, 2)

            @pl.loop(0, G)
            def _(g):
                up = rs_take(5 - k, g, k) * s.d1[k, group(g)]
                s.t1[group(g)] = up
                back_out(k, 1, g, up)
            point(k, 3)

            @pl.loop(0, G)
            def _(g):
                mine = shard(k, me_p)
                s.da1[k, mine, group(g)] = back_in(k, 1, g, s.t1[group(g)])
                ag_send(5 + side, g, s.da1.at[k], mine)
            if k == 0:
                grad_p0()
            point(k, 4)

            if k == 0:
                need(0)

            @pl.loop(0, G)
            def _(g):
                d = dot_nt(ag_take(5 + side, g, s.da1.at[k]), s.pq[2 * k])
                d = d.reshape(GM, R, c.cs) + s.e3[group(g)]
                if k == 1:
                    e = d * s.d3[0, group(g)]
                    s.e3[group(g)] = e
                    back_out(0, 3, g, e)
                else:
                    s.in_seg[group(g)] = d.astype(BF16)

            if k == 1 or not c.deep:
                grad_p(k)
            if k == 1:
                pass_one(0)
            point(k, 5)

        in_copy = pltpu.make_async_copy(s.in_seg, ig_out, s.out_r.at[1])
        in_copy.start()
        tail.append(in_copy.wait)
        view = s.norm_sum.at[me_p]
        for i in range(1, NP):
            remote(view, view, s.ns_s.at[0], s.ns_r.at[0], pipe_peer(i), me_d).start()
        tail.append(lambda: take_send(s.norm_sum.at[pl.ds(0, NP - 1)], s.ns_s.at[0], s.ns_r.at[0]))

        while c.deep and min(next_step.values()) < len(steps) - 1:
            advance(*[job for job in LAST if next_step[job] < len(steps) - 1])

        take_recv(s.bank_got.at[pl.ds(0, ND - 1)], s.bank_s.at[0], s.bank_r.at[0])
        tot = s.bank_got[0]
        for d in range(1, ND):
            tot = tot + s.bank_got[d]
        mb_out[...] = tot
        take_recv(s.norm_sum.at[pl.ds(0, NP - 1)], s.ns_s.at[0], s.ns_r.at[0])
        per = c.mid // LANES
        wide = c.cs // LANES
        each = (2 * per + c.ch // LANES) // NP
        for k in range(2):
            for n in range(each):
                q = me_p * each + n
                in_one = q < per
                in_two = (q >= per) & (q < 2 * per)
                sh = jnp.where(in_one, q, q - per)
                half = lax.rem(sh + k, 2)
                small = 2 * half + lax.div(sh, 2)
                far = q - 2 * per
                p = jnp.where(q < 2 * per, small, lax.div(far, wide))
                chunk = jnp.where(in_one, 0, jnp.where(in_two, 1, 2 + lax.rem(far, wide)))
                ns_out[n, 2 * k : 2 * k + 2, :] = s.norm_sum[p, chunk, 2 * k : 2 * k + 2, :]

        def drain():
            front_send().wait_send()
            for i in range(1, NP):
                proj_send(i).wait_send()
            for n in range(6):
                end_part(n)

            @pl.loop(0, G)
            def _(g):
                for wait in [*due.values(), *owed.values()]:
                    wait(g)

                @pl.when(me_p == 0)
                def _():
                    take_send(s.put.at[0, pl.ds(0, NP - 1), group(g)], s.rs_s.at[0, g], s.rs_r.at[0, g])
            for wait in tail:
                wait()

        drain()
        advance(*c.jobs)
        if c.deep:
            for job in c.jobs:
                job_end(job)
                job_store(job, "start")
            for job in c.jobs:
                job_store(job, "wait")

    work()

    if not c.deep:
        copies = [
            pltpu.make_async_copy(s.gp, gp_out, s.out_r.at[2]),
            pltpu.make_async_copy(s.gw, gw_out, s.out_r.at[3]),
        ]
        for copy in copies:
            copy.start()
        for copy in copies:
            copy.wait()


def on_device(mesh, block_input, proj_weight, spatial_weight, norm_gain, norm_shift, output_grad, image_ids):
    bank = 8
    c = Sizes(mesh, block_input, proj_weight, spatial_weight, bank)
    extra = ((0, 0), (0, c.pad - c.rows), (0, 0))
    u = jnp.pad(block_input, extra)
    go = lax.dynamic_slice_in_dim(output_grad, lax.axis_index("pipe") * c.cs, c.cs, axis=2)
    go = jnp.pad(go, extra)
    sw = spatial_weight.reshape(TAPS, c.mid, spatial_weight.shape[2])
    ids = jnp.broadcast_to(image_ids.reshape(-1, 1), (image_ids.size, LANES))
    items = scratch_list(c)
    names = [n for n, _ in items]
    anyspec = pl.BlockSpec(memory_space=pl.ANY)
    vspec = pl.BlockSpec(memory_space=pltpu.VMEM)
    if c.deep:
        gp_shape, gw_shape = (c.ch, c.mid), (TAPS * c.mid, 2 * LANES)
    else:
        gp_shape, gw_shape = (c.pipes, c.cs, c.mid), (2, TAPS * c.mid, LANES)
    each = (2 * c.mid + c.ch) // LANES // c.pipes
    outs = pl.pallas_call(
        functools.partial(body, c, names),
        out_shape=(
            jax.ShapeDtypeStruct((c.micro, c.pad, c.cs), BF16),
            jax.ShapeDtypeStruct((c.micro, c.pad, c.cs), BF16),
            jax.ShapeDtypeStruct(gp_shape, BF16),
            jax.ShapeDtypeStruct(gw_shape, BF16),
            jax.ShapeDtypeStruct((each, 4, LANES), F32),
            jax.ShapeDtypeStruct((bank, c.cs), F32),
        ),
        in_specs=[anyspec] * 4 + [vspec] * 3,
        out_specs=(anyspec, anyspec, anyspec, anyspec, vspec, vspec),
        scratch_shapes=[v for _, v in items],
        compiler_params=pltpu.CompilerParams(collective_id=0, has_side_effects=True, vmem_limit_bytes=60 << 20),
    )(u, go, proj_weight[0], sw, norm_gain, norm_shift, ids)
    bo, ig, gp, gw, ns, mb = outs
    if not c.deep:
        gp = lax.psum(gp.astype(F32), "dp")
        gw = lax.psum(gw.astype(F32), "dp")
        gp = lax.all_to_all(gp, "pipe", 0, 0, tiled=True).reshape(c.ch, c.mid)
        gw = lax.all_gather(gw, "pipe")
        me = lax.axis_index("pipe")
        y, x = me // 2, me % 2
        near = lax.dynamic_index_in_dim(gw, me, 0, keepdims=False)
        far = lax.dynamic_index_in_dim(gw, 2 * (1 - y) + x, 0, keepdims=False)
        gw = jnp.concatenate(
            [lax.dynamic_index_in_dim(near, y, 0, keepdims=False), lax.dynamic_index_in_dim(far, y, 0, keepdims=False)],
            axis=1,
        )
    ns = jnp.transpose(ns.reshape(each, 2, 2, LANES), (2, 1, 0, 3)).reshape(2, 2, each * LANES)
    return (
        bo[:, : c.rows],
        ig[:, : c.rows],
        gp.astype(F32)[None],
        gw.astype(F32)[None],
        ns[0],
        ns[1],
        mb,
    )


def solution(mesh):
    return jax.shard_map(
        functools.partial(on_device, mesh),
        mesh=mesh,
        in_specs=(
            P(None, "dp", None),
            P("pipe", None, None),
            P("pipe", None, None),
            P(),
            P(),
            P(None, "dp", None),
            P(None, "dp"),
        ),
        out_specs=(
            P(None, "dp", "pipe"),
            P(None, "dp", "pipe"),
            P("pipe", None, None),
            P("pipe", None, None),
            P(None, "pipe"),
            P(None, "pipe"),
            P("dp", "pipe"),
        ),
        check_vma=False,
    )
```

```python
import functools
import math
import types

import jax
import jax.numpy as jnp
from jax import lax
from jax.experimental import pallas as pl
from jax.experimental.pallas import tpu as pltpu
from jax.sharding import PartitionSpec as P

SIDE = 7
TAPS = 9
EPS = 1e-05
LANES = 128
GROUPS = 4
W_PIECES = 3
P_PIECES = 2
POINTS = (
    (0,),
    (0,),
    (0, 1, 2, 3),
    (0, 1, 2),
    (0, 1),
    (1, 2, 3, 4),
    (0, 1, 2, 3, 4, 5),
    (2, 3, 4, 5),
    (6, 7, 8, 1, 2, 3, 4, 5),
    (6, 7, 8, 5, 4),
    (9, 10, 6, 5),
    (9, 10, 6, 7, 8, 5, 3, 4),
)
LAST = (6, 7, 8, 9, 10, 5, 4, 3, 0, 1, 2)
MESH = pl.DeviceIdType.MESH
F32 = jnp.float32
BF16 = jnp.bfloat16


def gelu_pair(v):
    c0 = math.sqrt(2.0 / math.pi)
    c1 = 0.044715
    sq = v * v
    t = jnp.tanh(c0 * v * (1.0 + c1 * sq))
    half = 0.5 + 0.5 * t
    slope = half + (0.5 * c0) * v * (1.0 - t * t) * (1.0 + (3.0 * c1) * sq)
    return v * half, slope


def dot(a, b):
    return jnp.dot(a, b, preferred_element_type=F32)


def dot_nt(a, b):
    return lax.dot_general(a, b, (((1,), (1,)), ((), ())), preferred_element_type=F32)


def dot_tn(a, b):
    return lax.dot_general(a, b, (((0,), (0,)), ((), ())), preferred_element_type=F32)


class Sizes:
    def __init__(self, mesh, block_input, proj, spatial, bank_rows):
        self.pipes = mesh.shape["pipe"]
        self.dps = mesh.shape["dp"]
        self.micro = block_input.shape[0]
        self.rows = block_input.shape[1]
        self.pad = -(-self.rows // 16) * 16
        self.ch = block_input.shape[2]
        self.mid = proj.shape[2]
        self.images = self.rows // (SIDE * SIDE)
        self.cs = self.ch // self.pipes
        self.msd = self.mid // self.pipes
        self.groups = GROUPS
        self.gm = self.micro // self.groups
        self.zs = self.dps // 2
        self.total = self.rows * self.dps
        self.bank = bank_rows
        self.deep = self.zs == 4
        self.jobs = {}
        taps = TAPS // W_PIECES
        for k in (1, 0):
            self.jobs[len(self.jobs)] = ("q", k, self.cs // 2, 0, 1 - k)
            for i in range(W_PIECES):
                self.jobs[len(self.jobs)] = ("w", k, taps * self.mid // 2, i * taps * self.mid, (1 - k) * W_PIECES + i)
            if k == 1:
                self.jobs[len(self.jobs)] = ("p", k, self.cs // 2, 0, 2)
        for i in range(P_PIECES):
            self.jobs[len(self.jobs)] = ("0", 0, self.ch // P_PIECES // 2, i * self.ch // P_PIECES, i)


def scratch_list(c):
    full = (c.micro, c.pad)
    seg = (c.pipes, c.micro, c.pad, LANES)
    items = [
        ("u_all", pltpu.VMEM(full + (c.ch,), BF16)),
        ("u_seg", pltpu.VMEM((2,) + full + (c.cs,), BF16)),
        ("g_seg", pltpu.VMEM(full + (c.cs,), BF16)),
        ("p_own", pltpu.VMEM((c.ch, c.mid), BF16)),
        ("pq", pltpu.VMEM((c.pipes, c.cs, c.mid), BF16)),
        ("wf", pltpu.VMEM((2, TAPS, c.mid, LANES), BF16)),
        ("sw", pltpu.VMEM((2, TAPS, c.mid, LANES), BF16)),
        ("mask", pltpu.VMEM((TAPS, c.pad, LANES), F32)),
        ("z1", pltpu.VMEM((2,) + full + (LANES,), F32)),
        ("d1", pltpu.VMEM((2,) + full + (LANES,), F32)),
        ("z2", pltpu.VMEM((2,) + full + (LANES,), F32)),
        ("d2", pltpu.VMEM((2,) + full + (LANES,), F32)),
        ("z3", pltpu.VMEM((2,) + full + (c.cs,), F32)),
        ("d3", pltpu.VMEM((2,) + full + (c.cs,), F32)),
        ("e3", pltpu.VMEM(full + (c.cs,), F32)),
        ("t1", pltpu.VMEM(full + (LANES,), F32)),
        ("gr1", pltpu.VMEM((2, c.micro, 1, LANES), F32)),
        ("gr2", pltpu.VMEM((2, c.micro, 1, LANES), F32)),
        ("gr3", pltpu.VMEM((2, c.micro, 1, c.cs), F32)),
        ("h1", pltpu.VMEM((2,) + seg, BF16)),
        ("h2", pltpu.VMEM((2,) + seg, BF16)),
        ("da3", pltpu.VMEM((2,) + full + (c.cs,), BF16)),
        ("dcol", pltpu.VMEM((2,) + full + (TAPS * LANES,), BF16)),
        ("da1", pltpu.VMEM((2,) + seg, BF16)),
        ("first", pltpu.VMEM(full + (LANES,), BF16)),
        ("put", pltpu.VMEM((6,) + seg, BF16)),
        ("got", pltpu.VMEM((6,) + seg, BF16)),
        ("out_seg", pltpu.VMEM(full + (c.cs,), BF16)),
        ("in_seg", pltpu.VMEM(full + (c.cs,), BF16)),
        ("ar_small", pltpu.VMEM((8, c.dps, c.micro, 2, LANES), F32)),
        ("ar_wide", pltpu.VMEM((4, c.dps, c.micro, 2, c.cs), F32)),
        ("pool", pltpu.VMEM((c.micro * c.images, 1, c.cs), F32)),
        ("bank_put", pltpu.VMEM((c.dps, c.bank, c.cs), F32)),
        ("bank_got", pltpu.VMEM((c.dps, c.bank, c.cs), F32)),
        ("norm_sum", pltpu.VMEM((c.pipes, 6, 8, LANES), F32)),
        ("gp", pltpu.VMEM((c.pipes, c.cs, c.mid), BF16)),
        ("g0", pltpu.VMEM((c.ch, LANES), BF16)),
        ("gw", pltpu.VMEM((2, TAPS * c.mid, LANES), BF16)),
        ("ar_s", pltpu.SemaphoreType.DMA((12, c.groups))),
        ("ar_r", pltpu.SemaphoreType.DMA((12, c.groups))),
        ("ag_s", pltpu.SemaphoreType.DMA((8, c.groups))),
        ("ag_r", pltpu.SemaphoreType.DMA((8, c.groups))),
        ("rs_s", pltpu.SemaphoreType.DMA((6, c.groups))),
        ("rs_r", pltpu.SemaphoreType.DMA((6, c.groups))),
        ("w_s", pltpu.SemaphoreType.DMA((2, c.pipes))),
        ("pass_s", pltpu.SemaphoreType.DMA((6, 3))),
        ("w_r", pltpu.SemaphoreType.DMA((6,))),
        ("w_z", pltpu.SemaphoreType.DMA((6,))),
        ("w_q", pltpu.SemaphoreType.DMA((6,))),
        ("bank_s", pltpu.SemaphoreType.DMA((1,))),
        ("bank_r", pltpu.SemaphoreType.DMA((1,))),
        ("ns_s", pltpu.SemaphoreType.DMA((1,))),
        ("ns_r", pltpu.SemaphoreType.DMA((1,))),
        ("in_r", pltpu.SemaphoreType.DMA((6,))),
        ("out_r", pltpu.SemaphoreType.DMA((4 + c.pipes,))),
    ]
    if c.deep:
        for name, width in (("p", c.mid), ("w", LANES), ("0", LANES)):
            of = [job for job in c.jobs.values() if job[0] in {"p": "pq"}.get(name, name)]
            lead, n = len(of), of[0][2]
            items += [(key + name, pltpu.VMEM((lead, n // (1 + (key == "jd")), width), BF16)) for key in ("ja", "jb", "jc", "jd", "je")]
        count = len(c.jobs)
        items += [
            ("p_out", pltpu.VMEM((c.ch, c.mid), BF16)),
            ("p0_out", pltpu.VMEM((c.pipes, c.ch, LANES), BF16)),
            ("w_out", pltpu.VMEM((2, TAPS * c.mid, LANES), BF16)),
            ("gs", pltpu.SemaphoreType.DMA((count, 7))),
            ("gr", pltpu.SemaphoreType.DMA((count, 6))),
            ("own_s", pltpu.SemaphoreType.DMA((count,))),
            ("store", pltpu.SemaphoreType.DMA((count, c.pipes))),
            ("fin_s", pltpu.SemaphoreType.DMA((count,))),
            ("fin_r", pltpu.SemaphoreType.DMA((count,))),
        ]
    return items


def body(c, names, *refs):
    (u_hbm, go_hbm, pw_hbm, sw_hbm, gain_ref, shift_ref, ids_ref) = refs[:7]
    (bo_out, ig_out, gp_out, gw_out, ns_out, mb_out) = refs[7:13]
    s = types.SimpleNamespace(**dict(zip(names, refs[13:])))
    me_p = lax.axis_index("pipe")
    me_d = lax.axis_index("dp")
    me_x = lax.rem(me_p, 2)
    me_y = lax.div(me_p, 2)
    NP, ND, M, GM, G, R = c.pipes, c.dps, c.micro, c.gm, c.groups, c.pad
    flat = GM * R
    count = float(c.total)

    def shard(k, p):
        half = lax.div(p, 2)
        return 2 * lax.rem(p, 2) + (half if k == 0 else 1 - half)

    def pipe_peer(i):
        return lax.rem(me_p + i, NP)

    def dp_peer(i):
        return lax.rem(me_d + i, ND)

    def remote(src, dst, ss, rs, p, d):
        return pltpu.make_async_remote_copy(
            src_ref=src, dst_ref=dst, send_sem=ss, recv_sem=rs, device_id=(p, d), device_id_type=MESH
        )

    def take_recv(view, ss, rs):
        remote(view, view, ss, rs, me_p, me_d).wait_recv()

    def take_send(view, ss, rs):
        remote(view, view, ss, rs, me_p, me_d).wait_send()

    def group(g):
        return pl.ds(g * GM, GM)

    owed, due = {}, {}

    lane0 = pl.multiple_of(me_p * c.cs, LANES)
    seg_cols = pl.ds(lane0, c.cs)
    load_u = pltpu.make_async_copy(u_hbm.at[:, :, seg_cols], s.u_seg.at[0], s.in_r.at[0])
    load_g = pltpu.make_async_copy(go_hbm, s.g_seg, s.in_r.at[1])
    load_all = pltpu.make_async_copy(u_hbm, s.u_all, s.in_r.at[2])
    load_p = pltpu.make_async_copy(pw_hbm, s.p_own, s.in_r.at[3])
    load_w = [
        pltpu.make_async_copy(sw_hbm.at[:, :, pl.ds(h * LANES, LANES)], s.sw.at[h], s.in_r.at[4 + h]) for h in range(2)
    ]
    load_all.start()

    @pl.when(me_p == 0)
    def _():
        load_p.start()

    for load in load_w:
        load.start()
    load_u.start()
    load_g.start()

    barrier = pltpu.get_barrier_semaphore()
    for i in range(1, NP):
        pl.semaphore_signal(barrier, inc=1, device_id=(pipe_peer(i), me_d), device_id_type=MESH)

    @pl.loop(1, ND)
    def _(i):
        pl.semaphore_signal(barrier, inc=1, device_id=(me_p, dp_peer(i)), device_id_type=MESH)

    row = lax.broadcasted_iota(jnp.int32, (R, LANES), 0)
    image = jnp.zeros_like(row)
    for n in range(1, c.images):
        image = image + (row >= n * SIDE * SIDE).astype(jnp.int32)
    pixel = row - image * (SIDE * SIDE)
    up = jnp.zeros_like(row)
    for n in range(1, SIDE):
        up = up + (pixel >= n * SIDE).astype(jnp.int32)
    across = pixel - up * SIDE
    for t in range(TAPS):
        i, j = t // 3 - 1, t % 3 - 1
        ok = (up + i >= 0) & (up + i < SIDE) & (across + j >= 0) & (across + j < SIDE) & (row < c.rows)
        s.mask[t] = ok.astype(F32)
    s.norm_sum[...] = jnp.zeros_like(s.norm_sum)

    pl.semaphore_wait(barrier, NP - 1 + ND - 1)

    me_c = lax.rem(me_d, 2)
    me_z = lax.div(me_d, 2)
    sib = me_d + 1 - 2 * me_c

    def link_peer(i):
        flip = me_p + 1 - 2 * me_x
        return (None, flip, lax.rem(me_p + 2, NP), lax.rem(flip + 2, NP))[i]

    def on_pipes(*pipes):
        here = me_p == pipes[0]
        for p in pipes[1:]:
            here = here | (me_p == p)
        return pl.when(here)

    me_l = lax.rem(me_z, 2)
    low = 2 * (me_z + 1 - 2 * me_l) + me_c

    def quarter(part, core, z):
        if part < 4:
            return s.pq.at[part, pl.ds(pl.multiple_of((2 * core + z) * (c.cs // 4), 16), c.cs // 4)]
        return s.wf.at[part - 4, :, pl.ds(pl.multiple_of((2 * core + z) * (c.mid // 4), 16), c.mid // 4)]

    def whole_part(part, core):
        if part < 4:
            return s.pq.at[part] if core is None else s.pq.at[part, pl.ds(pl.multiple_of(core * (c.cs // 2), 16), c.cs // 2)]
        rows = pl.ds(0, c.mid) if core is None else pl.ds(pl.multiple_of(core * (c.mid // 2), 16), c.mid // 2)
        return s.wf.at[part - 4, :, rows]

    def here_already(part):
        return me_p == part if part < 4 else me_y == part - 4

    def proj_send(i):
        p = link_peer(i)
        n = c.cs // 4
        base = (2 * me_c + me_l) * n
        src = pw_hbm.at[pl.ds(pl.multiple_of(p * c.cs + base, 16), n)]
        dst = s.pq.at[me_p, pl.ds(pl.multiple_of(base, 16), n)]
        return remote(src, dst, s.w_s.at[0, i], s.w_r.at[me_p], p, me_d)

    def front_send():
        rows = pl.ds(pl.multiple_of((2 * me_c + me_l) * (c.mid // 4), 16), c.mid // 4)
        return remote(s.sw.at[1, :, rows], s.wf.at[me_y, :, rows], s.w_s.at[1, 0], s.w_r.at[4 + me_y], link_peer(2), me_d)

    def pass_copies(part):
        near, far = quarter(part, me_c, me_l), quarter(part, me_c, 1 - me_l)
        return (
            remote(near, near, s.pass_s.at[part, 0], s.w_z.at[part], me_p, low),
            remote(near, near, s.pass_s.at[part, 1], s.w_q.at[part], me_p, sib),
            remote(far, far, s.pass_s.at[part, 2], s.w_q.at[part], me_p, sib),
        )

    def pass_one(*parts):
        for part in parts:

            @pl.when(jnp.logical_not(here_already(part)))
            def _():
                take_recv(quarter(part, me_c, me_l), s.pass_s.at[part, 0], s.w_r.at[part])
                for copy in pass_copies(part)[:2]:
                    copy.start()

    def pass_two(*parts):
        for part in parts:

            @pl.when(jnp.logical_not(here_already(part)))
            def _():
                take_recv(quarter(part, me_c, 1 - me_l), s.pass_s.at[part, 0], s.w_z.at[part])
                pass_copies(part)[2].start()

    def need(*parts):
        for part in parts:

            @pl.when(jnp.logical_not(here_already(part)))
            def _():
                take_recv(whole_part(part, 1 - me_c), s.pass_s.at[part, 0], s.w_q.at[part])

            @pl.when(here_already(part))
            def _():
                pltpu.make_async_copy(whole_part(part, None), whole_part(part, None), s.w_r.at[part]).wait()

    def end_part(part):
        @pl.when(jnp.logical_not(here_already(part)))
        def _():
            for copy in pass_copies(part):
                copy.wait_send()

    for load in load_w:
        load.wait()

    front_send().start()

    @on_pipes(2)
    def _():
        for i in range(1, NP):
            proj_send(i).start()

    own_rows = pl.ds(pl.multiple_of(me_p * c.cs, 16), c.cs)
    pltpu.make_async_copy(pw_hbm.at[own_rows], s.pq.at[me_p], s.w_r.at[me_p]).start()
    pltpu.make_async_copy(s.sw.at[0], s.wf.at[me_y], s.w_r.at[4 + me_y]).start()

    def note(kind, idx, view, ss, rs):
        owed[kind, idx] = lambda g: take_send(view(g), ss.at[idx, g], rs.at[idx, g])
        due[kind, idx] = lambda g: take_recv(view(g), ss.at[idx, g], rs.at[idx, g])

    def grab(kind, idx, g):
        due.pop((kind, idx))(g)

    def ar_ref(idx):
        return s.ar_small.at[idx] if idx < 8 else s.ar_wide.at[idx - 8]

    def ar_send(idx, g, first, second):
        buf = ar_ref(idx)
        buf[me_d, group(g), 0:1, :] = first
        buf[me_d, group(g), 1:2, :] = second

        @pl.loop(1, ND)
        def _(i):
            view = buf.at[me_d, group(g)]
            remote(view, view, s.ar_s.at[idx, g], s.ar_r.at[idx, g], me_p, me_d ^ (ND - i)).start()

        note("ar", idx, lambda g: ar_ref(idx).at[pl.ds(0, ND - 1), group(g)], s.ar_s, s.ar_r)

    def ar_take(idx, g):
        buf = ar_ref(idx)
        grab("ar", idx, g)
        tot = buf[0, group(g)]
        for d in range(1, ND):
            tot = tot + buf[d, group(g)]
        return tot[:, 0:1, :], tot[:, 1:2, :]

    def ag_send(idx, g, buf, slot):
        view = buf.at[slot, group(g)]
        for i in (3, 1, 2):
            remote(view, view, s.ag_s.at[idx, g], s.ag_r.at[idx, g], link_peer(i), me_d).start()
        note("ag", idx, lambda g: s.h1.at[0, pl.ds(0, NP - 1), group(g)], s.ag_s, s.ag_r)

    def ag_take(idx, g, buf):
        grab("ag", idx, g)
        return jnp.concatenate([buf[j, group(g)].reshape(flat, LANES) for j in range(NP)], axis=1)

    def rs_send(idx, g, k, partial):
        for j in range(NP):
            s.put[idx, j, group(g)] = partial[:, j * LANES : (j + 1) * LANES].reshape(GM, R, LANES).astype(BF16)
        for i in (3, 1, 2):
            p = link_peer(i)
            remote(
                s.put.at[idx, shard(k, p), group(g)],
                s.got.at[idx, me_p, group(g)],
                s.rs_s.at[idx, g],
                s.rs_r.at[idx, g],
                p,
                me_d,
            ).start()
        note("rs", idx, lambda g: s.got.at[idx, pl.ds(0, NP - 1), group(g)], s.rs_s, s.rs_r)

    def rs_take(idx, g, k):
        grab("rs", idx, g)
        tot = s.put[idx, shard(k, me_p), group(g)].astype(F32)
        for i in range(1, NP):
            tot = tot + s.got[idx, pipe_peer(i), group(g)].astype(F32)
        return tot

    def shard_cols(base, k):
        return pl.ds(pl.multiple_of(base + shard(k, me_p) * LANES, LANES), LANES)

    def norm_cols(which, k):
        if which == 1:
            return shard_cols(0, k)
        if which == 2:
            return shard_cols(c.mid, k)
        return pl.ds(pl.multiple_of(2 * c.mid + me_p * c.cs, LANES), c.cs)

    def real_rows(width):
        return lax.broadcasted_iota(jnp.int32, (GM, R, width), 1) < c.rows

    ZD = {1: (s.z1, s.d1, s.gr1), 2: (s.z2, s.d2, s.gr2), 3: (s.z3, s.d3, s.gr3)}
    FWD = {(0, 1): 0, (0, 2): 1, (1, 1): 2, (1, 2): 3, (0, 3): 8, (1, 3): 9}
    BWD = {(1, 2): 4, (1, 1): 5, (0, 2): 6, (0, 1): 7, (1, 3): 10, (0, 3): 11}

    def stats_out(k, which, g, a):
        ZD[which][0][k, group(g)] = a
        ar_send(FWD[(k, which)], g, jnp.sum(a, axis=1, keepdims=True), jnp.sum(a * a, axis=1, keepdims=True))

    def normed(k, which, g):
        z_ref, _, gr_ref = ZD[which]
        one, two = ar_take(FWD[(k, which)], g)
        mean = one / count
        inv = lax.rsqrt(two / count - mean * mean + EPS)
        z = (z_ref[k, group(g)] - mean) * inv
        z_ref[k, group(g)] = z
        gain = gain_ref[k : k + 1, norm_cols(which, k)][None]
        gr_ref[k, group(g)] = gain * inv
        return z * gain + shift_ref[k : k + 1, norm_cols(which, k)][None]

    def hidden_out(k, which, g, idx, buf):
        act, slope = gelu_pair(normed(k, which, g))
        ZD[which][1][k, group(g)] = slope
        mine = shard(k, me_p)
        buf[k, mine, group(g)] = jnp.where(real_rows(LANES), act, 0.0).astype(BF16)
        ag_send(idx, g, buf.at[k], mine)

    def back_out(k, which, g, up):
        ar_send(
            BWD[(k, which)],
            g,
            jnp.sum(up, axis=1, keepdims=True),
            jnp.sum(up * ZD[which][0][k, group(g)], axis=1, keepdims=True),
        )

    def back_in(k, which, g, up):
        z_ref, _, gr_ref = ZD[which]
        one, two = ar_take(BWD[(k, which)], g)
        chunk0 = {1: 0, 2: 1, 3: 2}[which]
        for n in range(one.shape[-1] // LANES):
            lanes = slice(n * LANES, (n + 1) * LANES)
            s.norm_sum[me_p, chunk0 + n, 2 * k : 2 * k + 1, :] += jnp.sum(two[:, :, lanes], axis=0)
            s.norm_sum[me_p, chunk0 + n, 2 * k + 1 : 2 * k + 2, :] += jnp.sum(one[:, :, lanes], axis=0)
        grad = gr_ref[k, group(g)] * (up - one / count - z_ref[k, group(g)] * (two / count))
        return jnp.where(real_rows(grad.shape[-1]), grad, 0.0).astype(BF16)

    def shifted(v, by):
        by = by % flat
        return v if by == 0 else pltpu.roll(v, by, 0)

    def tap_shift(t):
        return SIDE * (t // 3 - 1) + (t % 3 - 1)

    def masked(v, t):
        return v.reshape(GM, R, LANES) * s.mask[t][None]

    def conv(k, h):
        acc = None
        for t0 in range(0, TAPS, 2):
            taps = [t for t in (t0, t0 + 1) if t < TAPS]
            w = s.wf[k, taps[0]] if len(taps) == 1 else jnp.concatenate([s.wf[k, t] for t in taps], axis=1)
            y = dot(h, w)
            for n, t in enumerate(taps):
                part = masked(shifted(y[:, n * LANES : (n + 1) * LANES], -tap_shift(t)), t)
                acc = part if acc is None else acc + part
        return acc

    def conv_back(k, g, d):
        flat_d = d.astype(F32)
        for t in range(TAPS):
            part = shifted((flat_d * s.mask[t][None]).reshape(flat, LANES), tap_shift(t))
            s.dcol[k, group(g), :, t * LANES : (t + 1) * LANES] = part.astype(BF16).reshape(GM, R, LANES)
        w = jnp.concatenate([s.wf[k, t] for t in range(TAPS)], axis=1)
        return dot_nt(s.dcol[k, group(g)].reshape(flat, TAPS * LANES), w)

    tail = []

    def work():
        load_all.wait()

        @pl.when(me_p == 0)
        def _():
            load_p.wait()

            @pl.loop(0, G)
            def _(g):
                a = dot(s.u_all[group(g)].reshape(flat, c.ch), s.p_own[...])
                for j in range(NP):
                    s.put[0, j, group(g)] = a[:, j * LANES : (j + 1) * LANES].reshape(GM, R, LANES).astype(BF16)
                s.first[group(g)] = s.put[0, 0, group(g)]
                for p in range(1, NP):
                    remote(
                        s.put.at[0, shard(0, jnp.int32(p)), group(g)], s.first.at[group(g)], s.rs_s.at[0, g], s.rs_r.at[0, g], p, me_d
                    ).start()


        for k in range(2):

            @pl.loop(0, G)
            def _(g):
                if k == 0:

                    @pl.when(me_p != 0)
                    def _():
                        take_recv(s.first.at[group(g)], s.rs_s.at[0, g], s.rs_r.at[0, g])

                    a = s.first[group(g)].astype(F32)
                else:
                    a = rs_take(1, g, 1)
                stats_out(k, 1, g, a)
            pass_one(*((4, 5) if k == 0 else (3,)))

            @pl.loop(0, G)
            def _(g):
                hidden_out(k, 1, g, 2 * k, s.h1)
            if k == 0:

                @on_pipes(1)
                def _():
                    for i in range(1, NP):
                        proj_send(i).start()

            else:
                pass_two(3)


            if k == 0:
                pass_two(4, 5)
            need(4 + k)

            @pl.loop(0, G)
            def _(g):
                stats_out(k, 2, g, conv(k, ag_take(2 * k, g, s.h1.at[k])))
            if k == 0:
                pass_one(1, 2)

            @pl.loop(0, G)
            def _(g):
                hidden_out(k, 2, g, 2 * k + 1, s.h2)
            if k == 0:
                pass_two(1, 2)

                @on_pipes(3)
                def _():
                    for i in range(1, NP):
                        proj_send(i).start()


            need(2 * k + 1)
            if k == 0:
                load_u.wait()

            @pl.loop(0, G)
            def _(g):
                a = dot_nt(ag_take(2 * k + 1, g, s.h2.at[k]), s.pq[2 * k + 1])
                stats_out(k, 3, g, a.reshape(GM, R, c.cs))

            if k == 0:
                need(2)

                @pl.loop(0, G)
                def _(g):
                    v = normed(0, 3, g) + s.u_seg[0, group(g)].astype(F32)
                    act, slope = gelu_pair(v)
                    s.d3[0, group(g)] = slope
                    o = jnp.where(real_rows(c.cs), act, 0.0).astype(BF16)
                    s.u_seg[1, group(g)] = o
                    rs_send(1, g, 1, dot(o.reshape(flat, c.cs), s.pq[2]))

        load_g.wait()

        @pl.loop(0, G)
        def _(g):
            v = normed(1, 3, g) + s.u_seg[1, group(g)].astype(F32)
            act, slope = gelu_pair(v)
            o = jnp.where(real_rows(c.cs), act, 0.0).astype(BF16)
            s.out_seg[group(g)] = o
            e = s.g_seg[group(g)].astype(F32) * slope
            s.e3[group(g)] = e
            back_out(1, 3, g, e)
            o32 = o.astype(F32)
            place = lax.broadcasted_iota(jnp.int32, (GM, R, c.cs), 1)
            for n in range(c.images):
                here = (place >= n * SIDE * SIDE) & (place < (n + 1) * SIDE * SIDE)
                mean = jnp.sum(jnp.where(here, o32, 0.0), axis=1, keepdims=True) / float(SIDE * SIDE)
                for m in range(GM):
                    s.pool[(g * GM + m) * c.images + n] = mean[m]

        out_copy = pltpu.make_async_copy(s.out_seg, bo_out, s.out_r.at[0])
        out_copy.start()
        tail.append(out_copy.wait)

        banks = ND * c.bank
        which = lax.broadcasted_iota(jnp.int32, (banks, c.cs), 0)
        term = jnp.zeros((banks, c.cs), F32)
        for n in range(M * c.images):
            ids = jnp.concatenate([ids_ref[n : n + 1, :]] * (c.cs // LANES), axis=1)
            term = term + jnp.where(which == ids, s.pool[n], 0.0)
        s.bank_put[...] = term.reshape(ND, c.bank, c.cs)

        @pl.loop(1, ND)
        def _(i):
            d = dp_peer(i)
            remote(s.bank_put.at[d], s.bank_got.at[me_d], s.bank_s.at[0], s.bank_r.at[0], me_p, d).start()

        tail.append(lambda: take_send(s.bank_got.at[pl.ds(0, ND - 1)], s.bank_s.at[0], s.bank_r.at[0]))

        s.bank_got[me_d] = s.bank_put[me_d]

        def all_rows(ref):
            return ref[...].reshape(M * R, ref.shape[-1])

        def all_seg(ref):
            return jnp.concatenate([ref[j].reshape(M * R, LANES) for j in range(NP)], axis=1)

        def grad_q(k):
            h = all_seg(s.h2.at[k])
            s.gp[2 * k + 1] = dot_tn(all_rows(s.da3.at[k]), h).astype(BF16)

        def grad_p0():
            d = s.da1[0, shard(0, me_p)].reshape(M * R, LANES)
            s.g0[...] = dot_tn(all_rows(s.u_all), d).astype(BF16)

        def grad_p(k):
            d = all_seg(s.da1.at[k])
            s.gp[2 * k] = dot_tn(all_rows(s.u_seg.at[k]), d).astype(BF16)

        def grad_w(k):
            h = all_seg(s.h1.at[k])
            for t0 in range(0, TAPS, 2):
                taps = [t for t in (t0, t0 + 1) if t < TAPS]
                d = s.dcol[k, :, :, t0 * LANES : (t0 + len(taps)) * LANES].reshape(M * R, len(taps) * LANES)
                v = dot_tn(h, d)
                for n, t in enumerate(taps):
                    s.gw[k, t * c.mid : (t + 1) * c.mid, :] = v[:, n * LANES : (n + 1) * LANES].astype(BF16)

        def part(base, n):
            return pl.ds(pl.multiple_of(base, 16), n)

        inner = (me_z == 1) | (me_z == 2)
        z_side = lax.div(me_z, 2)
        outer_dev = 2 * (3 * z_side) + me_c
        inner_dev = 2 * (1 + z_side) + me_c
        across_dev = 2 * (2 - z_side) + me_c

        def job_own(job):
            kind, k, n, base, slot = c.jobs[job]
            ref = s.g0 if kind == "0" else s.gw.at[k] if kind == "w" else s.gp.at[2 * k + (kind == "q")]
            return ref, base

        def job_ref(name, job):
            kind, k, n, base, slot = c.jobs[job]
            return getattr(s, name + ("p" if kind in "pq" else kind)).at[slot]

        def job_core(job):
            own, base = job_own(job)
            n = c.jobs[job][2]
            view = own.at[part(base + (1 - me_c) * n, n)]
            remote(view, job_ref("ja", job), s.gs.at[job, 0], s.gr.at[job, 0], me_p, sib).start()

        def job_in(job):
            own, base = job_own(job)
            n = c.jobs[job][2]
            got, tot = job_ref("ja", job), job_ref("jb", job)
            take_recv(got, s.gs.at[job, 0], s.gr.at[job, 0])
            tot[...] = (got[...].astype(F32) + own[part(base + me_c * n, n), :].astype(F32)).astype(BF16)
            @pl.when(jnp.logical_not(inner))
            def _():
                remote(tot, job_ref("jc", job), s.gs.at[job, 1], s.gr.at[job, 1], me_p, inner_dev).start()

        def job_halve(job):
            n = c.jobs[job][2]
            got, tot, half = job_ref("jc", job), job_ref("jb", job), job_ref("jd", job)

            @pl.when(inner)
            def _():
                take_recv(got, s.gs.at[job, 1], s.gr.at[job, 1])
                tot[...] = (got[...].astype(F32) + tot[...].astype(F32)).astype(BF16)
                view = tot.at[part((1 - z_side) * (n // 2), n // 2)]
                remote(view, half, s.gs.at[job, 2], s.gr.at[job, 2], me_p, across_dev).start()

        def job_sum(job):
            n = c.jobs[job][2]
            tot, half, fin = job_ref("jb", job), job_ref("jd", job), job_ref("je", job)
            mine = part(z_side * (n // 2), n // 2)

            @pl.when(inner)
            def _():
                take_recv(half, s.gs.at[job, 2], s.gr.at[job, 2])
                fin[mine, :] = (half[...].astype(F32) + tot[mine, :].astype(F32)).astype(BF16)
                view = fin.at[mine]
                remote(view, view, s.gs.at[job, 3], s.gr.at[job, 3], me_p, across_dev).start()
                remote(view, view, s.gs.at[job, 4], s.gr.at[job, 3], me_p, outer_dev).start()

        def job_out(job):
            n = c.jobs[job][2]
            fin = job_ref("je", job)
            view = fin.at[part((1 - z_side) * (n // 2), n // 2)]

            @pl.when(inner)
            def _():
                take_recv(view, s.gs.at[job, 3], s.gr.at[job, 3])
                remote(view, view, s.gs.at[job, 5], s.gr.at[job, 4], me_p, outer_dev).start()

        def job_place(job, p, core):
            kind, k, n, base, slot = c.jobs[job]
            if kind == "0":
                return s.p0_out.at[shard(0, p), part(base + core * n, n)]
            if kind == "w":
                return s.w_out.at[lax.div(p, 2) if k == 0 else 1 - lax.div(p, 2), part(base + core * n, n)]
            return s.p_out.at[part(p * 2 * n + core * n, n)]

        def job_home(job, p):
            kind, k = c.jobs[job][:2]
            return 2 * k + lax.rem(p, 2) if kind == "w" else jnp.int32(2 * k + (kind == "q"))

        def job_holds(job):
            kind, k = c.jobs[job][:2]
            return me_y == k if kind == "w" else me_p == 2 * k + (kind == "q")

        def job_plane(job):
            n = c.jobs[job][2]
            fin = job_ref("je", job)

            @pl.when(jnp.logical_not(inner))
            def _():
                for step in (3, 4):
                    take_recv(fin.at[0 : n // 2], s.gs.at[job, step], s.gr.at[job, step])

            home = job_home(job, me_p)

            @pl.when(me_p != home)
            def _():
                remote(fin, job_place(job, me_p, me_c), s.gs.at[job, 6], s.gr.at[job, 5], home, me_d).start()

            @pl.when(me_p == home)
            def _():
                pltpu.make_async_copy(fin, job_place(job, me_p, me_c), s.own_s.at[job]).start()

        def job_many(job, count):
            kind, k, n, base, slot = c.jobs[job]
            if kind == "0":
                return s.p0_out.at[pl.ds(0, count), pl.ds(0, n)]
            return s.w_out.at[pl.ds(0, count), pl.ds(0, n)] if kind == "w" else s.p_out.at[pl.ds(0, n * count)]

        def job_share(job):
            fin = job_ref("je", job)
            from_pipes = [0, 2] if c.jobs[job][0] == "w" else [0, 1, 2, 3]

            @pl.when(job_holds(job))
            def _():
                pltpu.make_async_copy(fin, job_place(job, me_p, me_c), s.own_s.at[job]).wait()
                take_recv(job_many(job, len(from_pipes) - 1), s.gs.at[job, 6], s.gr.at[job, 5])
                for i in from_pipes:
                    view = job_place(job, pipe_peer(i), me_c)
                    remote(view, view, s.fin_s.at[job], s.fin_r.at[job], me_p, sib).start()

        def job_end(job):
            got, half, fin = job_ref("ja", job), job_ref("jd", job), job_ref("je", job)
            take_send(got, s.gs.at[job, 0], s.gr.at[job, 0])

            @pl.when(inner)
            def _():
                for step in (2, 3, 4, 5):
                    take_send(half, s.gs.at[job, step], s.gr.at[job, 2])

            @pl.when(jnp.logical_not(inner))
            def _():
                take_send(got, s.gs.at[job, 1], s.gr.at[job, 1])

            @pl.when(me_p != job_home(job, me_p))
            def _():
                take_send(fin, s.gs.at[job, 6], s.gr.at[job, 5])

            @pl.when(job_holds(job))
            def _():
                view = job_many(job, 2 if c.jobs[job][0] == "w" else NP)
                take_recv(view, s.fin_s.at[job], s.fin_r.at[job])
                take_send(view, s.fin_s.at[job], s.fin_r.at[job])

        def job_store(job, act):
            kind, k, n, base, slot = c.jobs[job]
            rows = pl.ds(base, 2 * n)
            if kind == "0":
                parts = [(s.p0_out.at[j, rows], gp_out.at[rows, pl.ds(j * LANES, LANES)]) for j in range(NP)]
            elif kind == "w":
                parts = [(s.w_out.at[h, rows], gw_out.at[rows, pl.ds(h * LANES, LANES)]) for h in range(2)]
            else:
                parts = [(s.p_out, gp_out)]

            @pl.when(job_holds(job))
            def _():
                for i, (src, dst) in enumerate(parts):
                    getattr(pltpu.make_async_copy(src, dst, s.store.at[job, i]), act)()

        steps = (job_core, job_in, job_halve, job_sum, job_out, job_plane, job_share)
        next_step = dict.fromkeys(c.jobs, 0)

        def advance(*jobs):
            if c.deep:
                for job in jobs:
                    if next_step[job] < len(steps):
                        steps[next_step[job]](job)
                        next_step[job] += 1

        def point(k, n):
            advance(*POINTS[(1 - k) * 6 + n])

        for k in (1, 0):
            side = 2 * (1 - k)

            @pl.loop(0, G)
            def _(g):
                grad = back_in(k, 3, g, s.e3[group(g)])
                s.da3[k, group(g)] = grad
                rs_send(2 + (1 - k), g, k, dot(grad.reshape(flat, c.cs), s.pq[2 * k + 1]))

            grad_q(k)
            if k == 1:

                @on_pipes(0)
                def _():
                    for i in range(1, NP):
                        proj_send(i).start()

            point(k, 0)

            @pl.loop(0, G)
            def _(g):
                up = rs_take(2 + (1 - k), g, k) * s.d2[k, group(g)]
                s.t1[group(g)] = up
                back_out(k, 2, g, up)
            if k == 0:
                pass_one(0)
            point(k, 1)

            @pl.loop(0, G)
            def _(g):
                rs_send(5 - k, g, k, conv_back(k, g, back_in(k, 2, g, s.t1[group(g)])))

            grad_w(k)
            point(k, 2)

            @pl.loop(0, G)
            def _(g):
                up = rs_take(5 - k, g, k) * s.d1[k, group(g)]
                s.t1[group(g)] = up
                back_out(k, 1, g, up)
            if k == 0:
                pass_two(0)
            point(k, 3)

            @pl.loop(0, G)
            def _(g):
                mine = shard(k, me_p)
                s.da1[k, mine, group(g)] = back_in(k, 1, g, s.t1[group(g)])
                ag_send(5 + side, g, s.da1.at[k], mine)
            if k == 0:
                grad_p0()
            point(k, 4)

            if k == 0:
                need(0)

            @pl.loop(0, G)
            def _(g):
                d = dot_nt(ag_take(5 + side, g, s.da1.at[k]), s.pq[2 * k])
                d = d.reshape(GM, R, c.cs) + s.e3[group(g)]
                if k == 1:
                    e = d * s.d3[0, group(g)]
                    s.e3[group(g)] = e
                    back_out(0, 3, g, e)
                else:
                    s.in_seg[group(g)] = d.astype(BF16)

            if k == 1 or not c.deep:
                grad_p(k)
            point(k, 5)

        in_copy = pltpu.make_async_copy(s.in_seg, ig_out, s.out_r.at[1])
        in_copy.start()
        tail.append(in_copy.wait)
        view = s.norm_sum.at[me_p]
        for i in range(1, NP):
            remote(view, view, s.ns_s.at[0], s.ns_r.at[0], pipe_peer(i), me_d).start()
        tail.append(lambda: take_send(s.norm_sum.at[pl.ds(0, NP - 1)], s.ns_s.at[0], s.ns_r.at[0]))

        while c.deep and min(next_step.values()) < len(steps) - 1:
            advance(*[job for job in LAST if next_step[job] < len(steps) - 1])

        take_recv(s.bank_got.at[pl.ds(0, ND - 1)], s.bank_s.at[0], s.bank_r.at[0])
        tot = s.bank_got[0]
        for d in range(1, ND):
            tot = tot + s.bank_got[d]
        mb_out[...] = tot
        take_recv(s.norm_sum.at[pl.ds(0, NP - 1)], s.ns_s.at[0], s.ns_r.at[0])
        per = c.mid // LANES
        wide = c.cs // LANES
        each = (2 * per + c.ch // LANES) // NP
        for k in range(2):
            for n in range(each):
                q = me_p * each + n
                in_one = q < per
                in_two = (q >= per) & (q < 2 * per)
                sh = jnp.where(in_one, q, q - per)
                half = lax.rem(sh + k, 2)
                small = 2 * half + lax.div(sh, 2)
                far = q - 2 * per
                p = jnp.where(q < 2 * per, small, lax.div(far, wide))
                chunk = jnp.where(in_one, 0, jnp.where(in_two, 1, 2 + lax.rem(far, wide)))
                ns_out[n, 2 * k : 2 * k + 2, :] = s.norm_sum[p, chunk, 2 * k : 2 * k + 2, :]

        def drain():
            front_send().wait_send()
            for i in range(1, NP):
                proj_send(i).wait_send()
            for n in range(6):
                end_part(n)

            @pl.loop(0, G)
            def _(g):
                for wait in [*due.values(), *owed.values()]:
                    wait(g)

                @pl.when(me_p == 0)
                def _():
                    take_send(s.put.at[0, pl.ds(0, NP - 1), group(g)], s.rs_s.at[0, g], s.rs_r.at[0, g])
            for wait in tail:
                wait()

        drain()
        advance(*c.jobs)
        if c.deep:
            for job in c.jobs:
                job_end(job)
                job_store(job, "start")
            for job in c.jobs:
                job_store(job, "wait")

    work()

    if not c.deep:
        copies = [
            pltpu.make_async_copy(s.gp, gp_out, s.out_r.at[2]),
            pltpu.make_async_copy(s.gw, gw_out, s.out_r.at[3]),
        ]
        for copy in copies:
            copy.start()
        for copy in copies:
            copy.wait()


def on_device(mesh, block_input, proj_weight, spatial_weight, norm_gain, norm_shift, output_grad, image_ids):
    bank = 8
    c = Sizes(mesh, block_input, proj_weight, spatial_weight, bank)
    extra = ((0, 0), (0, c.pad - c.rows), (0, 0))
    u = jnp.pad(block_input, extra)
    go = lax.dynamic_slice_in_dim(output_grad, lax.axis_index("pipe") * c.cs, c.cs, axis=2)
    go = jnp.pad(go, extra)
    sw = spatial_weight.reshape(TAPS, c.mid, spatial_weight.shape[2])
    ids = jnp.broadcast_to(image_ids.reshape(-1, 1), (image_ids.size, LANES))
    items = scratch_list(c)
    names = [n for n, _ in items]
    anyspec = pl.BlockSpec(memory_space=pl.ANY)
    vspec = pl.BlockSpec(memory_space=pltpu.VMEM)
    if c.deep:
        gp_shape, gw_shape = (c.ch, c.mid), (TAPS * c.mid, 2 * LANES)
    else:
        gp_shape, gw_shape = (c.pipes, c.cs, c.mid), (2, TAPS * c.mid, LANES)
    each = (2 * c.mid + c.ch) // LANES // c.pipes
    outs = pl.pallas_call(
        functools.partial(body, c, names),
        out_shape=(
            jax.ShapeDtypeStruct((c.micro, c.pad, c.cs), BF16),
            jax.ShapeDtypeStruct((c.micro, c.pad, c.cs), BF16),
            jax.ShapeDtypeStruct(gp_shape, BF16),
            jax.ShapeDtypeStruct(gw_shape, BF16),
            jax.ShapeDtypeStruct((each, 4, LANES), F32),
            jax.ShapeDtypeStruct((bank, c.cs), F32),
        ),
        in_specs=[anyspec] * 4 + [vspec] * 3,
        out_specs=(anyspec, anyspec, anyspec, anyspec, vspec, vspec),
        scratch_shapes=[v for _, v in items],
        compiler_params=pltpu.CompilerParams(collective_id=0, has_side_effects=True, vmem_limit_bytes=60 << 20),
    )(u, go, proj_weight[0], sw, norm_gain, norm_shift, ids)
    bo, ig, gp, gw, ns, mb = outs
    if not c.deep:
        gp = lax.psum(gp.astype(F32), "dp")
        gw = lax.psum(gw.astype(F32), "dp")
        gp = lax.all_to_all(gp, "pipe", 0, 0, tiled=True).reshape(c.ch, c.mid)
        gw = lax.all_gather(gw, "pipe")
        me = lax.axis_index("pipe")
        y, x = me // 2, me % 2
        near = lax.dynamic_index_in_dim(gw, me, 0, keepdims=False)
        far = lax.dynamic_index_in_dim(gw, 2 * (1 - y) + x, 0, keepdims=False)
        gw = jnp.concatenate(
            [lax.dynamic_index_in_dim(near, y, 0, keepdims=False), lax.dynamic_index_in_dim(far, y, 0, keepdims=False)],
            axis=1,
        )
    ns = jnp.transpose(ns.reshape(each, 2, 2, LANES), (2, 1, 0, 3)).reshape(2, 2, each * LANES)
    return (
        bo[:, : c.rows],
        ig[:, : c.rows],
        gp.astype(F32)[None],
        gw.astype(F32)[None],
        ns[0],
        ns[1],
        mb,
    )


def solution(mesh):
    return jax.shard_map(
        functools.partial(on_device, mesh),
        mesh=mesh,
        in_specs=(
            P(None, "dp", None),
            P("pipe", None, None),
            P("pipe", None, None),
            P(),
            P(),
            P(None, "dp", None),
            P(None, "dp"),
        ),
        out_specs=(
            P(None, "dp", "pipe"),
            P(None, "dp", "pipe"),
            P("pipe", None, None),
            P("pipe", None, None),
            P(None, "pipe"),
            P(None, "pipe"),
            P("dp", "pipe"),
        ),
        check_vma=False,
    )
```

```python
import functools
import math
import types

import jax
import jax.numpy as jnp
from jax import lax
from jax.experimental import pallas as pl
from jax.experimental.pallas import tpu as pltpu
from jax.sharding import PartitionSpec as P

SIDE = 7
TAPS = 9
EPS = 1e-05
LANES = 128
GROUPS = 4
W_PIECES = 3
P_PIECES = 2
POINTS = (
    (0,),
    (0,),
    (0, 1, 2, 3),
    (0, 1, 2),
    (0, 1),
    (1, 2, 3, 4),
    (0, 1, 2, 3, 4, 5),
    (2, 3, 4, 5),
    (6, 7, 8, 1, 2, 3, 4, 5),
    (6, 7, 8, 5, 4),
    (9, 10, 6, 5),
    (9, 10, 6, 7, 8, 5, 3, 4),
)
LAST = (6, 7, 8, 9, 10, 5, 4, 3, 0, 1, 2)
MESH = pl.DeviceIdType.MESH
F32 = jnp.float32
BF16 = jnp.bfloat16


def gelu_pair(v):
    c0 = math.sqrt(2.0 / math.pi)
    c1 = 0.044715
    sq = v * v
    t = jnp.tanh(c0 * v * (1.0 + c1 * sq))
    half = 0.5 + 0.5 * t
    slope = half + (0.5 * c0) * v * (1.0 - t * t) * (1.0 + (3.0 * c1) * sq)
    return v * half, slope


def dot(a, b):
    return jnp.dot(a, b, preferred_element_type=F32)


def dot_nt(a, b):
    return lax.dot_general(a, b, (((1,), (1,)), ((), ())), preferred_element_type=F32)


def dot_tn(a, b):
    return lax.dot_general(a, b, (((0,), (0,)), ((), ())), preferred_element_type=F32)


class Sizes:
    def __init__(self, mesh, block_input, proj, spatial, bank_rows):
        self.pipes = mesh.shape["pipe"]
        self.dps = mesh.shape["dp"]
        self.micro = block_input.shape[0]
        self.rows = block_input.shape[1]
        self.pad = -(-self.rows // 16) * 16
        self.ch = block_input.shape[2]
        self.mid = proj.shape[2]
        self.images = self.rows // (SIDE * SIDE)
        self.cs = self.ch // self.pipes
        self.msd = self.mid // self.pipes
        self.groups = GROUPS
        self.gm = self.micro // self.groups
        self.zs = self.dps // 2
        self.total = self.rows * self.dps
        self.bank = bank_rows
        self.deep = self.zs == 4
        self.jobs = {}
        taps = TAPS // W_PIECES
        for k in (1, 0):
            self.jobs[len(self.jobs)] = ("q", k, self.cs // 2, 0, 1 - k)
            for i in range(W_PIECES):
                self.jobs[len(self.jobs)] = ("w", k, taps * self.mid // 2, i * taps * self.mid, (1 - k) * W_PIECES + i)
            if k == 1:
                self.jobs[len(self.jobs)] = ("p", k, self.cs // 2, 0, 2)
        for i in range(P_PIECES):
            self.jobs[len(self.jobs)] = ("0", 0, self.ch // P_PIECES // 2, i * self.ch // P_PIECES, i)


def scratch_list(c):
    full = (c.micro, c.pad)
    seg = (c.pipes, c.micro, c.pad, LANES)
    items = [
        ("u_all", pltpu.VMEM(full + (c.ch,), BF16)),
        ("u_seg", pltpu.VMEM((2,) + full + (c.cs,), BF16)),
        ("g_seg", pltpu.VMEM(full + (c.cs,), BF16)),
        ("p_own", pltpu.VMEM((c.ch, c.mid), BF16)),
        ("pq", pltpu.VMEM((c.pipes, c.cs, c.mid), BF16)),
        ("wf", pltpu.VMEM((2, TAPS, c.mid, LANES), BF16)),
        ("sw", pltpu.VMEM((2, TAPS, c.mid, LANES), BF16)),
        ("mask", pltpu.VMEM((TAPS, c.pad, LANES), F32)),
        ("z1", pltpu.VMEM((2,) + full + (LANES,), F32)),
        ("d1", pltpu.VMEM((2,) + full + (LANES,), F32)),
        ("z2", pltpu.VMEM((2,) + full + (LANES,), F32)),
        ("d2", pltpu.VMEM((2,) + full + (LANES,), F32)),
        ("z3", pltpu.VMEM((2,) + full + (c.cs,), F32)),
        ("d3", pltpu.VMEM((2,) + full + (c.cs,), F32)),
        ("e3", pltpu.VMEM(full + (c.cs,), F32)),
        ("t1", pltpu.VMEM(full + (LANES,), F32)),
        ("gr1", pltpu.VMEM((2, c.micro, 1, LANES), F32)),
        ("gr2", pltpu.VMEM((2, c.micro, 1, LANES), F32)),
        ("gr3", pltpu.VMEM((2, c.micro, 1, c.cs), F32)),
        ("h1", pltpu.VMEM((2,) + seg, BF16)),
        ("h2", pltpu.VMEM((2,) + seg, BF16)),
        ("da3", pltpu.VMEM((2,) + full + (c.cs,), BF16)),
        ("dcol", pltpu.VMEM((2,) + full + (TAPS * LANES,), BF16)),
        ("da1", pltpu.VMEM((2,) + seg, BF16)),
        ("first", pltpu.VMEM(full + (LANES,), BF16)),
        ("put", pltpu.VMEM((6,) + seg, BF16)),
        ("got", pltpu.VMEM((6,) + seg, BF16)),
        ("out_seg", pltpu.VMEM(full + (c.cs,), BF16)),
        ("in_seg", pltpu.VMEM(full + (c.cs,), BF16)),
        ("ar_small", pltpu.VMEM((8, c.dps, c.micro, 2, LANES), F32)),
        ("ar_wide", pltpu.VMEM((4, c.dps, c.micro, 2, c.cs), F32)),
        ("pool", pltpu.VMEM((c.micro * c.images, 1, c.cs), F32)),
        ("bank_put", pltpu.VMEM((c.dps, c.bank, c.cs), F32)),
        ("bank_got", pltpu.VMEM((c.dps, c.bank, c.cs), F32)),
        ("norm_sum", pltpu.VMEM((c.pipes, 6, 8, LANES), F32)),
        ("gp", pltpu.VMEM((c.pipes, c.cs, c.mid), BF16)),
        ("g0", pltpu.VMEM((c.ch, LANES), BF16)),
        ("gw", pltpu.VMEM((2, TAPS * c.mid, LANES), BF16)),
        ("ar_s", pltpu.SemaphoreType.DMA((12, c.groups))),
        ("ar_r", pltpu.SemaphoreType.DMA((12, c.groups))),
        ("ag_s", pltpu.SemaphoreType.DMA((8, c.groups))),
        ("ag_r", pltpu.SemaphoreType.DMA((8, c.groups))),
        ("rs_s", pltpu.SemaphoreType.DMA((6, c.groups))),
        ("rs_r", pltpu.SemaphoreType.DMA((6, c.groups))),
        ("w_s", pltpu.SemaphoreType.DMA((2, c.pipes))),
        ("pass_s", pltpu.SemaphoreType.DMA((6, 3))),
        ("w_r", pltpu.SemaphoreType.DMA((6,))),
        ("w_z", pltpu.SemaphoreType.DMA((6,))),
        ("w_q", pltpu.SemaphoreType.DMA((6,))),
        ("bank_s", pltpu.SemaphoreType.DMA((1,))),
        ("bank_r", pltpu.SemaphoreType.DMA((1,))),
        ("ns_s", pltpu.SemaphoreType.DMA((1,))),
        ("ns_r", pltpu.SemaphoreType.DMA((1,))),
        ("in_r", pltpu.SemaphoreType.DMA((6,))),
        ("out_r", pltpu.SemaphoreType.DMA((4 + c.pipes,))),
    ]
    if c.deep:
        for name, width in (("p", c.mid), ("w", LANES), ("0", LANES)):
            of = [job for job in c.jobs.values() if job[0] in {"p": "pq"}.get(name, name)]
            lead, n = len(of), of[0][2]
            items += [(key + name, pltpu.VMEM((lead, n // (1 + (key == "jd")), width), BF16)) for key in ("ja", "jb", "jc", "jd", "je")]
        count = len(c.jobs)
        items += [
            ("p_out", pltpu.VMEM((c.ch, c.mid), BF16)),
            ("p0_out", pltpu.VMEM((c.pipes, c.ch, LANES), BF16)),
            ("w_out", pltpu.VMEM((2, TAPS * c.mid, LANES), BF16)),
            ("gs", pltpu.SemaphoreType.DMA((count, 7))),
            ("gr", pltpu.SemaphoreType.DMA((count, 6))),
            ("own_s", pltpu.SemaphoreType.DMA((count,))),
            ("store", pltpu.SemaphoreType.DMA((count, c.pipes))),
            ("fin_s", pltpu.SemaphoreType.DMA((count,))),
            ("fin_r", pltpu.SemaphoreType.DMA((count,))),
        ]
    return items


def body(c, names, *refs):
    (u_hbm, go_hbm, pw_hbm, sw_hbm, gain_ref, shift_ref, ids_ref) = refs[:7]
    (bo_out, ig_out, gp_out, gw_out, ns_out, mb_out) = refs[7:13]
    s = types.SimpleNamespace(**dict(zip(names, refs[13:])))
    me_p = lax.axis_index("pipe")
    me_d = lax.axis_index("dp")
    me_x = lax.rem(me_p, 2)
    me_y = lax.div(me_p, 2)
    NP, ND, M, GM, G, R = c.pipes, c.dps, c.micro, c.gm, c.groups, c.pad
    flat = GM * R
    count = float(c.total)

    def shard(k, p):
        half = lax.div(p, 2)
        return 2 * lax.rem(p, 2) + (half if k == 0 else 1 - half)

    def pipe_peer(i):
        return lax.rem(me_p + i, NP)

    def dp_peer(i):
        return lax.rem(me_d + i, ND)

    def remote(src, dst, ss, rs, p, d):
        return pltpu.make_async_remote_copy(
            src_ref=src, dst_ref=dst, send_sem=ss, recv_sem=rs, device_id=(p, d), device_id_type=MESH
        )

    def take_recv(view, ss, rs):
        remote(view, view, ss, rs, me_p, me_d).wait_recv()

    def take_send(view, ss, rs):
        remote(view, view, ss, rs, me_p, me_d).wait_send()

    def group(g):
        return pl.ds(g * GM, GM)

    owed, due = {}, {}

    lane0 = pl.multiple_of(me_p * c.cs, LANES)
    seg_cols = pl.ds(lane0, c.cs)
    load_u = pltpu.make_async_copy(u_hbm.at[:, :, seg_cols], s.u_seg.at[0], s.in_r.at[0])
    load_g = pltpu.make_async_copy(go_hbm, s.g_seg, s.in_r.at[1])
    load_all = pltpu.make_async_copy(u_hbm, s.u_all, s.in_r.at[2])
    load_p = pltpu.make_async_copy(pw_hbm, s.p_own, s.in_r.at[3])
    load_w = [
        pltpu.make_async_copy(sw_hbm.at[:, :, pl.ds(h * LANES, LANES)], s.sw.at[h], s.in_r.at[4 + h]) for h in range(2)
    ]
    for load in reversed(load_w):
        load.start()
    load_all.start()

    @pl.when(me_p == 0)
    def _():
        load_p.start()

    load_u.start()
    load_g.start()

    barrier = pltpu.get_barrier_semaphore()
    for i in range(1, NP):
        pl.semaphore_signal(barrier, inc=1, device_id=(pipe_peer(i), me_d), device_id_type=MESH)

    @pl.loop(1, ND)
    def _(i):
        pl.semaphore_signal(barrier, inc=1, device_id=(me_p, dp_peer(i)), device_id_type=MESH)

    row = lax.broadcasted_iota(jnp.int32, (R, LANES), 0)
    image = jnp.zeros_like(row)
    for n in range(1, c.images):
        image = image + (row >= n * SIDE * SIDE).astype(jnp.int32)
    pixel = row - image * (SIDE * SIDE)
    up = jnp.zeros_like(row)
    for n in range(1, SIDE):
        up = up + (pixel >= n * SIDE).astype(jnp.int32)
    across = pixel - up * SIDE
    for t in range(TAPS):
        i, j = t // 3 - 1, t % 3 - 1
        ok = (up + i >= 0) & (up + i < SIDE) & (across + j >= 0) & (across + j < SIDE) & (row < c.rows)
        s.mask[t] = ok.astype(F32)
    s.norm_sum[...] = jnp.zeros_like(s.norm_sum)

    pl.semaphore_wait(barrier, NP - 1 + ND - 1)

    me_c = lax.rem(me_d, 2)
    me_z = lax.div(me_d, 2)
    sib = me_d + 1 - 2 * me_c

    def link_peer(i):
        flip = me_p + 1 - 2 * me_x
        return (None, flip, lax.rem(me_p + 2, NP), lax.rem(flip + 2, NP))[i]

    def on_pipes(*pipes):
        here = me_p == pipes[0]
        for p in pipes[1:]:
            here = here | (me_p == p)
        return pl.when(here)

    me_l = lax.rem(me_z, 2)
    low = 2 * (me_z + 1 - 2 * me_l) + me_c

    def quarter(part, core, z):
        if part < 4:
            return s.pq.at[part, pl.ds(pl.multiple_of((2 * core + z) * (c.cs // 4), 16), c.cs // 4)]
        return s.wf.at[part - 4, :, pl.ds(pl.multiple_of((2 * core + z) * (c.mid // 4), 16), c.mid // 4)]

    def whole_part(part, core):
        if part < 4:
            return s.pq.at[part] if core is None else s.pq.at[part, pl.ds(pl.multiple_of(core * (c.cs // 2), 16), c.cs // 2)]
        rows = pl.ds(0, c.mid) if core is None else pl.ds(pl.multiple_of(core * (c.mid // 2), 16), c.mid // 2)
        return s.wf.at[part - 4, :, rows]

    def here_already(part):
        return me_p == part if part < 4 else me_y == part - 4

    def proj_send(i):
        p = link_peer(i)
        n = c.cs // 4
        base = (2 * me_c + me_l) * n
        src = pw_hbm.at[pl.ds(pl.multiple_of(p * c.cs + base, 16), n)]
        dst = s.pq.at[me_p, pl.ds(pl.multiple_of(base, 16), n)]
        return remote(src, dst, s.w_s.at[0, i], s.w_r.at[me_p], p, me_d)

    def front_send():
        rows = pl.ds(pl.multiple_of((2 * me_c + me_l) * (c.mid // 4), 16), c.mid // 4)
        return remote(s.sw.at[1, :, rows], s.wf.at[me_y, :, rows], s.w_s.at[1, 0], s.w_r.at[4 + me_y], link_peer(2), me_d)

    def pass_copies(part):
        near, far = quarter(part, me_c, me_l), quarter(part, me_c, 1 - me_l)
        return (
            remote(near, near, s.pass_s.at[part, 0], s.w_z.at[part], me_p, low),
            remote(near, near, s.pass_s.at[part, 1], s.w_q.at[part], me_p, sib),
            remote(far, far, s.pass_s.at[part, 2], s.w_q.at[part], me_p, sib),
        )

    def pass_one(*parts):
        for part in parts:

            @pl.when(jnp.logical_not(here_already(part)))
            def _():
                take_recv(quarter(part, me_c, me_l), s.pass_s.at[part, 0], s.w_r.at[part])
                for copy in pass_copies(part)[:2]:
                    copy.start()

    def pass_two(*parts):
        for part in parts:

            @pl.when(jnp.logical_not(here_already(part)))
            def _():
                take_recv(quarter(part, me_c, 1 - me_l), s.pass_s.at[part, 0], s.w_z.at[part])
                pass_copies(part)[2].start()

    def need(*parts):
        for part in parts:

            @pl.when(jnp.logical_not(here_already(part)))
            def _():
                take_recv(whole_part(part, 1 - me_c), s.pass_s.at[part, 0], s.w_q.at[part])

            @pl.when(here_already(part))
            def _():
                pltpu.make_async_copy(whole_part(part, None), whole_part(part, None), s.w_r.at[part]).wait()

    def end_part(part):
        @pl.when(jnp.logical_not(here_already(part)))
        def _():
            for copy in pass_copies(part):
                copy.wait_send()

    for load in load_w:
        load.wait()

    front_send().start()

    @on_pipes(2)
    def _():
        for i in range(1, NP):
            proj_send(i).start()

    own_rows = pl.ds(pl.multiple_of(me_p * c.cs, 16), c.cs)
    pltpu.make_async_copy(pw_hbm.at[own_rows], s.pq.at[me_p], s.w_r.at[me_p]).start()
    pltpu.make_async_copy(s.sw.at[0], s.wf.at[me_y], s.w_r.at[4 + me_y]).start()

    def note(kind, idx, view, ss, rs):
        owed[kind, idx] = lambda g: take_send(view(g), ss.at[idx, g], rs.at[idx, g])
        due[kind, idx] = lambda g: take_recv(view(g), ss.at[idx, g], rs.at[idx, g])

    def grab(kind, idx, g):
        due.pop((kind, idx))(g)

    def ar_ref(idx):
        return s.ar_small.at[idx] if idx < 8 else s.ar_wide.at[idx - 8]

    def ar_send(idx, g, first, second):
        buf = ar_ref(idx)
        buf[me_d, group(g), 0:1, :] = first
        buf[me_d, group(g), 1:2, :] = second

        @pl.loop(1, ND)
        def _(i):
            view = buf.at[me_d, group(g)]
            remote(view, view, s.ar_s.at[idx, g], s.ar_r.at[idx, g], me_p, me_d ^ (ND - i)).start()

        note("ar", idx, lambda g: ar_ref(idx).at[pl.ds(0, ND - 1), group(g)], s.ar_s, s.ar_r)

    def ar_take(idx, g):
        buf = ar_ref(idx)
        grab("ar", idx, g)
        tot = buf[0, group(g)]
        for d in range(1, ND):
            tot = tot + buf[d, group(g)]
        return tot[:, 0:1, :], tot[:, 1:2, :]

    def ag_send(idx, g, buf, slot):
        view = buf.at[slot, group(g)]
        for i in (3, 1, 2):
            remote(view, view, s.ag_s.at[idx, g], s.ag_r.at[idx, g], link_peer(i), me_d).start()
        note("ag", idx, lambda g: s.h1.at[0, pl.ds(0, NP - 1), group(g)], s.ag_s, s.ag_r)

    def ag_take(idx, g, buf):
        grab("ag", idx, g)
        return jnp.concatenate([buf[j, group(g)].reshape(flat, LANES) for j in range(NP)], axis=1)

    def rs_send(idx, g, k, partial):
        for j in range(NP):
            s.put[idx, j, group(g)] = partial[:, j * LANES : (j + 1) * LANES].reshape(GM, R, LANES).astype(BF16)
        for i in (3, 1, 2):
            p = link_peer(i)
            remote(
                s.put.at[idx, shard(k, p), group(g)],
                s.got.at[idx, me_p, group(g)],
                s.rs_s.at[idx, g],
                s.rs_r.at[idx, g],
                p,
                me_d,
            ).start()
        note("rs", idx, lambda g: s.got.at[idx, pl.ds(0, NP - 1), group(g)], s.rs_s, s.rs_r)

    def rs_take(idx, g, k):
        grab("rs", idx, g)
        tot = s.put[idx, shard(k, me_p), group(g)].astype(F32)
        for i in range(1, NP):
            tot = tot + s.got[idx, pipe_peer(i), group(g)].astype(F32)
        return tot

    def shard_cols(base, k):
        return pl.ds(pl.multiple_of(base + shard(k, me_p) * LANES, LANES), LANES)

    def norm_cols(which, k):
        if which == 1:
            return shard_cols(0, k)
        if which == 2:
            return shard_cols(c.mid, k)
        return pl.ds(pl.multiple_of(2 * c.mid + me_p * c.cs, LANES), c.cs)

    def real_rows(width):
        return lax.broadcasted_iota(jnp.int32, (GM, R, width), 1) < c.rows

    ZD = {1: (s.z1, s.d1, s.gr1), 2: (s.z2, s.d2, s.gr2), 3: (s.z3, s.d3, s.gr3)}
    FWD = {(0, 1): 0, (0, 2): 1, (1, 1): 2, (1, 2): 3, (0, 3): 8, (1, 3): 9}
    BWD = {(1, 2): 4, (1, 1): 5, (0, 2): 6, (0, 1): 7, (1, 3): 10, (0, 3): 11}

    def stats_out(k, which, g, a):
        ZD[which][0][k, group(g)] = a
        ar_send(FWD[(k, which)], g, jnp.sum(a, axis=1, keepdims=True), jnp.sum(a * a, axis=1, keepdims=True))

    def normed(k, which, g):
        z_ref, _, gr_ref = ZD[which]
        one, two = ar_take(FWD[(k, which)], g)
        mean = one / count
        inv = lax.rsqrt(two / count - mean * mean + EPS)
        z = (z_ref[k, group(g)] - mean) * inv
        z_ref[k, group(g)] = z
        gain = gain_ref[k : k + 1, norm_cols(which, k)][None]
        gr_ref[k, group(g)] = gain * inv
        return z * gain + shift_ref[k : k + 1, norm_cols(which, k)][None]

    def hidden_out(k, which, g, idx, buf):
        act, slope = gelu_pair(normed(k, which, g))
        ZD[which][1][k, group(g)] = slope
        mine = shard(k, me_p)
        buf[k, mine, group(g)] = jnp.where(real_rows(LANES), act, 0.0).astype(BF16)
        ag_send(idx, g, buf.at[k], mine)

    def back_out(k, which, g, up):
        ar_send(
            BWD[(k, which)],
            g,
            jnp.sum(up, axis=1, keepdims=True),
            jnp.sum(up * ZD[which][0][k, group(g)], axis=1, keepdims=True),
        )

    def back_in(k, which, g, up):
        z_ref, _, gr_ref = ZD[which]
        one, two = ar_take(BWD[(k, which)], g)
        chunk0 = {1: 0, 2: 1, 3: 2}[which]
        for n in range(one.shape[-1] // LANES):
            lanes = slice(n * LANES, (n + 1) * LANES)
            s.norm_sum[me_p, chunk0 + n, 2 * k : 2 * k + 1, :] += jnp.sum(two[:, :, lanes], axis=0)
            s.norm_sum[me_p, chunk0 + n, 2 * k + 1 : 2 * k + 2, :] += jnp.sum(one[:, :, lanes], axis=0)
        grad = gr_ref[k, group(g)] * (up - one / count - z_ref[k, group(g)] * (two / count))
        return jnp.where(real_rows(grad.shape[-1]), grad, 0.0).astype(BF16)

    def shifted(v, by):
        by = by % flat
        return v if by == 0 else pltpu.roll(v, by, 0)

    def tap_shift(t):
        return SIDE * (t // 3 - 1) + (t % 3 - 1)

    def masked(v, t):
        return v.reshape(GM, R, LANES) * s.mask[t][None]

    def conv(k, h):
        acc = None
        for t0 in range(0, TAPS, 2):
            taps = [t for t in (t0, t0 + 1) if t < TAPS]
            w = s.wf[k, taps[0]] if len(taps) == 1 else jnp.concatenate([s.wf[k, t] for t in taps], axis=1)
            y = dot(h, w)
            for n, t in enumerate(taps):
                part = masked(shifted(y[:, n * LANES : (n + 1) * LANES], -tap_shift(t)), t)
                acc = part if acc is None else acc + part
        return acc

    def conv_back(k, g, d):
        flat_d = d.astype(F32)
        for t in range(TAPS):
            part = shifted((flat_d * s.mask[t][None]).reshape(flat, LANES), tap_shift(t))
            s.dcol[k, group(g), :, t * LANES : (t + 1) * LANES] = part.astype(BF16).reshape(GM, R, LANES)
        w = jnp.concatenate([s.wf[k, t] for t in range(TAPS)], axis=1)
        return dot_nt(s.dcol[k, group(g)].reshape(flat, TAPS * LANES), w)

    tail = []

    def work():
        load_all.wait()

        @pl.when(me_p == 0)
        def _():
            load_p.wait()

            @pl.loop(0, G)
            def _(g):
                a = dot(s.u_all[group(g)].reshape(flat, c.ch), s.p_own[...])
                for j in range(NP):
                    s.put[0, j, group(g)] = a[:, j * LANES : (j + 1) * LANES].reshape(GM, R, LANES).astype(BF16)
                s.first[group(g)] = s.put[0, 0, group(g)]
                for p in range(1, NP):
                    remote(
                        s.put.at[0, shard(0, jnp.int32(p)), group(g)], s.first.at[group(g)], s.rs_s.at[0, g], s.rs_r.at[0, g], p, me_d
                    ).start()


        for k in range(2):

            @pl.loop(0, G)
            def _(g):
                if k == 0:

                    @pl.when(me_p != 0)
                    def _():
                        take_recv(s.first.at[group(g)], s.rs_s.at[0, g], s.rs_r.at[0, g])

                    a = s.first[group(g)].astype(F32)
                else:
                    a = rs_take(1, g, 1)
                stats_out(k, 1, g, a)
            pass_one(*((4, 5) if k == 0 else (3,)))

            @pl.loop(0, G)
            def _(g):
                hidden_out(k, 1, g, 2 * k, s.h1)
            if k == 0:

                @on_pipes(1)
                def _():
                    for i in range(1, NP):
                        proj_send(i).start()

            else:
                pass_two(3)


            if k == 0:
                pass_two(4, 5)
            need(4 + k)

            @pl.loop(0, G)
            def _(g):
                stats_out(k, 2, g, conv(k, ag_take(2 * k, g, s.h1.at[k])))
            if k == 0:
                pass_one(1, 2)

            @pl.loop(0, G)
            def _(g):
                hidden_out(k, 2, g, 2 * k + 1, s.h2)
            if k == 0:
                pass_two(1, 2)

                @on_pipes(3)
                def _():
                    for i in range(1, NP):
                        proj_send(i).start()


            need(2 * k + 1)
            if k == 0:
                load_u.wait()

            @pl.loop(0, G)
            def _(g):
                a = dot_nt(ag_take(2 * k + 1, g, s.h2.at[k]), s.pq[2 * k + 1])
                stats_out(k, 3, g, a.reshape(GM, R, c.cs))

            if k == 0:
                need(2)

                @pl.loop(0, G)
                def _(g):
                    v = normed(0, 3, g) + s.u_seg[0, group(g)].astype(F32)
                    act, slope = gelu_pair(v)
                    s.d3[0, group(g)] = slope
                    o = jnp.where(real_rows(c.cs), act, 0.0).astype(BF16)
                    s.u_seg[1, group(g)] = o
                    rs_send(1, g, 1, dot(o.reshape(flat, c.cs), s.pq[2]))

        load_g.wait()

        @pl.loop(0, G)
        def _(g):
            v = normed(1, 3, g) + s.u_seg[1, group(g)].astype(F32)
            act, slope = gelu_pair(v)
            o = jnp.where(real_rows(c.cs), act, 0.0).astype(BF16)
            s.out_seg[group(g)] = o
            e = s.g_seg[group(g)].astype(F32) * slope
            s.e3[group(g)] = e
            back_out(1, 3, g, e)
            o32 = o.astype(F32)
            place = lax.broadcasted_iota(jnp.int32, (GM, R, c.cs), 1)
            for n in range(c.images):
                here = (place >= n * SIDE * SIDE) & (place < (n + 1) * SIDE * SIDE)
                mean = jnp.sum(jnp.where(here, o32, 0.0), axis=1, keepdims=True) / float(SIDE * SIDE)
                for m in range(GM):
                    s.pool[(g * GM + m) * c.images + n] = mean[m]

        out_copy = pltpu.make_async_copy(s.out_seg, bo_out, s.out_r.at[0])
        out_copy.start()
        tail.append(out_copy.wait)

        banks = ND * c.bank
        which = lax.broadcasted_iota(jnp.int32, (banks, c.cs), 0)
        term = jnp.zeros((banks, c.cs), F32)
        for n in range(M * c.images):
            ids = jnp.concatenate([ids_ref[n : n + 1, :]] * (c.cs // LANES), axis=1)
            term = term + jnp.where(which == ids, s.pool[n], 0.0)
        s.bank_put[...] = term.reshape(ND, c.bank, c.cs)

        @pl.loop(1, ND)
        def _(i):
            d = dp_peer(i)
            remote(s.bank_put.at[d], s.bank_got.at[me_d], s.bank_s.at[0], s.bank_r.at[0], me_p, d).start()

        tail.append(lambda: take_send(s.bank_got.at[pl.ds(0, ND - 1)], s.bank_s.at[0], s.bank_r.at[0]))

        s.bank_got[me_d] = s.bank_put[me_d]

        def all_rows(ref):
            return ref[...].reshape(M * R, ref.shape[-1])

        def all_seg(ref):
            return jnp.concatenate([ref[j].reshape(M * R, LANES) for j in range(NP)], axis=1)

        def grad_q(k):
            h = all_seg(s.h2.at[k])
            s.gp[2 * k + 1] = dot_tn(all_rows(s.da3.at[k]), h).astype(BF16)

        def grad_p0():
            d = s.da1[0, shard(0, me_p)].reshape(M * R, LANES)
            s.g0[...] = dot_tn(all_rows(s.u_all), d).astype(BF16)

        def grad_p(k):
            d = all_seg(s.da1.at[k])
            s.gp[2 * k] = dot_tn(all_rows(s.u_seg.at[k]), d).astype(BF16)

        def grad_w(k):
            h = all_seg(s.h1.at[k])
            for t0 in range(0, TAPS, 2):
                taps = [t for t in (t0, t0 + 1) if t < TAPS]
                d = s.dcol[k, :, :, t0 * LANES : (t0 + len(taps)) * LANES].reshape(M * R, len(taps) * LANES)
                v = dot_tn(h, d)
                for n, t in enumerate(taps):
                    s.gw[k, t * c.mid : (t + 1) * c.mid, :] = v[:, n * LANES : (n + 1) * LANES].astype(BF16)

        def part(base, n):
            return pl.ds(pl.multiple_of(base, 16), n)

        inner = (me_z == 1) | (me_z == 2)
        z_side = lax.div(me_z, 2)
        outer_dev = 2 * (3 * z_side) + me_c
        inner_dev = 2 * (1 + z_side) + me_c
        across_dev = 2 * (2 - z_side) + me_c

        def job_own(job):
            kind, k, n, base, slot = c.jobs[job]
            ref = s.g0 if kind == "0" else s.gw.at[k] if kind == "w" else s.gp.at[2 * k + (kind == "q")]
            return ref, base

        def job_ref(name, job):
            kind, k, n, base, slot = c.jobs[job]
            return getattr(s, name + ("p" if kind in "pq" else kind)).at[slot]

        def job_core(job):
            own, base = job_own(job)
            n = c.jobs[job][2]
            view = own.at[part(base + (1 - me_c) * n, n)]
            remote(view, job_ref("ja", job), s.gs.at[job, 0], s.gr.at[job, 0], me_p, sib).start()

        def job_in(job):
            own, base = job_own(job)
            n = c.jobs[job][2]
            got, tot = job_ref("ja", job), job_ref("jb", job)
            take_recv(got, s.gs.at[job, 0], s.gr.at[job, 0])
            tot[...] = (got[...].astype(F32) + own[part(base + me_c * n, n), :].astype(F32)).astype(BF16)
            @pl.when(jnp.logical_not(inner))
            def _():
                remote(tot, job_ref("jc", job), s.gs.at[job, 1], s.gr.at[job, 1], me_p, inner_dev).start()

        def job_halve(job):
            n = c.jobs[job][2]
            got, tot, half = job_ref("jc", job), job_ref("jb", job), job_ref("jd", job)

            @pl.when(inner)
            def _():
                take_recv(got, s.gs.at[job, 1], s.gr.at[job, 1])
                tot[...] = (got[...].astype(F32) + tot[...].astype(F32)).astype(BF16)
                view = tot.at[part((1 - z_side) * (n // 2), n // 2)]
                remote(view, half, s.gs.at[job, 2], s.gr.at[job, 2], me_p, across_dev).start()

        def job_sum(job):
            n = c.jobs[job][2]
            tot, half, fin = job_ref("jb", job), job_ref("jd", job), job_ref("je", job)
            mine = part(z_side * (n // 2), n // 2)

            @pl.when(inner)
            def _():
                take_recv(half, s.gs.at[job, 2], s.gr.at[job, 2])
                fin[mine, :] = (half[...].astype(F32) + tot[mine, :].astype(F32)).astype(BF16)
                view = fin.at[mine]
                remote(view, view, s.gs.at[job, 3], s.gr.at[job, 3], me_p, across_dev).start()
                remote(view, view, s.gs.at[job, 4], s.gr.at[job, 3], me_p, outer_dev).start()

        def job_out(job):
            n = c.jobs[job][2]
            fin = job_ref("je", job)
            view = fin.at[part((1 - z_side) * (n // 2), n // 2)]

            @pl.when(inner)
            def _():
                take_recv(view, s.gs.at[job, 3], s.gr.at[job, 3])
                remote(view, view, s.gs.at[job, 5], s.gr.at[job, 4], me_p, outer_dev).start()

        def job_place(job, p, core):
            kind, k, n, base, slot = c.jobs[job]
            if kind == "0":
                return s.p0_out.at[shard(0, p), part(base + core * n, n)]
            if kind == "w":
                return s.w_out.at[lax.div(p, 2) if k == 0 else 1 - lax.div(p, 2), part(base + core * n, n)]
            return s.p_out.at[part(p * 2 * n + core * n, n)]

        def job_home(job, p):
            kind, k = c.jobs[job][:2]
            return 2 * k + lax.rem(p, 2) if kind == "w" else jnp.int32(2 * k + (kind == "q"))

        def job_holds(job):
            kind, k = c.jobs[job][:2]
            return me_y == k if kind == "w" else me_p == 2 * k + (kind == "q")

        def job_plane(job):
            n = c.jobs[job][2]
            fin = job_ref("je", job)

            @pl.when(jnp.logical_not(inner))
            def _():
                for step in (3, 4):
                    take_recv(fin.at[0 : n // 2], s.gs.at[job, step], s.gr.at[job, step])

            home = job_home(job, me_p)

            @pl.when(me_p != home)
            def _():
                remote(fin, job_place(job, me_p, me_c), s.gs.at[job, 6], s.gr.at[job, 5], home, me_d).start()

            @pl.when(me_p == home)
            def _():
                pltpu.make_async_copy(fin, job_place(job, me_p, me_c), s.own_s.at[job]).start()

        def job_many(job, count):
            kind, k, n, base, slot = c.jobs[job]
            if kind == "0":
                return s.p0_out.at[pl.ds(0, count), pl.ds(0, n)]
            return s.w_out.at[pl.ds(0, count), pl.ds(0, n)] if kind == "w" else s.p_out.at[pl.ds(0, n * count)]

        def job_share(job):
            fin = job_ref("je", job)
            from_pipes = [0, 2] if c.jobs[job][0] == "w" else [0, 1, 2, 3]

            @pl.when(job_holds(job))
            def _():
                pltpu.make_async_copy(fin, job_place(job, me_p, me_c), s.own_s.at[job]).wait()
                take_recv(job_many(job, len(from_pipes) - 1), s.gs.at[job, 6], s.gr.at[job, 5])
                for i in from_pipes:
                    view = job_place(job, pipe_peer(i), me_c)
                    remote(view, view, s.fin_s.at[job], s.fin_r.at[job], me_p, sib).start()

        def job_end(job):
            got, half, fin = job_ref("ja", job), job_ref("jd", job), job_ref("je", job)
            take_send(got, s.gs.at[job, 0], s.gr.at[job, 0])

            @pl.when(inner)
            def _():
                for step in (2, 3, 4, 5):
                    take_send(half, s.gs.at[job, step], s.gr.at[job, 2])

            @pl.when(jnp.logical_not(inner))
            def _():
                take_send(got, s.gs.at[job, 1], s.gr.at[job, 1])

            @pl.when(me_p != job_home(job, me_p))
            def _():
                take_send(fin, s.gs.at[job, 6], s.gr.at[job, 5])

            @pl.when(job_holds(job))
            def _():
                view = job_many(job, 2 if c.jobs[job][0] == "w" else NP)
                take_recv(view, s.fin_s.at[job], s.fin_r.at[job])
                take_send(view, s.fin_s.at[job], s.fin_r.at[job])

        def job_store(job, act):
            kind, k, n, base, slot = c.jobs[job]
            rows = pl.ds(base, 2 * n)
            if kind == "0":
                parts = [(s.p0_out.at[j, rows], gp_out.at[rows, pl.ds(j * LANES, LANES)]) for j in range(NP)]
            elif kind == "w":
                parts = [(s.w_out.at[h, rows], gw_out.at[rows, pl.ds(h * LANES, LANES)]) for h in range(2)]
            else:
                parts = [(s.p_out, gp_out)]

            @pl.when(job_holds(job))
            def _():
                for i, (src, dst) in enumerate(parts):
                    getattr(pltpu.make_async_copy(src, dst, s.store.at[job, i]), act)()

        steps = (job_core, job_in, job_halve, job_sum, job_out, job_plane, job_share)
        next_step = dict.fromkeys(c.jobs, 0)

        def advance(*jobs):
            if c.deep:
                for job in jobs:
                    if next_step[job] < len(steps):
                        steps[next_step[job]](job)
                        next_step[job] += 1

        def point(k, n):
            advance(*POINTS[(1 - k) * 6 + n])

        for k in (1, 0):
            side = 2 * (1 - k)

            @pl.loop(0, G)
            def _(g):
                grad = back_in(k, 3, g, s.e3[group(g)])
                s.da3[k, group(g)] = grad
                rs_send(2 + (1 - k), g, k, dot(grad.reshape(flat, c.cs), s.pq[2 * k + 1]))

            grad_q(k)
            if k == 1:

                @on_pipes(0)
                def _():
                    for i in range(1, NP):
                        proj_send(i).start()

            point(k, 0)

            @pl.loop(0, G)
            def _(g):
                up = rs_take(2 + (1 - k), g, k) * s.d2[k, group(g)]
                s.t1[group(g)] = up
                back_out(k, 2, g, up)
            if k == 0:
                pass_one(0)
            point(k, 1)

            @pl.loop(0, G)
            def _(g):
                rs_send(5 - k, g, k, conv_back(k, g, back_in(k, 2, g, s.t1[group(g)])))

            grad_w(k)
            point(k, 2)

            @pl.loop(0, G)
            def _(g):
                up = rs_take(5 - k, g, k) * s.d1[k, group(g)]
                s.t1[group(g)] = up
                back_out(k, 1, g, up)
            if k == 0:
                pass_two(0)
            point(k, 3)

            @pl.loop(0, G)
            def _(g):
                mine = shard(k, me_p)
                s.da1[k, mine, group(g)] = back_in(k, 1, g, s.t1[group(g)])
                ag_send(5 + side, g, s.da1.at[k], mine)
            if k == 0:
                grad_p0()
            point(k, 4)

            if k == 0:
                need(0)

            @pl.loop(0, G)
            def _(g):
                d = dot_nt(ag_take(5 + side, g, s.da1.at[k]), s.pq[2 * k])
                d = d.reshape(GM, R, c.cs) + s.e3[group(g)]
                if k == 1:
                    e = d * s.d3[0, group(g)]
                    s.e3[group(g)] = e
                    back_out(0, 3, g, e)
                else:
                    s.in_seg[group(g)] = d.astype(BF16)

            if k == 1 or not c.deep:
                grad_p(k)
            point(k, 5)

        in_copy = pltpu.make_async_copy(s.in_seg, ig_out, s.out_r.at[1])
        in_copy.start()
        tail.append(in_copy.wait)
        view = s.norm_sum.at[me_p]
        for i in range(1, NP):
            remote(view, view, s.ns_s.at[0], s.ns_r.at[0], pipe_peer(i), me_d).start()
        tail.append(lambda: take_send(s.norm_sum.at[pl.ds(0, NP - 1)], s.ns_s.at[0], s.ns_r.at[0]))

        while c.deep and min(next_step.values()) < len(steps) - 1:
            advance(*[job for job in LAST if next_step[job] < len(steps) - 1])

        take_recv(s.bank_got.at[pl.ds(0, ND - 1)], s.bank_s.at[0], s.bank_r.at[0])
        tot = s.bank_got[0]
        for d in range(1, ND):
            tot = tot + s.bank_got[d]
        mb_out[...] = tot
        take_recv(s.norm_sum.at[pl.ds(0, NP - 1)], s.ns_s.at[0], s.ns_r.at[0])
        per = c.mid // LANES
        wide = c.cs // LANES
        each = (2 * per + c.ch // LANES) // NP
        for k in range(2):
            for n in range(each):
                q = me_p * each + n
                in_one = q < per
                in_two = (q >= per) & (q < 2 * per)
                sh = jnp.where(in_one, q, q - per)
                half = lax.rem(sh + k, 2)
                small = 2 * half + lax.div(sh, 2)
                far = q - 2 * per
                p = jnp.where(q < 2 * per, small, lax.div(far, wide))
                chunk = jnp.where(in_one, 0, jnp.where(in_two, 1, 2 + lax.rem(far, wide)))
                ns_out[n, 2 * k : 2 * k + 2, :] = s.norm_sum[p, chunk, 2 * k : 2 * k + 2, :]

        def drain():
            front_send().wait_send()
            for i in range(1, NP):
                proj_send(i).wait_send()
            for n in range(6):
                end_part(n)

            @pl.loop(0, G)
            def _(g):
                for wait in [*due.values(), *owed.values()]:
                    wait(g)

                @pl.when(me_p == 0)
                def _():
                    take_send(s.put.at[0, pl.ds(0, NP - 1), group(g)], s.rs_s.at[0, g], s.rs_r.at[0, g])
            for wait in tail:
                wait()

        drain()
        advance(*c.jobs)
        if c.deep:
            for job in c.jobs:
                job_end(job)
                job_store(job, "start")
            for job in c.jobs:
                job_store(job, "wait")

    work()

    if not c.deep:
        copies = [
            pltpu.make_async_copy(s.gp, gp_out, s.out_r.at[2]),
            pltpu.make_async_copy(s.gw, gw_out, s.out_r.at[3]),
        ]
        for copy in copies:
            copy.start()
        for copy in copies:
            copy.wait()


def on_device(mesh, block_input, proj_weight, spatial_weight, norm_gain, norm_shift, output_grad, image_ids):
    bank = 8
    c = Sizes(mesh, block_input, proj_weight, spatial_weight, bank)
    extra = ((0, 0), (0, c.pad - c.rows), (0, 0))
    u = jnp.pad(block_input, extra)
    go = lax.dynamic_slice_in_dim(output_grad, lax.axis_index("pipe") * c.cs, c.cs, axis=2)
    go = jnp.pad(go, extra)
    sw = spatial_weight.reshape(TAPS, c.mid, spatial_weight.shape[2])
    ids = jnp.broadcast_to(image_ids.reshape(-1, 1), (image_ids.size, LANES))
    items = scratch_list(c)
    names = [n for n, _ in items]
    anyspec = pl.BlockSpec(memory_space=pl.ANY)
    vspec = pl.BlockSpec(memory_space=pltpu.VMEM)
    if c.deep:
        gp_shape, gw_shape = (c.ch, c.mid), (TAPS * c.mid, 2 * LANES)
    else:
        gp_shape, gw_shape = (c.pipes, c.cs, c.mid), (2, TAPS * c.mid, LANES)
    each = (2 * c.mid + c.ch) // LANES // c.pipes
    outs = pl.pallas_call(
        functools.partial(body, c, names),
        out_shape=(
            jax.ShapeDtypeStruct((c.micro, c.pad, c.cs), BF16),
            jax.ShapeDtypeStruct((c.micro, c.pad, c.cs), BF16),
            jax.ShapeDtypeStruct(gp_shape, BF16),
            jax.ShapeDtypeStruct(gw_shape, BF16),
            jax.ShapeDtypeStruct((each, 4, LANES), F32),
            jax.ShapeDtypeStruct((bank, c.cs), F32),
        ),
        in_specs=[anyspec] * 4 + [vspec] * 3,
        out_specs=(anyspec, anyspec, anyspec, anyspec, vspec, vspec),
        scratch_shapes=[v for _, v in items],
        compiler_params=pltpu.CompilerParams(collective_id=0, has_side_effects=True, vmem_limit_bytes=60 << 20),
    )(u, go, proj_weight[0], sw, norm_gain, norm_shift, ids)
    bo, ig, gp, gw, ns, mb = outs
    if not c.deep:
        gp = lax.psum(gp.astype(F32), "dp")
        gw = lax.psum(gw.astype(F32), "dp")
        gp = lax.all_to_all(gp, "pipe", 0, 0, tiled=True).reshape(c.ch, c.mid)
        gw = lax.all_gather(gw, "pipe")
        me = lax.axis_index("pipe")
        y, x = me // 2, me % 2
        near = lax.dynamic_index_in_dim(gw, me, 0, keepdims=False)
        far = lax.dynamic_index_in_dim(gw, 2 * (1 - y) + x, 0, keepdims=False)
        gw = jnp.concatenate(
            [lax.dynamic_index_in_dim(near, y, 0, keepdims=False), lax.dynamic_index_in_dim(far, y, 0, keepdims=False)],
            axis=1,
        )
    ns = jnp.transpose(ns.reshape(each, 2, 2, LANES), (2, 1, 0, 3)).reshape(2, 2, each * LANES)
    return (
        bo[:, : c.rows],
        ig[:, : c.rows],
        gp.astype(F32)[None],
        gw.astype(F32)[None],
        ns[0],
        ns[1],
        mb,
    )


def solution(mesh):
    return jax.shard_map(
        functools.partial(on_device, mesh),
        mesh=mesh,
        in_specs=(
            P(None, "dp", None),
            P("pipe", None, None),
            P("pipe", None, None),
            P(),
            P(),
            P(None, "dp", None),
            P(None, "dp"),
        ),
        out_specs=(
            P(None, "dp", "pipe"),
            P(None, "dp", "pipe"),
            P("pipe", None, None),
            P("pipe", None, None),
            P(None, "pipe"),
            P(None, "pipe"),
            P("dp", "pipe"),
        ),
        check_vma=False,
    )
```
